128 devices in a mesh: ctx: 16 (over z, y), head: 8 (over x, core).
Axes of the slice: x: 4, y: 4, z: 4, core: 2. Of those that a mesh axis runs over, the one named last changes fastest.
Arguments:
- g_out: bfloat16 [8192, 8192], P('ctx', 'head'), may hold values from -6 to 6
- w_out: bfloat16 [8192, 8192], P('ctx', 'head'), may hold values from -0.0625 to 0.0625
- x_act: bfloat16 [8192, 8192], P('ctx', 'head'), may hold values from -6 to 6
- b_proj: bfloat16 [8192, 128], P('ctx'), may hold values from -0.5 to 0.5
- c_proj: bfloat16 [8192, 128], P('ctx'), may hold values from -0.0625 to 0.0625
- log_decay: float32 [128, 8192], P('head', 'ctx'), may hold values from -2 to 0
- kept_heads: int32 [64], replicated, may hold values from 0 to 127, as said below
Outputs:
- input_grad: bfloat16 [8192, 8192], P('ctx', 'head')
- b_grad: float32 [8192, 128], P('ctx')
- c_grad: float32 [8192, 128], P('ctx')
- decay_grad: float32 [128, 8192], P('head', 'ctx')
- weight_grad: bfloat16 [8192, 8192], P('ctx', 'head')
The draws below stay inside these ranges and needn't reach their ends.
Inputs may be any that keep to these rules, and one draw needn't show every extreme that they name: `kept_heads`: kept head indices are distinct and increasing; at most 12 of them fall in any group of 16 consecutive heads starting at a multiple of 16, and exactly 12 in one such group.
All inputs are finite; a program needn't handle non-finite values.
Results may differ from the reference program's by a relative error of at most 0.024.
Values may be sent and summed in bfloat16 or wider, within the bound.
A program may use at most 128 MiB of HBM per device.

```python
import math
import jax
import jax.numpy as jnp
from jax import lax

D = 8192
SSM_HEADS = 128
P_SIZE = 64
N = 128
KEPT = 64
Q = 128
TOK_DEV = 512
SEQUENCE_TOKENS = 8192
GROUP = 16
CAP = 12
N_CTX = 16


def draw_log_decay(key, part):
    key = jax.random.fold_in(key, 11)
    random_subkeys = jax.random.split(key, 7)
    fast_share = 0.5
    chooser = jax.random.uniform(random_subkeys[0], (SSM_HEADS,))
    fast_rate = jax.random.uniform(random_subkeys[1], (SSM_HEADS,), minval=1.0 / 50.0, maxval=1.0 / 30.0)
    slow_rate = jnp.exp(jax.random.uniform(random_subkeys[2], (SSM_HEADS,), minval=math.log(0.1), maxval=math.log(0.4))) / SEQUENCE_TOKENS
    decay_speed = jnp.where(chooser < fast_share, fast_rate, slow_rate)
    token_multiplier = jax.random.uniform(random_subkeys[3], (SSM_HEADS, SEQUENCE_TOKENS), minval=0.5, maxval=2.0)
    block_multiplier = jnp.repeat(jax.random.uniform(random_subkeys[4], (SSM_HEADS, SEQUENCE_TOKENS // TOK_DEV), minval=0.5, maxval=2.0), TOK_DEV, axis=1)
    spike_position = jax.random.randint(random_subkeys[5], (SSM_HEADS, 3), 0, SEQUENCE_TOKENS)
    spike_length = jax.random.uniform(random_subkeys[6], (SSM_HEADS, 3), minval=0.22, maxval=0.45)
    token_positions = jnp.arange(SEQUENCE_TOKENS, dtype=jnp.int32)
    spike_loss = jnp.sum(jnp.where(token_positions[None, None, :] == spike_position[:, :, None], spike_length[:, :, None], 0.0), axis=1)
    return -(decay_speed[:, None] * token_multiplier * block_multiplier + spike_loss)


def draw_kept_heads(key, part):
    key = jax.random.fold_in(key, 23)
    random_subkeys = jax.random.split(key, 2)
    group_count = SSM_HEADS // GROUP
    group_rank = jax.random.permutation(random_subkeys[0], group_count)
    base_count = (KEPT - CAP) // (group_count - 1)
    extra_count = (KEPT - CAP) % (group_count - 1)
    counts = jnp.where(group_rank == 0, CAP, base_count + (group_rank <= extra_count).astype(jnp.int32))
    orders = jax.vmap(lambda single: jax.random.permutation(single, GROUP))(jax.random.split(random_subkeys[1], group_count))
    keep_flag = (orders < counts[:, None]).reshape(SSM_HEADS)
    head_ids = jnp.arange(SSM_HEADS, dtype=jnp.int32)
    ordered = jnp.sort(jnp.where(keep_flag, head_ids, SSM_HEADS + head_ids))[:KEPT]
    return ordered.astype(jnp.int32)


def raised(values, rng, source, target, blocks, factor):
    owner, partner = [(jnp.arange(values.shape[dim]) // (values.shape[dim] // blocks)).reshape([-1 if axis == dim else 1 for axis in range(values.ndim)]) for dim in (source, target)]
    chosen = jax.random.permutation(rng, blocks)[partner]
    strong = (owner == chosen) | (owner == (partner + blocks // 2) % blocks)
    return jnp.where(strong, factor * values, values)


def steps_of(rng, extent, shards, low, high):
    loudness, own = 1.0, jax.random.fold_in(rng, 6)
    for position, blocks in shards:
        draws = jnp.exp(jax.random.uniform(jax.random.fold_in(own, position), (blocks,), jnp.float32, low / len(shards), high / len(shards)))
        loudness = loudness * jnp.repeat(draws, extent[position] // blocks).reshape([-1 if axis == position else 1 for axis in range(len(extent))])
    return loudness


def normal_values(own_key, dims, scale, limit, shards=(), kind=jnp.bfloat16):
    drawn = jax.random.normal(own_key, dims, jnp.float32) * scale
    if len(shards) > 0:
        drawn = steps_of(own_key, dims, shards, -0.22, 0.18) * drawn
    return jnp.clip(drawn, min=-limit, max=limit).astype(kind)


def heavy_noise(rng, shape, scale, bound, pieces, heavy, held_as=jnp.bfloat16):
    values = scale * jax.random.normal(rng, shape, jnp.float32)
    if pieces:
        values = values * steps_of(rng, shape, pieces, -0.22, 0.18)
    return jnp.clip(raised(values, jax.random.fold_in(rng, 3), *heavy), -bound, bound).astype(held_as)


def setup_inputs(seed: int = 0) -> dict:
    seeds = jax.random.split(jax.random.key(seed), 8)
    g_out = heavy_noise(seeds[0], (SEQUENCE_TOKENS, D), 1.0, 6.0, ((0, 16), (1, 8)), (0, 1, 16, 2.0))
    w_out = normal_values(seeds[1], (D, SSM_HEADS * P_SIZE), D ** -0.5, 0.0625, ((0, 16), (1, 8)))
    x_act = normal_values(seeds[2], (SEQUENCE_TOKENS, SSM_HEADS * P_SIZE), 1.0, 6.0, ((0, 16), (1, 8)))
    b_proj = normal_values(seeds[3], (SEQUENCE_TOKENS, N), N ** -0.5, 0.5, ((0, 16),))
    c_proj = normal_values(seeds[4], (SEQUENCE_TOKENS, N), SEQUENCE_TOKENS ** -0.5, 0.0625, ((0, 16),))
    log_decay = draw_log_decay(jax.random.fold_in(seeds[7], 71), 0)
    kept_heads = draw_kept_heads(jax.random.fold_in(seeds[7], 71), 0)
    return dict(g_out=g_out, w_out=w_out, x_act=x_act, b_proj=b_proj, c_proj=c_proj, log_decay=log_decay, kept_heads=kept_heads)


highest = lax.Precision.HIGHEST

def state_terms(cumulative, span_total, inputs, b_mat):
    tail = jnp.exp(span_total[..., None] - cumulative)
    return jnp.einsum('scip,scin->scpn', inputs, tail[..., None] * b_mat[None], precision=highest)

def adjoint_terms(cumulative, out_grad, c_mat):
    return jnp.einsum('sctp,sctn->scpn', out_grad, jnp.exp(cumulative)[..., None] * c_mat[None], precision=highest)

def fold_forward(span_total, parts):

    def advance(state, inputs_now):
        total_now, part_now = inputs_now
        return (jnp.exp(total_now)[:, None, None] * state + part_now, state)
    closing, entering = lax.scan(advance, jnp.zeros_like(parts[:, 0]), (jnp.transpose(span_total), jnp.moveaxis(parts, 1, 0)))
    return (closing, jnp.moveaxis(entering, 0, 1))

def fold_backward(span_total, parts):

    def advance(state, inputs_now):
        total_now, part_now = inputs_now
        return (jnp.exp(total_now)[:, None, None] * state + part_now, state)
    opening, ending = lax.scan(advance, jnp.zeros_like(parts[:, 0]), (jnp.transpose(span_total), jnp.moveaxis(parts, 1, 0)), reverse=True)
    return (opening, jnp.moveaxis(ending, 0, 1))

def span_outputs(cumulative, span_total, inputs, b_mat, c_mat, out_grad, state_in, adjoint_end):
    length = cumulative.shape[-1]
    triangle = jnp.tril(jnp.ones((length, length), jnp.float32))
    allowed = triangle > 0.5
    differ = cumulative[..., :, None] - cumulative[..., None, :]
    weights_low = jnp.where(allowed, jnp.exp(jnp.where(allowed, differ, 0.0)), 0.0)
    cross_cb = jnp.einsum('ctn,cin->cti', c_mat, b_mat, precision=highest)
    cross_gx = jnp.einsum('sctp,scip->scti', out_grad, inputs, precision=highest)
    mixed_cb = weights_low * cross_cb[None]
    mixed_gx = weights_low * cross_gx
    head_w = jnp.exp(cumulative)
    tail = jnp.exp(span_total[..., None] - cumulative)
    read_state = jnp.einsum('ctn,scpn->sctp', c_mat, state_in, precision=highest)
    read_adjoint = jnp.einsum('cin,scpn->scip', b_mat, adjoint_end, precision=highest)
    outputs = head_w[..., None] * read_state + jnp.einsum('scti,scip->sctp', mixed_cb, inputs, precision=highest)
    in_grad = jnp.einsum('scti,sctp->scip', mixed_cb, out_grad, precision=highest) + tail[..., None] * read_adjoint
    b_part = jnp.einsum('scti,ctn->cin', mixed_gx, c_mat, precision=highest) + jnp.einsum('scip,scpn->cin', tail[..., None] * inputs, adjoint_end, precision=highest)
    c_part = jnp.einsum('sctp,scpn->ctn', head_w[..., None] * out_grad, state_in, precision=highest) + jnp.einsum('scti,cin->ctn', mixed_gx, b_mat, precision=highest)
    constant = jnp.exp(span_total) * lax.optimization_barrier(jnp.sum(adjoint_end * state_in, axis=(-2, -1)))
    prior_sum = jnp.einsum('ti,sci->sct', triangle, tail * lax.optimization_barrier(jnp.sum(inputs * read_adjoint, axis=-1)), precision=highest)
    later_sum = jnp.einsum('it,sci->sct', triangle, head_w * lax.optimization_barrier(jnp.sum(out_grad * read_state, axis=-1)), precision=highest)
    suffix = jnp.einsum('kt,scki->scti', triangle, mixed_gx * cross_cb[None], precision=highest)
    inside_sum = lax.optimization_barrier(jnp.sum(suffix * triangle, axis=-1))
    decay_part = constant[..., None] + prior_sum + later_sum + inside_sum - lax.optimization_barrier(jnp.sum(in_grad * inputs, axis=-1))
    return (outputs, in_grad, b_part, c_part, decay_part)

def reference(g_out, w_out, x_act, b_proj, c_proj, log_decay, kept_heads):
    head_ids = jnp.arange(SSM_HEADS, dtype=jnp.int32)
    kept_flag = jnp.any(kept_heads[:, None] == head_ids[None, :], axis=0).astype(jnp.float32)
    column_flag = jnp.repeat(kept_flag, P_SIZE).astype(jnp.bfloat16)
    head_grad = jnp.dot(g_out, w_out, preferred_element_type=jnp.float32).astype(jnp.bfloat16) * column_flag[None, :]
    spans = SEQUENCE_TOKENS // Q
    b_mat = b_proj.astype(jnp.float32).reshape(spans, Q, N)
    c_mat = c_proj.astype(jnp.float32).reshape(spans, Q, N)

    def per_head(sums, head):
        offset = head * P_SIZE
        inputs = lax.dynamic_slice_in_dim(x_act, offset, P_SIZE, 1).astype(jnp.float32).reshape(1, spans, Q, P_SIZE)
        out_grad = lax.dynamic_slice_in_dim(head_grad, offset, P_SIZE, 1).astype(jnp.float32).reshape(1, spans, Q, P_SIZE)
        decays = lax.dynamic_index_in_dim(log_decay, head, 0, keepdims=False).reshape(1, spans, Q)
        cumulative = jnp.cumsum(decays, axis=-1)
        span_total = cumulative[..., -1]
        unused_a, state_in = fold_forward(span_total, state_terms(cumulative, span_total, inputs, b_mat))
        unused_b, adjoint_end = fold_backward(span_total, adjoint_terms(cumulative, out_grad, c_mat))
        outputs, in_grad, b_part, c_part, decay_part = span_outputs(cumulative, span_total, inputs, b_mat, c_mat, out_grad, state_in, adjoint_end)
        outputs = outputs * lax.dynamic_index_in_dim(kept_flag, head, 0, keepdims=False)
        return ((sums[0] + b_part, sums[1] + c_part), (outputs.reshape(SEQUENCE_TOKENS, P_SIZE).astype(jnp.bfloat16), in_grad.reshape(SEQUENCE_TOKENS, P_SIZE).astype(jnp.bfloat16), decay_part.reshape(SEQUENCE_TOKENS)))
    start_sums = (jnp.zeros((spans, Q, N), jnp.float32), jnp.zeros((spans, Q, N), jnp.float32))
    sums, stacked = lax.scan(per_head, start_sums, head_ids)
    y_out = jnp.transpose(stacked[0], (1, 0, 2)).reshape(SEQUENCE_TOKENS, SSM_HEADS * P_SIZE)
    input_grad = jnp.transpose(stacked[1], (1, 0, 2)).reshape(SEQUENCE_TOKENS, SSM_HEADS * P_SIZE)
    decay_grad = stacked[2] / math.sqrt(P_SIZE * SEQUENCE_TOKENS)
    b_grad = sums[0].reshape(SEQUENCE_TOKENS, N) / math.sqrt(KEPT * P_SIZE)
    c_grad = sums[1].reshape(SEQUENCE_TOKENS, N) * math.sqrt(N / (KEPT * P_SIZE * SEQUENCE_TOKENS))
    scale = 1.0 / math.sqrt(SEQUENCE_TOKENS)

    def block_term(running, block):
        offset = block * TOK_DEV
        rows_g = lax.dynamic_slice_in_dim(g_out, offset, TOK_DEV, 0)
        rows_y = lax.dynamic_slice_in_dim(y_out, offset, TOK_DEV, 0)
        term = jnp.dot(rows_g.T, rows_y, preferred_element_type=jnp.float32) * scale
        term = lax.optimization_barrier(term.astype(jnp.bfloat16)).astype(jnp.float32)
        return (running + term, None)
    weight_sum, unused_c = lax.scan(block_term, jnp.zeros((D, SSM_HEADS * P_SIZE), jnp.float32), jnp.arange(N_CTX, dtype=jnp.int32))
    return (input_grad, b_grad, c_grad, decay_grad, weight_sum.astype(jnp.bfloat16))
```

```python
import math

import jax
import jax.numpy as jnp
from jax import lax
from jax.experimental import pallas as pl
from jax.experimental.pallas import tpu as pltpu
from jax.sharding import PartitionSpec as P

D = 8192
P_SIZE = 64
N = 128
KEPT = 64
Q = 128
TOK = 512
SPANS = TOK // Q
GROUP = 16
CAP = 12
COLS = CAP * P_SIZE
WIDE = GROUP * P_SIZE
PAIRS = CAP // 2
N_CTX = 16
N_HEAD = 8

F32 = jnp.float32
BF = jnp.bfloat16
HIGH = lax.Precision.HIGHEST
MESH = pl.DeviceIdType.MESH
NN = (((1,), (0,)), ((), ()))
NT = (((1,), (1,)), ((), ()))
TN = (((0,), (0,)), ((), ()))


def dot(a, b, dims=NN, precision=None):
    return lax.dot_general(a, b, dims, precision=precision, preferred_element_type=F32)


def rcopy(src, dst, send_sem, recv_sem, device):
    return pltpu.make_async_remote_copy(
        src_ref=src,
        dst_ref=dst,
        send_sem=send_sem,
        recv_sem=recv_sem,
        device_id=device,
        device_id_type=MESH,
    )


def aligned(start, size, unit):
    return pl.ds(pl.multiple_of(start, unit), size)


def loop(lo, hi, body):
    def step(i, carry):
        body(i)
        return carry

    lax.fori_loop(lo, hi, step, 0)


class Gather:
    def __init__(self, block, half, send, recv, me, left, right, device):
        self.block, self.half, self.send, self.recv = block, half, send, recv
        self.me, self.left, self.right = me, left, right
        self.to_left, self.to_right = device(left), device(right)
        self.far = lax.rem(me + 2, 4)

    def copy(self, i):
        ref = (
            lambda: self.block(self.me),
            lambda: self.block(self.me),
            lambda: self.half(self.left, 0),
            lambda: self.half(self.right, 1),
        )[i]()
        return rcopy(ref, ref, self.send(i), self.recv(i), self.to_left if i % 2 else self.to_right)

    def landed(self, slot, ref):
        rcopy(ref, ref, self.send(slot), self.recv(slot), self.to_right).wait_recv()

    def start(self):
        self.copy(0).start()
        self.copy(1).start()

    def forward(self):
        self.landed(0, self.block(self.left))
        self.copy(2).start()
        self.landed(1, self.block(self.right))
        self.copy(3).start()

    def finish(self):
        self.landed(2, self.half(self.far, 0))
        self.landed(3, self.half(self.far, 1))

    def drain(self):
        for i in range(4):
            self.copy(i).wait_send()


class Scatter:
    def __init__(self, term, rows, far, right, left, via_l, via_r, from_l, from_r, own, send, recv, me, device):
        self.term, self.rows, self.h = term, rows, rows // 2
        self.far_buf, self.right_buf, self.left_buf = far, right, left
        self.via_l, self.via_r, self.from_l, self.from_r, self.own = via_l, via_r, from_l, from_r, own
        self.send, self.recv = send, recv
        self.me = me
        self.right, self.left, self.far = lax.rem(me + 1, 4), lax.rem(me + 3, 4), lax.rem(me + 2, 4)
        self.to_right, self.to_left = device(self.right), device(self.left)

    def copy(self, i):
        h = self.h
        lo, hi = pl.ds(0, h), pl.ds(h, h)
        src, dst, to = (
            (self.far_buf.at[lo], self.via_l, self.to_right),
            (self.far_buf.at[hi], self.via_r, self.to_left),
            (self.right_buf.at[hi], self.from_l.at[hi], self.to_right),
            (self.left_buf.at[lo], self.from_r.at[lo], self.to_left),
            (self.right_buf.at[lo], self.from_l.at[lo], self.to_right),
            (self.left_buf.at[hi], self.from_r.at[hi], self.to_left),
        )[i]
        return rcopy(src, dst, self.send.at[i], self.recv.at[i], to)

    def first(self):
        h = self.h
        self.far_buf[:h] = self.term(self.far, 0).astype(BF)
        self.copy(0).start()
        self.far_buf[h:] = self.term(self.far, 1).astype(BF)
        self.copy(1).start()
        self.right_buf[h:] = self.term(self.right, 1).astype(BF)
        self.copy(2).start()
        self.left_buf[:h] = self.term(self.left, 0).astype(BF)
        self.copy(3).start()

    def second(self):
        h = self.h
        self.own[:h] = self.term(self.right, 0)
        self.copy(0).wait_recv()
        self.right_buf[:h] = (self.own[:h] + self.via_l[...].astype(F32)).astype(BF)
        self.copy(4).start()
        self.own[h:] = self.term(self.left, 1)
        self.copy(1).wait_recv()
        self.left_buf[h:] = (self.own[h:] + self.via_r[...].astype(F32)).astype(BF)
        self.copy(5).start()

    def last(self):
        h = self.h
        self.own[:h] = self.term(self.me, 0)
        self.own[h:] = self.term(self.me, 1)

    def finish(self):
        for i in (2, 3, 4, 5):
            self.copy(i).wait_recv()

    def drain(self):
        for i in range(6):
            self.copy(i).wait_send()


class Exchange:
    def __init__(self, source, landed, back, entering, sems, ci, hi):
        self.source, self.landed_ref, self.back, self.entering = source, landed, back, entering
        self.sems, self.ci, self.hi = sems, ci, hi

    def out_copy(self, k, at):
        to = lax.rem(self.ci + k, N_CTX)
        return rcopy(
            self.source.at[aligned(8 * to, 8, 8)],
            self.landed_ref.at[at],
            self.sems.at[0, k],
            self.sems.at[1, k],
            (to, self.hi),
        )

    def back_copy(self, k, at):
        to = lax.rem(self.ci + k, N_CTX)
        return rcopy(
            self.back.at[to],
            self.entering.at[aligned(8 * at, 8, 8)],
            self.sems.at[2, k],
            self.sems.at[3, k],
            (to, self.hi),
        )

    def start(self):
        loop(1, N_CTX, lambda k: self.out_copy(k, self.ci).start())
        self.landed_ref[self.ci] = self.source[aligned(8 * self.ci, 8, 8), :]

    def landed(self):
        loop(1, N_CTX, lambda k: self.out_copy(k, lax.rem(self.ci + N_CTX - k, N_CTX)).wait_recv())

    def reply(self):
        loop(1, N_CTX, lambda k: self.back_copy(k, self.ci).start())
        self.entering[aligned(8 * self.ci, 8, 8), :] = self.back[self.ci]

    def replied(self):
        loop(1, N_CTX, lambda k: self.back_copy(k, lax.rem(self.ci + N_CTX - k, N_CTX)).wait_recv())

    def drain(self):
        def one(k):
            self.out_copy(k, self.ci).wait_send()
            self.back_copy(k, self.ci).wait_send()

        loop(1, N_CTX, one)


def kernel(
    g, w, x, b, c, logd, colidx, headof, sel,
    out_ig, out_b, out_c, out_decay, out_w,
    S, E16, G, W, YT, XS, XT, CUME, CUMR, PART, STIN, YF, YI, L, MS, GK, GH, IG, IGB, SG,
    CFD, RF, EF, ENT, DEC, OPN, RA, EA, AEN, BC, RB, SUM, BCF,
    h_far, h_right, h_left, h_vl, h_vr, h_fl, h_fr, h_own,
    w_far, w_right, w_left, w_vl, w_vr, w_fl, w_fr, w_own,
    loc_sem, a2a_sem, xs_sem, xr_sem, sib_sem, wag_sem, yag_sem, hrs_sem, wrs_sem, fex_sem, bex_sem, bc_sem,
):
    ci, hi = lax.axis_index("ctx"), lax.axis_index("head")
    z, y = ci // 4, lax.rem(ci, 4)
    xx, cc = hi // 2, lax.rem(hi, 2)
    half = y // 2
    cross = lax.rem(half + cc, 2)
    at_x = lambda p: (ci, 2 * p + cc)
    at_y = lambda p: (4 * z + p, hi)
    at_z = lambda p: (4 * p + y, hi)
    sibling = (ci, 2 * xx + 1 - cc)
    nxt = lambda p: lax.rem(p + 1, 4)
    prv = lambda p: lax.rem(p + 3, 4)

    barrier = pltpu.get_barrier_semaphore()

    def greet(device):
        pl.semaphore_signal(barrier, inc=1, device_id=device, device_id_type=MESH)

    loop(1, N_CTX, lambda k: greet((lax.rem(ci + k, N_CTX), hi)))
    loop(1, N_HEAD, lambda k: greet((ci, lax.rem(hi + k, N_HEAD))))

    @pl.when(cross == 1)
    def _():
        for p in range(2):
            greet((4 * z + 2 * cc + p, 2 * xx + 1 - cc))

    def build(i):
        rows = lax.broadcasted_iota(jnp.int32, (128, COLS), 0) + 128 * i
        S[aligned(128 * i, 128, 128), :] = jnp.where(rows == colidx[0:1, :], 1.0, 0.0).astype(BF)

    loop(0, WIDE // 128, build)
    E16[...] = jnp.where(
        lax.broadcasted_iota(jnp.int32, (GROUP, COLS), 0) == headof[0:1, :], 1.0, 0.0
    ).astype(F32)

    def pick_w(i):
        W[aligned(TOK * z + 128 * i, 128, 128), :] = dot(w[aligned(128 * i, 128, 128), :], S[...]).astype(BF)

    loop(0, TOK // 128, pick_w)

    pl.semaphore_wait(barrier, N_CTX - 1 + N_HEAD - 1 + 2 * cross)

    def g_tile(token, feature):
        return G.at[aligned(TOK * token, TOK, TOK), aligned(TOK * feature, TOK, TOK)]

    for p in range(2):
        target = 2 * cc + p
        src = g.at[:, pl.ds(TOK * p, TOK)]

        @pl.when(target == y)
        def _():
            pltpu.make_async_copy(src, g_tile(y, xx), loc_sem.at[0]).start()

        @pl.when(target != y)
        def _():
            rcopy(
                src, g_tile(y, xx), a2a_sem.at[0, p], a2a_sem.at[1, lax.rem(y, 2)], (4 * z + target, 2 * xx + half)
            ).start()

    w_gather = Gather(
        lambda p: W.at[aligned(TOK * p, TOK, TOK), :],
        lambda p, h: W.at[aligned(TOK * p + TOK // 2 * h, TOK // 2, TOK // 2), :],
        lambda i: wag_sem.at[0, i],
        lambda i: wag_sem.at[1, i],
        z, prv(z), nxt(z), at_z,
    )
    w_gather.start()

    sub = lax.broadcasted_iota(jnp.int32, (Q, Q), 0)
    lane = lax.broadcasted_iota(jnp.int32, (Q, Q), 1)
    upto = jnp.where(sub <= lane, 1.0, 0.0).astype(F32)
    below = jnp.where(sub < lane, 1.0, 0.0).astype(F32)
    spread = jnp.where(
        lax.broadcasted_iota(jnp.int32, (128, COLS), 1) // P_SIZE == lax.broadcasted_iota(jnp.int32, (128, COLS), 0),
        1.0,
        0.0,
    ).astype(F32)

    CFD[...] = jnp.zeros_like(CFD)
    DEC[0] = jnp.zeros((8, COLS), F32)

    def local_states(s):
        rows = aligned(Q * s, Q, Q)
        cum = dot(logd[:, rows], upto, precision=HIGH)
        CUMR[:, rows] = dot(sel[...], cum, precision=HIGH)
        cume = dot(cum, E16[...], TN, precision=HIGH)
        CUME[rows, :] = cume
        total = cume[Q - 1 : Q, :]
        xs = dot(x[rows, :], S[...])
        XS[rows, :] = xs.astype(BF)
        xt = (jnp.exp(total - cume) * xs).astype(BF)
        XT[rows, :] = xt
        part = dot(b[rows, :], xt, TN)
        PART[s] = part
        CFD[:, :COLS] = jnp.exp(total) * CFD[:, :COLS] + part
        DEC[0] = DEC[0] + total

    loop(0, SPANS, local_states)
    pick = jnp.where(
        lax.broadcasted_iota(jnp.int32, (COLS, 128), 0) == P_SIZE * lax.broadcasted_iota(jnp.int32, (COLS, 128), 1),
        1.0,
        0.0,
    ).astype(F32)
    totals = dot(DEC[0], pick, precision=HIGH)
    CFD[:, COLS:] = jnp.broadcast_to(totals[0:1, :], (N, 128))
    forward = Exchange(CFD, RF, EF, ENT, fex_sem, ci, hi)
    forward.start()

    x_gathers = []
    for t in range(2):
        token = 2 * cc + t
        x_gathers.append(
            Gather(
                lambda p, token=token: g_tile(token, p),
                lambda p, h, token=token: G.at[
                    aligned(TOK * token + TOK // 2 * h, TOK // 2, TOK // 2), aligned(TOK * p, TOK, TOK)
                ],
                lambda i, t=t: xs_sem.at[t, i],
                lambda i, t=t: xr_sem.at[t, i],
                xx, prv(xx), nxt(xx), at_x,
            )
        )
    ring_x = (xx, prv(xx), nxt(xx), lax.rem(xx + 2, 4))

    def to_sibling(t, j):
        tile = g_tile(2 * cc + t, ring_x[j])
        return rcopy(tile, tile, sib_sem.at[0, t, j], sib_sem.at[1, t, j], sibling)

    def from_sibling(t, j):
        tile = g_tile(2 * (1 - cc) + t, ring_x[j])
        rcopy(tile, tile, sib_sem.at[0, t, j], sib_sem.at[1, t, j], sibling).wait_recv()

    for t in range(2):
        token = 2 * cc + t

        @pl.when(token == y)
        def _():
            pltpu.make_async_copy(g.at[:, pl.ds(0, TOK)], g_tile(token, xx), loc_sem.at[0]).wait()

        @pl.when(token != y)
        def _():
            rcopy(
                g.at[:, pl.ds(0, TOK)], g_tile(token, xx), a2a_sem.at[0, t], a2a_sem.at[1, t], sibling
            ).wait_recv()

        x_gathers[t].start()
        to_sibling(t, 0).start()

    left_half = lane < P_SIZE
    causal = lane <= sub

    def inside(s):
        rows = aligned(Q * s, Q, Q)
        cb = dot(c[rows, :], b[rows, :], NT)
        for k in range(PAIRS):
            cols = pl.ds(Q * k, Q)
            for h in range(2):
                head = 2 * k + h
                differ = CUME[rows, pl.ds(P_SIZE * head, 1)] - CUMR[pl.ds(head, 1), rows]
                low = jnp.where(causal, jnp.exp(jnp.where(causal, differ, 0.0)), 0.0)
                L[PAIRS * s + k, pl.ds(Q * h, Q), :] = low
                MS[PAIRS * s + k, pl.ds(Q * h, Q), :] = (low * cb).astype(BF)
            both = dot(MS[PAIRS * s + k], XS[rows, cols])
            YF[rows, cols] = jnp.where(left_half, both[:Q], both[Q:])

    loop(0, SPANS, inside)

    forward.landed()
    for i in range(N_CTX):
        DEC[i] = jnp.exp(dot(RF[i, :, COLS:], spread, precision=HIGH))
    state = jnp.zeros((8, COLS), F32)
    for i in range(N_CTX):
        EF[i] = state
        state = DEC[i] * state + RF[i, :, :COLS]
    forward.reply()
    w_gather.forward()
    x_gathers[0].forward()
    to_sibling(0, 1).start()
    to_sibling(0, 2).start()
    forward.replied()

    def outputs(s):
        rows = aligned(Q * s, Q, Q)
        cume = CUME[rows, :]
        state_in = ENT[...]
        STIN[s] = state_in
        inter = jnp.exp(cume) * dot(c[rows, :], state_in.astype(BF))
        YI[rows, :] = inter
        whole = YF[rows, :] + inter
        YF[rows, :] = whole
        YT[:, aligned(TOK * y + Q * s, Q, Q)] = whole.T.astype(BF)
        ENT[...] = jnp.exp(cume[Q - 1 : Q, :]) * state_in + PART[s]

    loop(0, SPANS, outputs)
    y_gather = Gather(
        lambda p: YT.at[:, aligned(TOK * p, TOK, TOK)],
        lambda p, h: YT.at[pl.ds(COLS // 2 * h, COLS // 2), aligned(TOK * p, TOK, TOK)],
        lambda i: yag_sem.at[0, i],
        lambda i: yag_sem.at[1, i],
        y, prv(y), nxt(y), at_y,
    )
    y_gather.start()
    x_gathers[1].forward()
    to_sibling(1, 1).start()
    to_sibling(1, 2).start()
    x_gathers[0].finish()
    to_sibling(0, 3).start()
    w_gather.finish()
    x_gathers[1].finish()
    to_sibling(1, 3).start()
    for t in range(2):
        for j in range(4):
            from_sibling(t, j)

    def head_term(block, h):
        return dot(G[aligned(TOK * block + TOK // 2 * h, TOK // 2, TOK // 2), :], W[...])

    def weight_term(block, h):
        return dot(YT[pl.ds(COLS // 2 * h, COLS // 2), :], G[:, aligned(TOK * block, TOK, TOK)])

    heads = Scatter(
        head_term, TOK, h_far, h_right, h_left, h_vl, h_vr, h_fl, h_fr, h_own,
        hrs_sem.at[0], hrs_sem.at[1], y, at_y,
    )
    weights = Scatter(
        weight_term, COLS, w_far, w_right, w_left, w_vl, w_vr, w_fl, w_fr, w_own,
        wrs_sem.at[0], wrs_sem.at[1], z, at_z,
    )
    heads.first()
    y_gather.forward()
    y_gather.finish()
    weights.first()
    heads.second()
    heads.last()
    weights.second()
    weights.last()
    heads.finish()

    def settle(i):
        rows = aligned(128 * i, 128, 128)
        GK[rows, :] = (h_own[rows, :] + h_fl[rows, :].astype(F32) + h_fr[rows, :].astype(F32)).astype(BF)

    loop(0, TOK // 128, settle)

    OPN[...] = jnp.zeros_like(OPN)

    def local_adjoint(i):
        s = SPANS - 1 - i
        rows = aligned(Q * s, Q, Q)
        cume = CUME[rows, :]
        gh = (jnp.exp(cume) * GK[rows, :].astype(F32)).astype(BF)
        GH[rows, :] = gh
        part = dot(c[rows, :], gh, TN)
        PART[s] = part
        OPN[...] = jnp.exp(cume[Q - 1 : Q, :]) * OPN[...] + part

    loop(0, SPANS, local_adjoint)
    backward = Exchange(OPN, RA, EA, AEN, bex_sem, ci, hi)
    backward.start()

    def inside_grad(s):
        rows = aligned(Q * s, Q, Q)
        total = jnp.zeros((Q, Q), F32)
        for k in range(PAIRS):
            cols = pl.ds(Q * k, Q)
            gk = GK[rows, cols].astype(F32)
            stack = jnp.concatenate(
                [jnp.where(left_half, gk, 0.0), jnp.where(left_half, 0.0, gk)], axis=0
            ).astype(BF)
            weighted = L[PAIRS * s + k] * dot(stack, XS[rows, cols], NT)
            total = total + weighted[:Q] + weighted[Q:]
            IG[rows, cols] = dot(MS[PAIRS * s + k], stack, TN)
        SG[s] = total.astype(BF)

    loop(0, SPANS // 2, inside_grad)
    backward.landed()
    state = jnp.zeros((8, COLS), F32)
    for i in reversed(range(N_CTX)):
        EA[i] = state
        state = DEC[i] * state + RA[i]
    backward.reply()
    loop(SPANS // 2, SPANS, inside_grad)
    backward.replied()

    def closing(i):
        s = SPANS - 1 - i
        rows = aligned(Q * s, Q, Q)
        cume = CUME[rows, :]
        total = cume[Q - 1 : Q, :]
        adjoint = AEN[...]
        low = adjoint.astype(BF)
        in_grad = IG[rows, :] + jnp.exp(total - cume) * dot(b[rows, :], low)
        IGB[rows, :] = in_grad.astype(BF)
        sg = SG[s]
        BC[rows, :N] = (dot(sg, c[rows, :], TN) + dot(XT[rows, :], low, NT)).astype(BF)
        BC[rows, N:] = (dot(sg, b[rows, :]) + dot(GH[rows, :], STIN[s].astype(BF), NT)).astype(BF)
        gk = GK[rows, :].astype(F32)
        step = XS[rows, :].astype(F32) * in_grad - gk * YF[rows, :]
        start = jnp.sum(gk * YI[rows, :], axis=0, keepdims=True) + jnp.exp(total) * jnp.sum(
            adjoint * STIN[s], axis=0, keepdims=True
        )
        steps = dot(E16[...], step, NT, precision=HIGH)
        starts = dot(E16[...], jnp.broadcast_to(start, (Q, COLS)), NT, precision=HIGH)
        out_decay[:, rows] = (starts + dot(steps, below, precision=HIGH)) * (1.0 / math.sqrt(P_SIZE * D))
        AEN[...] = jnp.exp(total) * adjoint + PART[s]

    loop(0, SPANS, closing)

    share = TOK // N_HEAD

    def bc_out(k, at):
        to = lax.rem(hi + k, N_HEAD)
        return rcopy(
            BC.at[aligned(share * to, share, share), :], RB.at[at], bc_sem.at[0, k], bc_sem.at[1, k], (ci, to)
        )

    def bc_back(k, at):
        to = lax.rem(hi + k, N_HEAD)
        return rcopy(SUM, BCF.at[aligned(share * at, share, share), :], bc_sem.at[2, k], bc_sem.at[3, k], (ci, to))

    loop(1, N_HEAD, lambda k: bc_out(k, hi).start())
    RB[hi] = BC[aligned(share * hi, share, share), :]

    def spread_in(i):
        rows = aligned(128 * i, 128, 128)
        out_ig[rows, :] = dot(IGB[rows, :], S[...], NT).astype(BF)

    loop(0, TOK // 128, spread_in)
    loop(1, N_HEAD, lambda k: bc_out(k, lax.rem(hi + N_HEAD - k, N_HEAD)).wait_recv())
    summed = RB[0].astype(F32)
    for i in range(1, N_HEAD):
        summed = summed + RB[i].astype(F32)
    SUM[...] = summed.astype(BF)
    BCF[aligned(share * hi, share, share), :] = SUM[...]
    loop(1, N_HEAD, lambda k: bc_back(k, hi).start())

    weights.finish()

    def spread_w(i):
        cols = aligned(128 * i, 128, 128)
        block = (
            (w_own[:, cols] + w_fl[:, cols].astype(F32) + w_fr[:, cols].astype(F32)) * (1.0 / math.sqrt(D))
        ).astype(BF)
        out_w[cols, :] = dot(block, S[...], (((0,), (1,)), ((), ()))).astype(BF)

    loop(0, TOK // 128, spread_w)

    loop(1, N_HEAD, lambda k: bc_back(k, lax.rem(hi + N_HEAD - k, N_HEAD)).wait_recv())
    out_b[...] = BCF[:, :N].astype(F32) / math.sqrt(KEPT * P_SIZE)
    out_c[...] = BCF[:, N:].astype(F32) * math.sqrt(N / (KEPT * P_SIZE * D))

    for p in range(2):

        @pl.when(2 * cc + p != y)
        def _():
            rcopy(
                g.at[:, pl.ds(TOK * p, TOK)], g_tile(y, xx), a2a_sem.at[0, p], a2a_sem.at[1, 0], sibling
            ).wait_send()

    for gather in (w_gather, y_gather, *x_gathers):
        gather.drain()
    for t in range(2):
        for j in range(4):
            to_sibling(t, j).wait_send()
    heads.drain()
    weights.drain()
    forward.drain()
    backward.drain()

    def bc_drain(k):
        bc_out(k, hi).wait_send()
        bc_back(k, hi).wait_send()

    loop(1, N_HEAD, bc_drain)


def per_device(g_out, w_out, x_act, b_proj, c_proj, log_decay, kept_heads):
    head = lax.axis_index("head")
    local = kept_heads - head * GROUP
    mine = (local >= 0) & (local < GROUP)
    rank = jnp.cumsum(mine.astype(jnp.int32)) - 1
    slots = jnp.arange(GROUP, dtype=jnp.int32)
    hit = mine[None, :] & (rank[None, :] == slots[:, None])
    head_of_slot = jnp.sum(jnp.where(hit, local[None, :] + 1, 0), axis=1) - 1
    sel = (head_of_slot[:, None] == slots[None, :]).astype(F32)
    headof = jnp.repeat(head_of_slot[:CAP], P_SIZE)
    colidx = jnp.where(headof >= 0, headof * P_SIZE + jnp.arange(COLS, dtype=jnp.int32) % P_SIZE, -1)
    vmem = pl.BlockSpec(memory_space=pltpu.VMEM)
    buf = pltpu.VMEM
    dma = pltpu.SemaphoreType.DMA

    def ring(rows, cols):
        h = rows // 2
        return [
            buf((rows, cols), BF), buf((rows, cols), BF), buf((rows, cols), BF), buf((h, cols), BF), buf((h, cols), BF),
            buf((rows, cols), BF), buf((rows, cols), BF), buf((rows, cols), F32),
        ]

    return pl.pallas_call(
        kernel,
        out_shape=(
            jax.ShapeDtypeStruct((TOK, WIDE), BF),
            jax.ShapeDtypeStruct((TOK, N), F32),
            jax.ShapeDtypeStruct((TOK, N), F32),
            jax.ShapeDtypeStruct((GROUP, TOK), F32),
            jax.ShapeDtypeStruct((TOK, WIDE), BF),
        ),
        in_specs=[pl.BlockSpec(memory_space=pl.ANY)] + [vmem] * 8,
        out_specs=[vmem] * 5,
        scratch_shapes=[
            buf((WIDE, COLS), BF), buf((GROUP, COLS), F32),
            buf((4 * TOK, 4 * TOK), BF), buf((4 * TOK, COLS), BF), buf((COLS, 4 * TOK), BF),
            buf((TOK, COLS), BF), buf((TOK, COLS), BF), buf((TOK, COLS), F32), buf((GROUP, TOK), F32),
            buf((SPANS, N, COLS), F32), buf((SPANS, N, COLS), F32), buf((TOK, COLS), F32), buf((TOK, COLS), F32),
            buf((SPANS * PAIRS, 2 * Q, Q), F32), buf((SPANS * PAIRS, 2 * Q, Q), BF),
            buf((TOK, COLS), BF), buf((TOK, COLS), BF), buf((TOK, COLS), F32), buf((TOK, COLS), BF),
            buf((SPANS, Q, Q), BF),
            buf((N, COLS + 128), F32), buf((N_CTX, 8, COLS + 128), F32), buf((N_CTX, 8, COLS), F32),
            buf((N, COLS), F32), buf((N_CTX, 8, COLS), F32),
            buf((N, COLS), F32), buf((N_CTX, 8, COLS), F32), buf((N_CTX, 8, COLS), F32), buf((N, COLS), F32),
            buf((TOK, 2 * N), BF), buf((N_HEAD, TOK // N_HEAD, 2 * N), BF), buf((TOK // N_HEAD, 2 * N), BF),
            buf((TOK, 2 * N), BF),
            *ring(TOK, COLS), *ring(COLS, TOK),
            dma((1,)), dma((2, 2)), dma((2, 4)), dma((2, 4)), dma((2, 2, 4)), dma((2, 4)), dma((2, 4)),
            dma((2, 6)), dma((2, 6)), dma((4, N_CTX)), dma((4, N_CTX)), dma((4, N_HEAD)),
        ],
        compiler_params=pltpu.CompilerParams(
            collective_id=0, has_side_effects=True, vmem_limit_bytes=62 * 1024 * 1024
        ),
        cost_estimate=pl.CostEstimate(flops=14_000_000_000, bytes_accessed=8_000_000, transcendentals=4_000_000),
    )(
        g_out, w_out, x_act, b_proj, c_proj, log_decay,
        jnp.broadcast_to(colidx[None, :], (8, COLS)), jnp.broadcast_to(headof[None, :], (8, COLS)), sel,
    )


def solution(mesh):
    in_specs = (
        P("ctx", "head"),
        P("ctx", "head"),
        P("ctx", "head"),
        P("ctx", None),
        P("ctx", None),
        P("head", "ctx"),
        P(),
    )
    out_specs = (
        P("ctx", "head"),
        P("ctx", None),
        P("ctx", None),
        P("head", "ctx"),
        P("ctx", "head"),
    )
    return jax.shard_map(
        per_device, mesh=mesh, in_specs=in_specs, out_specs=out_specs, check_vma=False
    )
```

```python
import math

import jax
import jax.numpy as jnp
from jax import lax
from jax.experimental import pallas as pl
from jax.experimental.pallas import tpu as pltpu
from jax.sharding import PartitionSpec as P

D = 8192
P_SIZE = 64
N = 128
KEPT = 64
Q = 128
TOK = 512
SPANS = TOK // Q
GROUP = 16
CAP = 12
COLS = CAP * P_SIZE
WIDE = GROUP * P_SIZE
PAIRS = CAP // 2
N_CTX = 16
N_HEAD = 8
HALF = COLS // 2
VMEM_LIMIT = 62 * 1024 * 1024

F32 = jnp.float32
BF = jnp.bfloat16
HIGH = lax.Precision.HIGHEST
MESH = pl.DeviceIdType.MESH
NN = (((1,), (0,)), ((), ()))
NT = (((1,), (1,)), ((), ()))
TN = (((0,), (0,)), ((), ()))


def dot(a, b, dims=NN, precision=None):
    return lax.dot_general(a, b, dims, precision=precision, preferred_element_type=F32)


def rcopy(src, dst, send_sem, recv_sem, device):
    return pltpu.make_async_remote_copy(
        src_ref=src,
        dst_ref=dst,
        send_sem=send_sem,
        recv_sem=recv_sem,
        device_id=device,
        device_id_type=MESH,
    )


def aligned(start, size, unit):
    return pl.ds(pl.multiple_of(start, unit), size)


def loop(lo, hi, body):
    def step(i, carry):
        body(i)
        return carry

    lax.fori_loop(lo, hi, step, 0)


class Gather:
    def __init__(self, block, half, send, recv, me, left, right, device):
        self.block, self.half, self.send, self.recv = block, half, send, recv
        self.me, self.left, self.right = me, left, right
        self.to_left, self.to_right = device(left), device(right)
        self.far = lax.rem(me + 2, 4)

    def copy(self, i):
        ref = (
            lambda: self.block(self.me),
            lambda: self.block(self.me),
            lambda: self.half(self.left, 0),
            lambda: self.half(self.right, 1),
        )[i]()
        return rcopy(ref, ref, self.send(i), self.recv(i), self.to_left if i % 2 else self.to_right)

    def landed(self, slot, ref):
        rcopy(ref, ref, self.send(slot), self.recv(slot), self.to_right).wait_recv()

    def start(self):
        self.copy(0).start()
        self.copy(1).start()

    def forward(self):
        self.landed(0, self.block(self.left))
        self.copy(2).start()
        self.landed(1, self.block(self.right))
        self.copy(3).start()

    def finish(self):
        self.landed(2, self.half(self.far, 0))
        self.landed(3, self.half(self.far, 1))

    def drain(self):
        for i in range(4):
            self.copy(i).wait_send()


class Scatter:
    def __init__(self, term, rows, far, right, left, via_l, via_r, from_l, from_r, own, send, recv, me, device):
        self.term, self.h = term, rows // 2
        self.far_buf, self.right_buf, self.left_buf = far, right, left
        self.via_l, self.via_r, self.from_l, self.from_r, self.own = via_l, via_r, from_l, from_r, own
        self.send, self.recv = send, recv
        self.me = me
        self.right, self.left, self.far = lax.rem(me + 1, 4), lax.rem(me + 3, 4), lax.rem(me + 2, 4)
        self.to_right, self.to_left = device(self.right), device(self.left)

    def copy(self, i):
        lo, hi = pl.ds(0, self.h), pl.ds(self.h, self.h)
        src, dst, to = (
            (self.far_buf.at[lo], self.via_l, self.to_right),
            (self.far_buf.at[hi], self.via_r, self.to_left),
            (self.right_buf.at[hi], self.from_l.at[hi], self.to_right),
            (self.left_buf.at[lo], self.from_r.at[lo], self.to_left),
            (self.right_buf.at[lo], self.from_l.at[lo], self.to_right),
            (self.left_buf.at[hi], self.from_r.at[hi], self.to_left),
        )[i]
        return rcopy(src, dst, self.send.at[i], self.recv.at[i], to)

    def first(self):
        h = self.h
        self.far_buf[...] = self.term(self.far).astype(BF)
        self.copy(0).start()
        self.copy(1).start()
        term = self.term(self.right)
        self.right_buf[h:] = term[h:].astype(BF)
        self.copy(2).start()
        self.own[:h] = term[:h]
        term = self.term(self.left)
        self.left_buf[:h] = term[:h].astype(BF)
        self.copy(3).start()
        self.own[h:] = term[h:]

    def second(self):
        h = self.h
        self.copy(0).wait_recv()
        self.right_buf[:h] = (self.own[:h] + self.via_l[...].astype(F32)).astype(BF)
        self.copy(4).start()
        self.copy(1).wait_recv()
        self.left_buf[h:] = (self.own[h:] + self.via_r[...].astype(F32)).astype(BF)
        self.copy(5).start()

    def last(self):
        self.own[...] = self.term(self.me)

    def finish(self):
        for i in (2, 3, 4, 5):
            self.copy(i).wait_recv()

    def result(self, rows, cols=slice(None)):
        return self.own[rows, cols] + self.from_l[rows, cols].astype(F32) + self.from_r[rows, cols].astype(F32)

    def drain(self):
        for i in range(6):
            self.copy(i).wait_send()


class Exchange:
    def __init__(self, source, landed, back, entering, sems, ci, hi):
        self.source, self.landed_ref, self.back, self.entering = source, landed, back, entering
        self.sems, self.ci, self.hi = sems, ci, hi

    def cut(self, r):
        return aligned(16 * (r // 2), 16, 16), aligned(HALF * lax.rem(r, 2), HALF, 128)

    def slot(self, r):
        return aligned(16 * r, 16, 16)

    def out_copy(self, k, at):
        to = lax.rem(self.ci + k, N_CTX)
        return rcopy(
            self.source.at[self.cut(to)], self.landed_ref.at[self.slot(at), :],
            self.sems.at[0, k], self.sems.at[1, k], (to, self.hi),
        )

    def back_copy(self, k, at):
        to = lax.rem(self.ci + k, N_CTX)
        return rcopy(
            self.back.at[self.slot(to), :], self.entering.at[self.cut(at)],
            self.sems.at[2, k], self.sems.at[3, k], (to, self.hi),
        )

    def start(self):
        loop(1, N_CTX, lambda k: self.out_copy(k, self.ci).start())
        self.landed_ref[self.slot(self.ci), :] = self.source[self.cut(self.ci)]

    def landed(self):
        loop(1, N_CTX, lambda k: self.out_copy(k, lax.rem(self.ci + N_CTX - k, N_CTX)).wait_recv())

    def scan(self, decays, order):
        state = jnp.zeros((16, HALF), F32)
        for i in order:
            rows = pl.ds(16 * i, 16)
            self.back[rows, :] = state.astype(BF)
            state = decays[pl.ds(8 * i, 1), :] * state + self.landed_ref[rows, :].astype(F32)

    def reply(self):
        loop(1, N_CTX, lambda k: self.back_copy(k, self.ci).start())
        self.entering[self.cut(self.ci)] = self.back[self.slot(self.ci), :]

    def replied(self):
        loop(1, N_CTX, lambda k: self.back_copy(k, lax.rem(self.ci + N_CTX - k, N_CTX)).wait_recv())

    def drain(self):
        def one(k):
            self.out_copy(k, self.ci).wait_send()
            self.back_copy(k, self.ci).wait_send()

        loop(1, N_CTX, one)


class HeadSum:
    def __init__(self, part, landed, total, whole, sems, ci, hi):
        self.part, self.landed_ref, self.total, self.whole = part, landed, total, whole
        self.sems, self.ci, self.hi = sems, ci, hi

    def share(self, r):
        return aligned(TOK // N_HEAD * r, TOK // N_HEAD, TOK // N_HEAD)

    def out_copy(self, k, at):
        to = lax.rem(self.hi + k, N_HEAD)
        return rcopy(
            self.part.at[self.share(to), :], self.landed_ref.at[at],
            self.sems.at[0, k], self.sems.at[1, k], (self.ci, to),
        )

    def back_copy(self, k, at):
        to = lax.rem(self.hi + k, N_HEAD)
        return rcopy(
            self.total, self.whole.at[self.share(at), :], self.sems.at[2, k], self.sems.at[3, k], (self.ci, to)
        )

    def start(self):
        loop(1, N_HEAD, lambda k: self.out_copy(k, self.hi).start())
        self.landed_ref[self.hi] = self.part[self.share(self.hi), :]

    def reduce(self):
        loop(1, N_HEAD, lambda k: self.out_copy(k, lax.rem(self.hi + N_HEAD - k, N_HEAD)).wait_recv())
        total = self.landed_ref[0].astype(F32)
        for i in range(1, N_HEAD):
            total = total + self.landed_ref[i].astype(F32)
        self.total[...] = total.astype(BF)
        loop(1, N_HEAD, lambda k: self.back_copy(k, self.hi).start())
        self.whole[self.share(self.hi), :] = self.total[...]

    def finish(self):
        loop(1, N_HEAD, lambda k: self.back_copy(k, lax.rem(self.hi + N_HEAD - k, N_HEAD)).wait_recv())

    def drain(self):
        def one(k):
            self.out_copy(k, self.hi).wait_send()
            self.back_copy(k, self.hi).wait_send()

        loop(1, N_HEAD, one)


def one_hot(rows, cols, hit):
    r = lax.broadcasted_iota(jnp.int32, (rows, cols), 0)
    k = lax.broadcasted_iota(jnp.int32, (rows, cols), 1)
    return jnp.where(hit(r, k), 1.0, 0.0).astype(F32)


def kernel(
    kept, g, w_in, x_in, b_in, c_in, logd_in,
    out_ig, out_b, out_c, out_decay, out_w,
    w, x, b, c, logd, S, E16, E16B, G, W, YT, XS, XT, CUME, CUMR, PART, STIN, ADJ, YF, YI, L, MS, GK, GH, IG, IGB, B0,
    TOT, RD, DEC, ST, FL, FB, FE, AL, AB, AE, BP, BL, BT, BW, CP, CL, CT, CW, O_IG, O_B, O_C, O_D, O_W,
    a_far, a_right, a_left, a_vl, a_vr, a_fl, a_fr, a_own,
    b_far, b_right, b_left, b_vl, b_vr, b_fl, b_fr, b_own,
    w_far, w_right, w_left, w_vl, w_vr, w_fl, w_fr, w_own,
    loc_sem, own_sem, a2a_sem, xs_sem, xr_sem, sib_sem, wag_sem, yag_sem, hrs_sem, wrs_sem, dec_sem, fex_sem, bex_sem,
    b_sem, c_sem, out_sem,
):
    ci, hi = lax.axis_index("ctx"), lax.axis_index("head")
    z, y = ci // 4, lax.rem(ci, 4)
    xx, cc = hi // 2, lax.rem(hi, 2)
    half = y // 2
    cross = lax.rem(half + cc, 2)
    at_x = lambda p: (ci, 2 * p + cc)
    at_y = lambda p: (4 * z + p, hi)
    at_z = lambda p: (4 * p + y, hi)
    sibling = (ci, 2 * xx + 1 - cc)
    nxt = lambda p: lax.rem(p + 1, 4)
    prv = lambda p: lax.rem(p + 3, 4)

    barrier = pltpu.get_barrier_semaphore()

    def greet(device):
        pl.semaphore_signal(barrier, inc=1, device_id=device, device_id_type=MESH)

    loop(1, N_CTX, lambda k: greet((lax.rem(ci + k, N_CTX), hi)))
    loop(1, N_HEAD, lambda k: greet((ci, lax.rem(hi + k, N_HEAD))))

    @pl.when(cross == 1)
    def _():
        for p in range(2):
            greet((4 * z + 2 * cc + p, 2 * xx + 1 - cc))

    loads = [
        pltpu.make_async_copy(src, dst, loc_sem.at[i])
        for i, (src, dst) in enumerate(((w_in, w), (x_in, x), (b_in, b), (c_in, c), (logd_in, logd)))
    ]
    for load in loads:
        load.start()

    lanes = lax.broadcasted_iota(jnp.int32, (8, COLS), 1)

    def place(k, carry):
        headof, rank = carry
        local = kept[k] - GROUP * hi
        mine = (local >= 0) & (local < GROUP)
        headof = jnp.where(lanes // P_SIZE == jnp.where(mine, rank, -1), local, headof)
        return headof, rank + jnp.where(mine, 1, 0)

    headof, _ = lax.fori_loop(0, KEPT, place, (jnp.full((8, COLS), -1, jnp.int32), jnp.int32(0)))
    headof = headof[0:1, :]
    colidx = jnp.where(headof >= 0, P_SIZE * headof + lax.rem(lanes[0:1, :], P_SIZE), -1)

    def build(i):
        rows = lax.broadcasted_iota(jnp.int32, (128, COLS), 0) + 128 * i
        S[aligned(128 * i, 128, 128), :] = jnp.where(rows == colidx, 1.0, 0.0).astype(BF)

    loop(0, WIDE // 128, build)
    E16[...] = jnp.where(lax.broadcasted_iota(jnp.int32, (GROUP, COLS), 0) == headof, 1.0, 0.0).astype(F32)
    E16B[...] = E16[...].astype(BF)

    pl.semaphore_wait(barrier, N_CTX - 1 + N_HEAD - 1 + 2 * cross)

    def g_tile(token, feature, q):
        return G.at[token, :, q, :, aligned(TOK * feature, TOK, TOK)]

    def quarter(q, p):
        return g.at[:, q, :, pl.ds(TOK * p, TOK)]

    def a2a_copy(q, p, slot):
        return rcopy(
            quarter(q, p), g_tile(y, xx, q), a2a_sem.at[0, q, p], a2a_sem.at[1, q, slot], (4 * z + 2 * cc + p, 2 * xx + half)
        )

    def a2a_start(q):
        for p in range(2):

            @pl.when(2 * cc + p == y)
            def _():
                pltpu.make_async_copy(quarter(q, p), g_tile(y, xx, q), own_sem.at[q]).start()

            @pl.when(2 * cc + p != y)
            def _():
                a2a_copy(q, p, lax.rem(y, 2)).start()

    def a2a_landed(q, t):
        token = 2 * cc + t

        @pl.when(token == y)
        def _():
            pltpu.make_async_copy(quarter(q, 0), g_tile(token, xx, q), own_sem.at[q]).wait()

        @pl.when(token != y)
        def _():
            rcopy(
                quarter(q, 0), g_tile(token, xx, q), a2a_sem.at[0, q, t], a2a_sem.at[1, q, t], sibling
            ).wait_recv()

    a2a_start(0)

    for load in loads:
        load.wait()

    def pick_w(i):
        W[aligned(TOK * z + 128 * i, 128, 128), :] = dot(w[aligned(128 * i, 128, 128), :], S[...]).astype(BF)

    loop(0, TOK // 128, pick_w)
    w_gather = Gather(
        lambda p: W.at[aligned(TOK * p, TOK, TOK), :],
        lambda p, h: W.at[aligned(TOK * p + TOK // 2 * h, TOK // 2, TOK // 2), :],
        lambda i: wag_sem.at[0, i],
        lambda i: wag_sem.at[1, i],
        z, prv(z), nxt(z), at_z,
    )
    w_gather.start()

    upto = one_hot(Q, Q, lambda r, k: r <= k)
    pick = one_hot(COLS, 128, lambda r, k: r == P_SIZE * k)
    slots = dot(E16[...], pick)[:, :GROUP]

    def decays(s):
        rows = aligned(Q * s, Q, Q)
        cum = dot(logd[:, rows], upto, precision=HIGH)
        CUMR[:, rows] = dot(slots, cum, TN, precision=HIGH)
        CUME[rows, :] = dot(cum, E16[...], TN, precision=HIGH)

    loop(0, SPANS, decays)
    totals = sum(CUMR[:, pl.ds(Q * s + Q - 1, 1)] for s in range(SPANS))
    TOT[...] = dot(jnp.broadcast_to(totals, (GROUP, 8)), one_hot(GROUP, 128, lambda r, k: r == k), TN, precision=HIGH)

    def decay_copy(k, at):
        to = lax.rem(ci + k, N_CTX)
        return rcopy(TOT, RD.at[aligned(8 * at, 8, 8), :], dec_sem.at[0, k], dec_sem.at[1, k], (to, hi))

    loop(1, N_CTX, lambda k: decay_copy(k, ci).start())
    RD[aligned(8 * ci, 8, 8), :] = TOT[...]

    STIN[0] = jnp.zeros((N, COLS), F32)

    def local_states(s):
        rows = aligned(Q * s, Q, Q)
        cume = CUME[rows, :]
        total = cume[Q - 1 : Q, :]
        xs = dot(x[rows, :], S[...])
        XS[rows, :] = xs.astype(BF)
        xt = (jnp.exp(total - cume) * xs).astype(BF)
        XT[rows, :] = xt
        part = dot(b[rows, :], xt, TN)
        PART[s] = part
        STIN[0] = jnp.exp(total) * STIN[0] + part

    loop(0, SPANS, local_states)
    ST[0] = STIN[0].astype(BF)
    forward = Exchange(ST.at[0], FL, FB, FE, fex_sem, ci, hi)
    forward.start()

    def x_gather(q, t):
        token = 2 * cc + t
        return Gather(
            lambda p: g_tile(token, p, q),
            lambda p, h: G.at[token, h, q, :, aligned(TOK * p, TOK, TOK)],
            lambda i: xs_sem.at[q, t, i],
            lambda i: xr_sem.at[q, t, i],
            xx, prv(xx), nxt(xx), at_x,
        )

    x_gathers = [[x_gather(q, t) for t in range(2)] for q in range(2)]
    ring_x = (xx, prv(xx), nxt(xx), lax.rem(xx + 2, 4))

    def sibling_copy(q, t, j, core):
        tile = g_tile(2 * core + t, ring_x[j], q)
        return rcopy(tile, tile, sib_sem.at[0, q, t, j], sib_sem.at[1, q, t, j], sibling)

    def x_start(q):
        for t in range(2):
            a2a_landed(q, t)
            x_gathers[q][t].start()
            sibling_copy(q, t, 0, cc).start()

    def x_forward(q):
        for t in range(2):
            x_gathers[q][t].forward()
            sibling_copy(q, t, 1, cc).start()
            sibling_copy(q, t, 2, cc).start()

    def x_finish(q):
        for t in range(2):
            x_gathers[q][t].finish()
            sibling_copy(q, t, 3, cc).start()
        for t in range(2):
            for j in range(4):
                sibling_copy(q, t, j, 1 - cc).wait_recv()

    x_start(0)
    a2a_start(1)

    sub = lax.broadcasted_iota(jnp.int32, (Q, Q), 0)
    lane = lax.broadcasted_iota(jnp.int32, (Q, Q), 1)
    left_half = lane < P_SIZE
    causal = lane <= sub

    def inside(s):
        rows = aligned(Q * s, Q, Q)
        cb = dot(c[rows, :], b[rows, :], NT)
        for k in range(PAIRS):
            cols = pl.ds(Q * k, Q)
            for h in range(2):
                head = 2 * k + h
                differ = CUME[rows, pl.ds(P_SIZE * head, 1)] - CUMR[pl.ds(head, 1), rows]
                low = jnp.where(causal, jnp.exp(jnp.where(causal, differ, 0.0)), 0.0)
                L[PAIRS * s + k, pl.ds(Q * h, Q), :] = low
                MS[PAIRS * s + k, pl.ds(Q * h, Q), :] = (low * cb).astype(BF)
            both = dot(MS[PAIRS * s + k], XS[rows, cols])
            YF[rows, cols] = jnp.where(left_half, both[:Q], both[Q:])

    loop(0, SPANS, inside)

    loop(1, N_CTX, lambda k: decay_copy(k, lax.rem(ci + N_CTX - k, N_CTX)).wait_recv())
    first_slot = CAP // 2 * lax.rem(ci, 2)
    DEC[...] = jnp.exp(dot(RD[...], one_hot(128, HALF, lambda r, k: r == k // P_SIZE + first_slot), precision=HIGH))
    forward.landed()
    forward.scan(DEC, range(N_CTX))
    forward.reply()
    w_gather.forward()
    forward.replied()
    STIN[0] = FE[...].astype(F32)

    def outputs(s):
        rows = aligned(Q * s, Q, Q)
        cume = CUME[rows, :]
        state_in = STIN[s]
        inter = jnp.exp(cume) * dot(c[rows, :], state_in.astype(BF))
        YI[rows, :] = inter
        whole = YF[rows, :] + inter
        YF[rows, :] = whole
        YT[:, aligned(TOK * y + Q * s, Q, Q)] = whole.T.astype(BF)
        STIN[s + 1] = jnp.exp(cume[Q - 1 : Q, :]) * state_in + PART[s]

    loop(0, SPANS, outputs)
    y_gather = Gather(
        lambda p: YT.at[:, aligned(TOK * p, TOK, TOK)],
        lambda p, h: YT.at[pl.ds(HALF * h, HALF), aligned(TOK * p, TOK, TOK)],
        lambda i: yag_sem.at[0, i],
        lambda i: yag_sem.at[1, i],
        y, prv(y), nxt(y), at_y,
    )
    y_gather.start()

    def head_term(q):
        return lambda block: dot(G[block, :, q].reshape(TOK // 2, 4 * TOK), W[...])

    def weight_term(block):
        return dot(YT[...], G[:, :, :, :, aligned(TOK * block, TOK, TOK)].reshape(4 * TOK, TOK))

    heads = (
        Scatter(
            head_term(0), TOK // 2, a_far, a_right, a_left, a_vl, a_vr, a_fl, a_fr, a_own,
            hrs_sem.at[0, 0], hrs_sem.at[0, 1], y, at_y,
        ),
        Scatter(
            head_term(1), TOK // 2, b_far, b_right, b_left, b_vl, b_vr, b_fl, b_fr, b_own,
            hrs_sem.at[1, 0], hrs_sem.at[1, 1], y, at_y,
        ),
    )
    weights = Scatter(
        weight_term, COLS, w_far, w_right, w_left, w_vl, w_vr, w_fl, w_fr, w_own,
        wrs_sem.at[0], wrs_sem.at[1], z, at_z,
    )

    def local_adjoint(s):
        rows = pl.ds(Q * s, Q)
        GK[rows, :] = heads[s % 2].result(pl.ds(Q * (s // 2), Q)).astype(BF)
        gh = (jnp.exp(CUME[rows, :]) * GK[rows, :].astype(F32)).astype(BF)
        GH[rows, :] = gh
        PART[s] = dot(c[rows, :], gh, TN)

    def inside_grad(s):
        rows = aligned(Q * s, Q, Q)
        total = jnp.zeros((Q, Q), F32)
        for k in range(PAIRS):
            cols = pl.ds(Q * k, Q)
            gk = GK[rows, cols].astype(F32)
            stack = jnp.concatenate(
                [jnp.where(left_half, gk, 0.0), jnp.where(left_half, 0.0, gk)], axis=0
            ).astype(BF)
            weighted = L[PAIRS * s + k] * dot(stack, XS[rows, cols], NT)
            total = total + weighted[:Q] + weighted[Q:]
            IG[rows, cols] = dot(MS[PAIRS * s + k], stack, TN)
        sg = total.astype(BF)
        B0[rows, :] = dot(sg, c[rows, :], TN)
        CP[rows, :] = (dot(sg, b[rows, :]) + dot(GH[rows, :], STIN[s].astype(BF), NT)).astype(BF)

    x_forward(0)
    x_start(1)
    w_gather.finish()
    x_finish(0)
    heads[0].first()
    x_forward(1)
    y_gather.forward()
    heads[0].second()
    heads[0].last()
    x_finish(1)
    heads[1].first()
    heads[0].finish()
    local_adjoint(0)
    local_adjoint(2)
    y_gather.finish()
    heads[1].second()
    weights.first()
    heads[1].last()
    inside_grad(0)
    inside_grad(2)
    weights.second()
    heads[1].finish()
    local_adjoint(1)
    local_adjoint(3)

    ADJ[0] = PART[SPANS - 1]
    for s in reversed(range(SPANS - 1)):
        ADJ[0] = jnp.exp(CUME[pl.ds(Q * s + Q - 1, 1), :]) * ADJ[0] + PART[s]
    ST[1] = ADJ[0].astype(BF)
    backward = Exchange(ST.at[1], AL, AB, AE, bex_sem, ci, hi)
    backward.start()
    inside_grad(1)
    inside_grad(3)
    c_sum = HeadSum(CP, CL, CT, CW, c_sem, ci, hi)
    c_sum.start()
    backward.landed()
    backward.scan(DEC, reversed(range(N_CTX)))
    backward.reply()
    weights.last()
    c_sum.reduce()
    backward.replied()
    ADJ[SPANS] = AE[...].astype(F32)
    for s in reversed(range(SPANS)):
        rows = pl.ds(Q * s, Q)
        BP[rows, :] = (B0[rows, :] + dot(XT[rows, :], ADJ[s + 1].astype(BF), NT)).astype(BF)
        if s > 0:
            ADJ[s] = jnp.exp(CUME[pl.ds(Q * s + Q - 1, 1), :]) * ADJ[s + 1] + PART[s]
    b_sum = HeadSum(BP, BL, BT, BW, b_sem, ci, hi)
    b_sum.start()

    def closing(s):
        rows = aligned(Q * s, Q, Q)
        cume = CUME[rows, :]
        total = cume[Q - 1 : Q, :]
        adjoint = ADJ[s + 1]
        in_grad = IG[rows, :] + jnp.exp(total - cume) * dot(b[rows, :], adjoint.astype(BF))
        IGB[rows, :] = in_grad.astype(BF)
        gk = GK[rows, :].astype(F32)
        step = XS[rows, :].astype(F32) * in_grad - gk * YF[rows, :]
        start = jnp.sum(gk * YI[rows, :], axis=0, keepdims=True) + jnp.exp(total) * jnp.sum(
            adjoint * STIN[s], axis=0, keepdims=True
        )
        row = lax.broadcasted_iota(jnp.int32, (Q, COLS), 0)
        step = jnp.where(row == 0, start, pltpu.roll(step, 1, 0))
        high = step.astype(BF)
        rest = (step - high.astype(F32)).astype(BF)
        steps = dot(E16B[...], high, NT) + dot(E16B[...], rest, NT)
        O_D[:, rows] = dot(steps, upto, precision=HIGH) * (1.0 / math.sqrt(P_SIZE * D))

    def spread_in(i):
        rows = aligned(128 * i, 128, 128)
        O_IG[rows, :] = dot(IGB[rows, :], S[...], NT).astype(BF)

    def spread_w(i):
        cols = aligned(128 * i, 128, 128)
        block = (weights.result(slice(None), cols) * (1.0 / math.sqrt(D))).astype(BF)
        O_W[cols, :] = dot(block, S[...], (((0,), (1,)), ((), ()))).astype(BF)

    stores = [
        pltpu.make_async_copy(src, dst, out_sem.at[i])
        for i, (src, dst) in enumerate(((O_IG, out_ig), (O_B, out_b), (O_C, out_c), (O_D, out_decay), (O_W, out_w)))
    ]
    loop(0, SPANS, closing)
    stores[3].start()
    b_sum.reduce()
    loop(0, TOK // 128, spread_in)
    stores[0].start()
    weights.finish()
    loop(0, TOK // 128, spread_w)
    stores[4].start()
    c_sum.finish()
    O_C[...] = CW[...].astype(F32) * math.sqrt(N / (KEPT * P_SIZE * D))
    stores[2].start()
    b_sum.finish()
    O_B[...] = BW[...].astype(F32) / math.sqrt(KEPT * P_SIZE)
    stores[1].start()

    for q in range(2):
        for p in range(2):

            @pl.when(2 * cc + p != y)
            def _():
                a2a_copy(q, p, 0).wait_send()

        for t in range(2):
            x_gathers[q][t].drain()
            for j in range(4):
                sibling_copy(q, t, j, cc).wait_send()
        heads[q].drain()
    w_gather.drain()
    y_gather.drain()
    weights.drain()
    loop(1, N_CTX, lambda k: decay_copy(k, ci).wait_send())
    forward.drain()
    backward.drain()
    c_sum.drain()
    b_sum.drain()
    for store in stores:
        store.wait()


def hand_over(*refs):
    count = len(refs) // 3
    ins, outs, held, sems = refs[:count], refs[count : 2 * count], refs[2 * count : -1], refs[-1]
    reads = [pltpu.make_async_copy(ins[i], held[i], sems.at[0, i]) for i in range(count)]
    writes = [pltpu.make_async_copy(held[i], outs[i], sems.at[1, i]) for i in range(count)]
    for read in reads:
        read.start()
    for read, write in zip(reads, writes):
        read.wait()
        write.start()
    for write in writes:
        write.wait()


def per_device(g_out, w_out, x_act, b_proj, c_proj, log_decay, kept_heads):
    hbm = pl.BlockSpec(memory_space=pl.ANY)
    buf = pltpu.VMEM
    dma = pltpu.SemaphoreType.DMA

    def ring(rows, cols):
        h = rows // 2
        return [
            buf((rows, cols), BF), buf((rows, cols), BF), buf((rows, cols), BF), buf((h, cols), BF), buf((h, cols), BF),
            buf((rows, cols), BF), buf((rows, cols), BF), buf((rows, cols), F32),
        ]

    def head_sum():
        return [
            buf((TOK, N), BF), buf((N_HEAD, TOK // N_HEAD, N), BF), buf((TOK // N_HEAD, N), BF), buf((TOK, N), BF)
        ]

    outs = (
        jax.ShapeDtypeStruct((TOK, WIDE), BF),
        jax.ShapeDtypeStruct((TOK, N), F32),
        jax.ShapeDtypeStruct((TOK, N), F32),
        jax.ShapeDtypeStruct((GROUP, TOK), F32),
        jax.ShapeDtypeStruct((TOK, WIDE), BF),
    )
    results = pl.pallas_call(
        kernel,
        out_shape=outs,
        in_specs=[pl.BlockSpec(memory_space=pltpu.SMEM)] + [hbm] * 6,
        out_specs=[hbm] * 5,
        scratch_shapes=[
            buf((TOK, WIDE), BF), buf((TOK, WIDE), BF), buf((TOK, N), BF), buf((TOK, N), BF), buf((GROUP, TOK), F32),
            buf((WIDE, COLS), BF), buf((GROUP, COLS), F32), buf((GROUP, COLS), BF),
            buf((4, 2, 2, TOK // 4, 4 * TOK), BF), buf((4 * TOK, COLS), BF), buf((COLS, 4 * TOK), BF),
            buf((TOK, COLS), BF), buf((TOK, COLS), BF), buf((TOK, COLS), F32), buf((GROUP, TOK), F32),
            buf((SPANS, N, COLS), F32), buf((SPANS + 1, N, COLS), F32), buf((SPANS + 1, N, COLS), F32),
            buf((TOK, COLS), F32), buf((TOK, COLS), F32),
            buf((SPANS * PAIRS, 2 * Q, Q), F32), buf((SPANS * PAIRS, 2 * Q, Q), BF),
            buf((TOK, COLS), BF), buf((TOK, COLS), BF), buf((TOK, COLS), F32), buf((TOK, COLS), BF),
            buf((TOK, N), F32),
            buf((8, 128), F32), buf((8 * N_CTX, 128), F32), buf((8 * N_CTX, HALF), F32), buf((2, N, COLS), BF),
            buf((16 * N_CTX, HALF), BF), buf((16 * N_CTX, HALF), BF), buf((N, COLS), BF),
            buf((16 * N_CTX, HALF), BF), buf((16 * N_CTX, HALF), BF), buf((N, COLS), BF),
            *head_sum(), *head_sum(),
            buf((TOK, WIDE), BF), buf((TOK, N), F32), buf((TOK, N), F32), buf((GROUP, TOK), F32), buf((TOK, WIDE), BF),
            *ring(TOK // 2, COLS), *ring(TOK // 2, COLS), *ring(COLS, TOK),
            dma((5,)), dma((2,)), dma((2, 2, 2)), dma((2, 2, 4)), dma((2, 2, 4)), dma((2, 2, 2, 4)), dma((2, 4)),
            dma((2, 4)), dma((2, 2, 6)), dma((2, 6)), dma((2, N_CTX)), dma((4, N_CTX)), dma((4, N_CTX)),
            dma((4, N_HEAD)), dma((4, N_HEAD)), dma((5,)),
        ],
        compiler_params=pltpu.CompilerParams(
            collective_id=0, has_side_effects=True, vmem_limit_bytes=VMEM_LIMIT
        ),
        cost_estimate=pl.CostEstimate(flops=14_000_000_000, bytes_accessed=8_000_000, transcendentals=4_000_000),
    )(
        kept_heads, g_out.reshape(2, 2, TOK // 4, WIDE), w_out, x_act, b_proj, c_proj, log_decay,
    )
    return pl.pallas_call(
        hand_over,
        out_shape=outs,
        in_specs=[hbm] * 5,
        out_specs=[hbm] * 5,
        scratch_shapes=[*(buf(out.shape, out.dtype) for out in outs), dma((2, 5))],
        compiler_params=pltpu.CompilerParams(has_side_effects=True, vmem_limit_bytes=VMEM_LIMIT),
    )(*results)


def solution(mesh):
    in_specs = (
        P("ctx", "head"),
        P("ctx", "head"),
        P("ctx", "head"),
        P("ctx", None),
        P("ctx", None),
        P("head", "ctx"),
        P(),
    )
    out_specs = (
        P("ctx", "head"),
        P("ctx", None),
        P("ctx", None),
        P("head", "ctx"),
        P("ctx", "head"),
    )
    return jax.shard_map(
        per_device, mesh=mesh, in_specs=in_specs, out_specs=out_specs, check_vma=False
    )
```

```python
import math

import jax
import jax.numpy as jnp
from jax import lax
from jax.experimental import pallas as pl
from jax.experimental.pallas import tpu as pltpu
from jax.sharding import PartitionSpec as P

D = 8192
P_SIZE = 64
N = 128
KEPT = 64
Q = 128
TOK = 512
SPANS = TOK // Q
GROUP = 16
CAP = 12
COLS = CAP * P_SIZE
WIDE = GROUP * P_SIZE
PAIRS = CAP // 2
N_CTX = 16
N_HEAD = 8
HALF = COLS // 2
VMEM_LIMIT = 62 * 1024 * 1024

F32 = jnp.float32
BF = jnp.bfloat16
HIGH = lax.Precision.HIGHEST
MESH = pl.DeviceIdType.MESH
NN = (((1,), (0,)), ((), ()))
NT = (((1,), (1,)), ((), ()))
TN = (((0,), (0,)), ((), ()))


def dot(a, b, dims=NN, precision=None):
    return lax.dot_general(a, b, dims, precision=precision, preferred_element_type=F32)


def rcopy(src, dst, send_sem, recv_sem, device):
    return pltpu.make_async_remote_copy(
        src_ref=src,
        dst_ref=dst,
        send_sem=send_sem,
        recv_sem=recv_sem,
        device_id=device,
        device_id_type=MESH,
    )


def aligned(start, size, unit):
    return pl.ds(pl.multiple_of(start, unit), size)


def loop(lo, hi, body):
    def step(i, carry):
        body(i)
        return carry

    lax.fori_loop(lo, hi, step, 0)


class Gather:
    def __init__(self, block, half, send, recv, me, left, right, device):
        self.block, self.half, self.send, self.recv = block, half, send, recv
        self.me, self.left, self.right = me, left, right
        self.to_left, self.to_right = device(left), device(right)
        self.far = lax.rem(me + 2, 4)

    def copy(self, i):
        ref = (
            lambda: self.block(self.me),
            lambda: self.block(self.me),
            lambda: self.half(self.left, 0),
            lambda: self.half(self.right, 1),
        )[i]()
        return rcopy(ref, ref, self.send(i), self.recv(i), self.to_left if i % 2 else self.to_right)

    def landed(self, slot, ref):
        rcopy(ref, ref, self.send(slot), self.recv(slot), self.to_right).wait_recv()

    def start(self):
        self.copy(0).start()
        self.copy(1).start()

    def forward(self):
        self.landed(0, self.block(self.left))
        self.copy(2).start()
        self.landed(1, self.block(self.right))
        self.copy(3).start()

    def finish(self):
        self.landed(2, self.half(self.far, 0))
        self.landed(3, self.half(self.far, 1))

    def drain(self):
        for i in range(4):
            self.copy(i).wait_send()


class Scatter:
    def __init__(self, term, rows, far, right, left, via_l, via_r, from_l, from_r, own, send, recv, me, device):
        self.term, self.h = term, rows // 2
        self.far_buf, self.right_buf, self.left_buf = far, right, left
        self.via_l, self.via_r, self.from_l, self.from_r, self.own = via_l, via_r, from_l, from_r, own
        self.send, self.recv = send, recv
        self.me = me
        self.right, self.left, self.far = lax.rem(me + 1, 4), lax.rem(me + 3, 4), lax.rem(me + 2, 4)
        self.to_right, self.to_left = device(self.right), device(self.left)

    def copy(self, i):
        lo, hi = pl.ds(0, self.h), pl.ds(self.h, self.h)
        src, dst, to = (
            (self.far_buf.at[lo], self.via_l, self.to_right),
            (self.far_buf.at[hi], self.via_r, self.to_left),
            (self.right_buf.at[hi], self.from_l.at[hi], self.to_right),
            (self.left_buf.at[lo], self.from_r.at[lo], self.to_left),
            (self.right_buf.at[lo], self.from_l.at[lo], self.to_right),
            (self.left_buf.at[hi], self.from_r.at[hi], self.to_left),
        )[i]
        return rcopy(src, dst, self.send.at[i], self.recv.at[i], to)

    def first(self):
        h = self.h
        self.far_buf[...] = self.term(self.far).astype(BF)
        self.copy(0).start()
        self.copy(1).start()
        term = self.term(self.right)
        self.right_buf[h:] = term[h:].astype(BF)
        self.copy(2).start()
        self.own[:h] = term[:h]
        term = self.term(self.left)
        self.left_buf[:h] = term[:h].astype(BF)
        self.copy(3).start()
        self.own[h:] = term[h:]

    def second(self):
        h = self.h
        self.copy(0).wait_recv()
        self.right_buf[:h] = (self.own[:h] + self.via_l[...].astype(F32)).astype(BF)
        self.copy(4).start()
        self.copy(1).wait_recv()
        self.left_buf[h:] = (self.own[h:] + self.via_r[...].astype(F32)).astype(BF)
        self.copy(5).start()

    def last(self):
        self.own[...] = self.term(self.me)

    def finish(self):
        for i in (2, 3, 4, 5):
            self.copy(i).wait_recv()

    def result(self, rows, cols=slice(None)):
        return self.own[rows, cols] + self.from_l[rows, cols].astype(F32) + self.from_r[rows, cols].astype(F32)

    def drain(self):
        for i in range(6):
            self.copy(i).wait_send()


class Exchange:
    def __init__(self, source, landed, back, entering, sems, ci, hi):
        self.source, self.landed_ref, self.back, self.entering = source, landed, back, entering
        self.sems, self.ci, self.hi = sems, ci, hi

    def cut(self, r):
        return aligned(16 * (r // 2), 16, 16), aligned(HALF * lax.rem(r, 2), HALF, 128)

    def slot(self, r):
        return aligned(16 * r, 16, 16)

    def out_copy(self, k, at):
        to = lax.rem(self.ci + k, N_CTX)
        return rcopy(
            self.source.at[self.cut(to)], self.landed_ref.at[self.slot(at), :],
            self.sems.at[0, k], self.sems.at[1, k], (to, self.hi),
        )

    def back_copy(self, k, at):
        to = lax.rem(self.ci + k, N_CTX)
        return rcopy(
            self.back.at[self.slot(to), :], self.entering.at[self.cut(at)],
            self.sems.at[2, k], self.sems.at[3, k], (to, self.hi),
        )

    def start(self):
        loop(1, N_CTX, lambda k: self.out_copy(k, self.ci).start())
        self.landed_ref[self.slot(self.ci), :] = self.source[self.cut(self.ci)]

    def landed(self):
        loop(1, N_CTX, lambda k: self.out_copy(k, lax.rem(self.ci + N_CTX - k, N_CTX)).wait_recv())

    def scan(self, decays, order):
        state = jnp.zeros((16, HALF), F32)
        for i in order:
            rows = pl.ds(16 * i, 16)
            self.back[rows, :] = state.astype(BF)
            state = decays[pl.ds(8 * i, 1), :] * state + self.landed_ref[rows, :].astype(F32)

    def reply(self):
        loop(1, N_CTX, lambda k: self.back_copy(k, self.ci).start())
        self.entering[self.cut(self.ci)] = self.back[self.slot(self.ci), :]

    def replied(self):
        loop(1, N_CTX, lambda k: self.back_copy(k, lax.rem(self.ci + N_CTX - k, N_CTX)).wait_recv())

    def drain(self):
        def one(k):
            self.out_copy(k, self.ci).wait_send()
            self.back_copy(k, self.ci).wait_send()

        loop(1, N_CTX, one)


class HeadSum:
    def __init__(self, part, landed, total, whole, sems, ci, hi):
        self.part, self.landed_ref, self.total, self.whole = part, landed, total, whole
        self.sems, self.ci, self.hi = sems, ci, hi

    def share(self, r):
        return aligned(TOK // N_HEAD * r, TOK // N_HEAD, TOK // N_HEAD)

    def out_copy(self, k, at):
        to = lax.rem(self.hi + k, N_HEAD)
        return rcopy(
            self.part.at[self.share(to), :], self.landed_ref.at[at],
            self.sems.at[0, k], self.sems.at[1, k], (self.ci, to),
        )

    def back_copy(self, k, at):
        to = lax.rem(self.hi + k, N_HEAD)
        return rcopy(
            self.total, self.whole.at[self.share(at), :], self.sems.at[2, k], self.sems.at[3, k], (self.ci, to)
        )

    def start(self):
        loop(1, N_HEAD, lambda k: self.out_copy(k, self.hi).start())
        self.landed_ref[self.hi] = self.part[self.share(self.hi), :]

    def reduce(self):
        loop(1, N_HEAD, lambda k: self.out_copy(k, lax.rem(self.hi + N_HEAD - k, N_HEAD)).wait_recv())
        total = self.landed_ref[0].astype(F32)
        for i in range(1, N_HEAD):
            total = total + self.landed_ref[i].astype(F32)
        self.total[...] = total.astype(BF)
        loop(1, N_HEAD, lambda k: self.back_copy(k, self.hi).start())
        self.whole[self.share(self.hi), :] = self.total[...]

    def finish(self):
        loop(1, N_HEAD, lambda k: self.back_copy(k, lax.rem(self.hi + N_HEAD - k, N_HEAD)).wait_recv())

    def drain(self):
        def one(k):
            self.out_copy(k, self.hi).wait_send()
            self.back_copy(k, self.hi).wait_send()

        loop(1, N_HEAD, one)


def one_hot(rows, cols, hit):
    r = lax.broadcasted_iota(jnp.int32, (rows, cols), 0)
    k = lax.broadcasted_iota(jnp.int32, (rows, cols), 1)
    return jnp.where(hit(r, k), 1.0, 0.0).astype(F32)


def parts(a):
    high = a.astype(BF)
    rest = a - high.astype(F32)
    middle = rest.astype(BF)
    return jnp.concatenate([high, middle, (rest - middle.astype(F32)).astype(BF)], axis=0)


def kernel(
    kept, g, w_in, x_in, b_in, c_in, logd_in,
    out_ig, out_b, out_c, out_decay, out_w,
    w, x, b, c, logd, S, E16, E16B, G, W, YT, XS, XT, CUME, CUMR, PART, STIN, ADJ, YF, YI, L, MS, GK, GH, IG, IGB, B0,
    TOT, RD, DEC, ST, FL, FB, FE, AL, AB, AE, BP, BL, BT, BW, CP, CL, CT, CW, O_IG, O_B, O_C, O_D, O_W,
    a_far, a_right, a_left, a_vl, a_vr, a_fl, a_fr, a_own,
    b_far, b_right, b_left, b_vl, b_vr, b_fl, b_fr, b_own,
    w_far, w_right, w_left, w_vl, w_vr, w_fl, w_fr, w_own,
    loc_sem, own_sem, a2a_sem, xs_sem, xr_sem, sib_sem, wag_sem, yag_sem, hrs_sem, wrs_sem, dec_sem, fex_sem, bex_sem,
    b_sem, c_sem, out_sem,
):
    ci, hi = lax.axis_index("ctx"), lax.axis_index("head")
    z, y = ci // 4, lax.rem(ci, 4)
    xx, cc = hi // 2, lax.rem(hi, 2)
    half = y // 2
    cross = lax.rem(half + cc, 2)
    at_x = lambda p: (ci, 2 * p + cc)
    at_y = lambda p: (4 * z + p, hi)
    at_z = lambda p: (4 * p + y, hi)
    sibling = (ci, 2 * xx + 1 - cc)
    nxt = lambda p: lax.rem(p + 1, 4)
    prv = lambda p: lax.rem(p + 3, 4)

    barrier = pltpu.get_barrier_semaphore()

    def greet(device):
        pl.semaphore_signal(barrier, inc=1, device_id=device, device_id_type=MESH)

    loop(1, N_CTX, lambda k: greet((lax.rem(ci + k, N_CTX), hi)))
    loop(1, N_HEAD, lambda k: greet((ci, lax.rem(hi + k, N_HEAD))))

    @pl.when(cross == 1)
    def _():
        for p in range(2):
            greet((4 * z + 2 * cc + p, 2 * xx + 1 - cc))

    loads = [
        pltpu.make_async_copy(src, dst, loc_sem.at[i])
        for i, (src, dst) in enumerate(((w_in, w), (x_in, x), (b_in, b), (c_in, c), (logd_in, logd)))
    ]
    for load in loads:
        load.start()

    lanes = lax.broadcasted_iota(jnp.int32, (8, COLS), 1)

    def place(k, carry):
        headof, rank = carry
        local = kept[k] - GROUP * hi
        mine = (local >= 0) & (local < GROUP)
        headof = jnp.where(lanes // P_SIZE == jnp.where(mine, rank, -1), local, headof)
        return headof, rank + jnp.where(mine, 1, 0)

    headof, _ = lax.fori_loop(0, KEPT, place, (jnp.full((8, COLS), -1, jnp.int32), jnp.int32(0)))
    headof = headof[0:1, :]
    colidx = jnp.where(headof >= 0, P_SIZE * headof + lax.rem(lanes[0:1, :], P_SIZE), -1)

    def build(i):
        rows = lax.broadcasted_iota(jnp.int32, (128, COLS), 0) + 128 * i
        S[aligned(128 * i, 128, 128), :] = jnp.where(rows == colidx, 1.0, 0.0).astype(BF)

    loop(0, WIDE // 128, build)
    E16[...] = jnp.where(lax.broadcasted_iota(jnp.int32, (GROUP, COLS), 0) == headof, 1.0, 0.0).astype(F32)
    for i in range(3):
        E16B[pl.ds(GROUP * i, GROUP), :] = E16[...].astype(BF)

    for load in loads:
        load.wait()

    upto = one_hot(Q, Q, lambda r, k: r <= k)
    pick = one_hot(COLS, 128, lambda r, k: r == P_SIZE * k)
    slots = dot(E16[...], pick)[:, :GROUP].astype(BF)
    slots3 = jnp.concatenate([slots] * 3, axis=0)
    upto_low = upto.astype(BF)

    def decays(s):
        rows = aligned(Q * s, Q, Q)
        sums = dot(parts(logd[:, rows]), upto_low)
        cum = parts(sums[:GROUP] + sums[GROUP : 2 * GROUP] + sums[2 * GROUP :])
        CUMR[:, rows] = dot(slots3, cum, TN)
        CUME[rows, :] = dot(cum, E16B[...], TN)

    loop(0, SPANS, decays)
    totals = sum(CUMR[:, pl.ds(Q * s + Q - 1, 1)] for s in range(SPANS))
    TOT[...] = dot(jnp.broadcast_to(totals, (GROUP, 8)), one_hot(GROUP, 128, lambda r, k: r == k), TN, precision=HIGH)

    STIN[0] = jnp.zeros((N, COLS), F32)

    def local_states(s):
        rows = aligned(Q * s, Q, Q)
        cume = CUME[rows, :]
        total = cume[Q - 1 : Q, :]
        xs = dot(x[rows, :], S[...])
        XS[rows, :] = xs.astype(BF)
        xt = (jnp.exp(total - cume) * xs).astype(BF)
        XT[rows, :] = xt
        part = dot(b[rows, :], xt, TN)
        PART[s] = part
        STIN[0] = jnp.exp(total) * STIN[0] + part

    loop(0, SPANS, local_states)
    ST[0] = STIN[0].astype(BF)

    pl.semaphore_wait(barrier, N_CTX - 1 + N_HEAD - 1 + 2 * cross)

    def decay_copy(k, at):
        to = lax.rem(ci + k, N_CTX)
        return rcopy(TOT, RD.at[aligned(8 * at, 8, 8), :], dec_sem.at[0, k], dec_sem.at[1, k], (to, hi))

    loop(1, N_CTX, lambda k: decay_copy(k, ci).start())
    RD[aligned(8 * ci, 8, 8), :] = TOT[...]

    forward = Exchange(ST.at[0], FL, FB, FE, fex_sem, ci, hi)
    forward.start()


    def g_tile(token, feature, q):
        return G.at[token, :, q, :, aligned(TOK * feature, TOK, TOK)]

    def quarter(q, p):
        return g.at[:, q, :, pl.ds(TOK * p, TOK)]

    def a2a_copy(q, p, slot):
        return rcopy(
            quarter(q, p), g_tile(y, xx, q), a2a_sem.at[0, q, p], a2a_sem.at[1, q, slot], (4 * z + 2 * cc + p, 2 * xx + half)
        )

    def a2a_start(q):
        for p in range(2):

            @pl.when(2 * cc + p != y)
            def _():
                a2a_copy(q, p, lax.rem(y, 2)).start()

    def x_gather(q, t):
        token = 2 * cc + t
        return Gather(
            lambda p: g_tile(token, p, q),
            lambda p, h: G.at[token, h, q, :, aligned(TOK * p, TOK, TOK)],
            lambda i: xs_sem.at[q, t, i],
            lambda i: xr_sem.at[q, t, i],
            xx, prv(xx), nxt(xx), at_x,
        )

    x_gathers = [[x_gather(q, t) for t in range(2)] for q in range(2)]
    ring_x = (xx, prv(xx), nxt(xx), lax.rem(xx + 2, 4))

    def sibling_copy(q, t, j, core):
        tile = g_tile(2 * core + t, ring_x[j], q)
        return rcopy(tile, tile, sib_sem.at[0, q, t, j], sib_sem.at[1, q, t, j], sibling)

    def x_launch(q, t):
        x_gathers[q][t].start()
        sibling_copy(q, t, 0, cc).start()

    def own_copy(q, p):
        return pltpu.make_async_copy(quarter(q, p), g_tile(y, xx, q), own_sem.at[q])

    def x_own():
        for p in range(2):

            @pl.when(2 * cc + p == y)
            def _():
                for q in range(2):
                    own_copy(q, p).start()
                for q in range(2):
                    own_copy(q, p).wait()
                    x_launch(q, p)

    def x_rest(q):
        for t in range(2):

            @pl.when(2 * cc + t != y)
            def _():
                rcopy(
                    quarter(q, t), g_tile(2 * cc + t, xx, q), a2a_sem.at[0, q, t], a2a_sem.at[1, q, t], sibling
                ).wait_recv()
                x_launch(q, t)

    def x_forward(q):
        for t in range(2):
            x_gathers[q][t].forward()
            sibling_copy(q, t, 1, cc).start()
            sibling_copy(q, t, 2, cc).start()

    def x_finish(q):
        for t in range(2):
            x_gathers[q][t].finish()
            sibling_copy(q, t, 3, cc).start()
        for t in range(2):
            for j in range(4):
                sibling_copy(q, t, j, 1 - cc).wait_recv()

    x_own()

    def pick_w(i):
        W[aligned(TOK * z + 128 * i, 128, 128), :] = dot(w[aligned(128 * i, 128, 128), :], S[...]).astype(BF)

    loop(0, TOK // 128, pick_w)
    sub = lax.broadcasted_iota(jnp.int32, (Q, Q), 0)
    lane = lax.broadcasted_iota(jnp.int32, (Q, Q), 1)
    left_half = lane < P_SIZE
    causal = lane <= sub

    def inside(s):
        rows = aligned(Q * s, Q, Q)
        cb = dot(c[rows, :], b[rows, :], NT)
        for k in range(PAIRS):
            cols = pl.ds(Q * k, Q)
            for h in range(2):
                head = 2 * k + h
                differ = CUME[rows, pl.ds(P_SIZE * head, 1)] - CUMR[pl.ds(head, 1), rows]
                low = jnp.where(causal, jnp.exp(jnp.where(causal, differ, 0.0)), 0.0)
                L[PAIRS * s + k, pl.ds(Q * h, Q), :] = low
                MS[PAIRS * s + k, pl.ds(Q * h, Q), :] = (low * cb).astype(BF)
            both = dot(MS[PAIRS * s + k], XS[rows, cols])
            YF[rows, cols] = jnp.where(left_half, both[:Q], both[Q:])

    loop(0, SPANS, inside)

    loop(1, N_CTX, lambda k: decay_copy(k, lax.rem(ci + N_CTX - k, N_CTX)).wait_recv())
    first_slot = CAP // 2 * lax.rem(ci, 2)
    DEC[...] = jnp.exp(dot(RD[...], one_hot(128, HALF, lambda r, k: r == k // P_SIZE + first_slot), precision=HIGH))
    forward.landed()
    forward.scan(DEC, range(N_CTX))
    forward.reply()
    a2a_start(0)
    w_gather = Gather(
        lambda p: W.at[aligned(TOK * p, TOK, TOK), :],
        lambda p, h: W.at[aligned(TOK * p + TOK // 2 * h, TOK // 2, TOK // 2), :],
        lambda i: wag_sem.at[0, i],
        lambda i: wag_sem.at[1, i],
        z, prv(z), nxt(z), at_z,
    )
    w_gather.start()
    forward.replied()
    STIN[0] = FE[...].astype(F32)

    def outputs(s):
        rows = aligned(Q * s, Q, Q)
        cume = CUME[rows, :]
        state_in = STIN[s]
        inter = jnp.exp(cume) * dot(c[rows, :], state_in.astype(BF))
        YI[rows, :] = inter
        whole = YF[rows, :] + inter
        YF[rows, :] = whole
        YT[:, aligned(TOK * y + Q * s, Q, Q)] = whole.T.astype(BF)
        STIN[s + 1] = jnp.exp(cume[Q - 1 : Q, :]) * state_in + PART[s]

    loop(0, SPANS, outputs)
    y_gather = Gather(
        lambda p: YT.at[:, aligned(TOK * p, TOK, TOK)],
        lambda p, h: YT.at[pl.ds(HALF * h, HALF), aligned(TOK * p, TOK, TOK)],
        lambda i: yag_sem.at[0, i],
        lambda i: yag_sem.at[1, i],
        y, prv(y), nxt(y), at_y,
    )
    y_gather.start()

    def head_term(q):
        return lambda block: dot(G[block, :, q].reshape(TOK // 2, 4 * TOK), W[...])

    def weight_term(block):
        return dot(YT[...], G[:, :, :, :, aligned(TOK * block, TOK, TOK)].reshape(4 * TOK, TOK))

    heads = (
        Scatter(
            head_term(0), TOK // 2, a_far, a_right, a_left, a_vl, a_vr, a_fl, a_fr, a_own,
            hrs_sem.at[0, 0], hrs_sem.at[0, 1], y, at_y,
        ),
        Scatter(
            head_term(1), TOK // 2, b_far, b_right, b_left, b_vl, b_vr, b_fl, b_fr, b_own,
            hrs_sem.at[1, 0], hrs_sem.at[1, 1], y, at_y,
        ),
    )
    weights = Scatter(
        weight_term, COLS, w_far, w_right, w_left, w_vl, w_vr, w_fl, w_fr, w_own,
        wrs_sem.at[0], wrs_sem.at[1], z, at_z,
    )

    def local_adjoint(s):
        rows = pl.ds(Q * s, Q)
        GK[rows, :] = heads[s % 2].result(pl.ds(Q * (s // 2), Q)).astype(BF)
        gh = (jnp.exp(CUME[rows, :]) * GK[rows, :].astype(F32)).astype(BF)
        GH[rows, :] = gh
        PART[s] = dot(c[rows, :], gh, TN)

    def inside_grad(s):
        rows = aligned(Q * s, Q, Q)
        total = jnp.zeros((Q, Q), F32)
        for k in range(PAIRS):
            cols = pl.ds(Q * k, Q)
            gk = GK[rows, cols].astype(F32)
            stack = jnp.concatenate(
                [jnp.where(left_half, gk, 0.0), jnp.where(left_half, 0.0, gk)], axis=0
            ).astype(BF)
            weighted = L[PAIRS * s + k] * dot(stack, XS[rows, cols], NT)
            total = total + weighted[:Q] + weighted[Q:]
            IG[rows, cols] = dot(MS[PAIRS * s + k], stack, TN)
        sg = total.astype(BF)
        B0[rows, :] = dot(sg, c[rows, :], TN)
        CP[rows, :] = (dot(sg, b[rows, :]) + dot(GH[rows, :], STIN[s].astype(BF), NT)).astype(BF)

    x_rest(0)
    a2a_start(1)
    w_gather.forward()
    x_forward(0)
    x_rest(1)
    y_gather.forward()
    w_gather.finish()
    x_finish(0)
    heads[0].first()
    x_forward(1)
    x_finish(1)
    heads[0].second()
    y_gather.finish()
    weights.first()
    heads[1].first()
    heads[0].last()
    heads[0].finish()
    local_adjoint(0)
    local_adjoint(2)
    heads[1].second()
    heads[1].last()
    inside_grad(0)
    inside_grad(2)
    heads[1].finish()
    local_adjoint(1)
    local_adjoint(3)

    ADJ[0] = PART[SPANS - 1]
    for s in reversed(range(SPANS - 1)):
        ADJ[0] = jnp.exp(CUME[pl.ds(Q * s + Q - 1, 1), :]) * ADJ[0] + PART[s]
    ST[1] = ADJ[0].astype(BF)
    backward = Exchange(ST.at[1], AL, AB, AE, bex_sem, ci, hi)
    backward.start()
    inside_grad(1)
    inside_grad(3)
    c_sum = HeadSum(CP, CL, CT, CW, c_sem, ci, hi)
    c_sum.start()
    backward.landed()
    backward.scan(DEC, reversed(range(N_CTX)))
    backward.reply()
    weights.second()
    weights.last()
    c_sum.reduce()
    backward.replied()
    ADJ[SPANS] = AE[...].astype(F32)
    for s in reversed(range(SPANS)):
        rows = pl.ds(Q * s, Q)
        BP[rows, :] = (B0[rows, :] + dot(XT[rows, :], ADJ[s + 1].astype(BF), NT)).astype(BF)
        if s > 0:
            ADJ[s] = jnp.exp(CUME[pl.ds(Q * s + Q - 1, 1), :]) * ADJ[s + 1] + PART[s]
    b_sum = HeadSum(BP, BL, BT, BW, b_sem, ci, hi)
    b_sum.start()

    def closing(s):
        rows = aligned(Q * s, Q, Q)
        cume = CUME[rows, :]
        total = cume[Q - 1 : Q, :]
        adjoint = ADJ[s + 1]
        in_grad = IG[rows, :] + jnp.exp(total - cume) * dot(b[rows, :], adjoint.astype(BF))
        IGB[rows, :] = in_grad.astype(BF)
        gk = GK[rows, :].astype(F32)
        step = XS[rows, :].astype(F32) * in_grad - gk * YF[rows, :]
        start = jnp.sum(gk * YI[rows, :], axis=0, keepdims=True) + jnp.exp(total) * jnp.sum(
            adjoint * STIN[s], axis=0, keepdims=True
        )
        row = lax.broadcasted_iota(jnp.int32, (Q, COLS), 0)
        step = jnp.where(row == 0, start, pltpu.roll(step, 1, 0))
        high = step.astype(BF)
        rest = (step - high.astype(F32)).astype(BF)
        steps = dot(E16B[:GROUP], high, NT) + dot(E16B[:GROUP], rest, NT)
        O_D[:, rows] = dot(steps, upto, precision=HIGH) * (1.0 / math.sqrt(P_SIZE * D))

    def spread_in(i):
        rows = aligned(128 * i, 128, 128)
        O_IG[rows, :] = dot(IGB[rows, :], S[...], NT).astype(BF)

    def spread_w(i):
        cols = aligned(128 * i, 128, 128)
        block = (weights.result(slice(None), cols) * (1.0 / math.sqrt(D))).astype(BF)
        O_W[cols, :] = dot(block, S[...], (((0,), (1,)), ((), ()))).astype(BF)

    stores = [
        pltpu.make_async_copy(src, dst, out_sem.at[i])
        for i, (src, dst) in enumerate(((O_IG, out_ig), (O_B, out_b), (O_C, out_c), (O_D, out_decay), (O_W, out_w)))
    ]
    loop(0, SPANS, closing)
    stores[3].start()
    b_sum.reduce()
    loop(0, TOK // 128, spread_in)
    stores[0].start()
    weights.finish()
    loop(0, TOK // 128, spread_w)
    stores[4].start()
    c_sum.finish()
    O_C[...] = CW[...].astype(F32) * math.sqrt(N / (KEPT * P_SIZE * D))
    stores[2].start()
    b_sum.finish()
    O_B[...] = BW[...].astype(F32) / math.sqrt(KEPT * P_SIZE)
    stores[1].start()

    for q in range(2):
        for p in range(2):

            @pl.when(2 * cc + p != y)
            def _():
                a2a_copy(q, p, 0).wait_send()

        for t in range(2):
            x_gathers[q][t].drain()
            for j in range(4):
                sibling_copy(q, t, j, cc).wait_send()
        heads[q].drain()
    w_gather.drain()
    y_gather.drain()
    weights.drain()
    loop(1, N_CTX, lambda k: decay_copy(k, ci).wait_send())
    forward.drain()
    backward.drain()
    c_sum.drain()
    b_sum.drain()
    for store in stores:
        store.wait()


def hand_over(*refs):
    count = len(refs) // 3
    ins, outs, held, sems = refs[:count], refs[count : 2 * count], refs[2 * count : -1], refs[-1]
    reads = [pltpu.make_async_copy(ins[i], held[i], sems.at[0, i]) for i in range(count)]
    writes = [pltpu.make_async_copy(held[i], outs[i], sems.at[1, i]) for i in range(count)]
    for read in reads:
        read.start()
    for read, write in zip(reads, writes):
        read.wait()
        write.start()
    for write in writes:
        write.wait()


def per_device(g_out, w_out, x_act, b_proj, c_proj, log_decay, kept_heads):
    hbm = pl.BlockSpec(memory_space=pl.ANY)
    buf = pltpu.VMEM
    dma = pltpu.SemaphoreType.DMA

    def ring(rows, cols):
        h = rows // 2
        return [
            buf((rows, cols), BF), buf((rows, cols), BF), buf((rows, cols), BF), buf((h, cols), BF), buf((h, cols), BF),
            buf((rows, cols), BF), buf((rows, cols), BF), buf((rows, cols), F32),
        ]

    def head_sum():
        return [
            buf((TOK, N), BF), buf((N_HEAD, TOK // N_HEAD, N), BF), buf((TOK // N_HEAD, N), BF), buf((TOK, N), BF)
        ]

    outs = (
        jax.ShapeDtypeStruct((TOK, WIDE), BF),
        jax.ShapeDtypeStruct((TOK, N), F32),
        jax.ShapeDtypeStruct((TOK, N), F32),
        jax.ShapeDtypeStruct((GROUP, TOK), F32),
        jax.ShapeDtypeStruct((TOK, WIDE), BF),
    )
    results = pl.pallas_call(
        kernel,
        out_shape=outs,
        in_specs=[pl.BlockSpec(memory_space=pltpu.SMEM)] + [hbm] * 6,
        out_specs=[hbm] * 5,
        scratch_shapes=[
            buf((TOK, WIDE), BF), buf((TOK, WIDE), BF), buf((TOK, N), BF), buf((TOK, N), BF), buf((GROUP, TOK), F32),
            buf((WIDE, COLS), BF), buf((GROUP, COLS), F32), buf((3 * GROUP, COLS), BF),
            buf((4, 2, 2, TOK // 4, 4 * TOK), BF), buf((4 * TOK, COLS), BF), buf((COLS, 4 * TOK), BF),
            buf((TOK, COLS), BF), buf((TOK, COLS), BF), buf((TOK, COLS), F32), buf((GROUP, TOK), F32),
            buf((SPANS, N, COLS), F32), buf((SPANS + 1, N, COLS), F32), buf((SPANS + 1, N, COLS), F32),
            buf((TOK, COLS), F32), buf((TOK, COLS), F32),
            buf((SPANS * PAIRS, 2 * Q, Q), F32), buf((SPANS * PAIRS, 2 * Q, Q), BF),
            buf((TOK, COLS), BF), buf((TOK, COLS), BF), buf((TOK, COLS), F32), buf((TOK, COLS), BF),
            buf((TOK, N), F32),
            buf((8, 128), F32), buf((8 * N_CTX, 128), F32), buf((8 * N_CTX, HALF), F32), buf((2, N, COLS), BF),
            buf((16 * N_CTX, HALF), BF), buf((16 * N_CTX, HALF), BF), buf((N, COLS), BF),
            buf((16 * N_CTX, HALF), BF), buf((16 * N_CTX, HALF), BF), buf((N, COLS), BF),
            *head_sum(), *head_sum(),
            buf((TOK, WIDE), BF), buf((TOK, N), F32), buf((TOK, N), F32), buf((GROUP, TOK), F32), buf((TOK, WIDE), BF),
            *ring(TOK // 2, COLS), *ring(TOK // 2, COLS), *ring(COLS, TOK),
            dma((5,)), dma((2,)), dma((2, 2, 2)), dma((2, 2, 4)), dma((2, 2, 4)), dma((2, 2, 2, 4)), dma((2, 4)),
            dma((2, 4)), dma((2, 2, 6)), dma((2, 6)), dma((2, N_CTX)), dma((4, N_CTX)), dma((4, N_CTX)),
            dma((4, N_HEAD)), dma((4, N_HEAD)), dma((5,)),
        ],
        compiler_params=pltpu.CompilerParams(
            collective_id=0, has_side_effects=True, vmem_limit_bytes=VMEM_LIMIT
        ),
        cost_estimate=pl.CostEstimate(flops=14_000_000_000, bytes_accessed=8_000_000, transcendentals=4_000_000),
    )(
        kept_heads, g_out.reshape(2, 2, TOK // 4, WIDE), w_out, x_act, b_proj, c_proj, log_decay,
    )
    return pl.pallas_call(
        hand_over,
        out_shape=outs,
        in_specs=[hbm] * 5,
        out_specs=[hbm] * 5,
        scratch_shapes=[*(buf(out.shape, out.dtype) for out in outs), dma((2, 5))],
        compiler_params=pltpu.CompilerParams(has_side_effects=True, vmem_limit_bytes=VMEM_LIMIT),
    )(*results)


def solution(mesh):
    in_specs = (
        P("ctx", "head"),
        P("ctx", "head"),
        P("ctx", "head"),
        P("ctx", None),
        P("ctx", None),
        P("head", "ctx"),
        P(),
    )
    out_specs = (
        P("ctx", "head"),
        P("ctx", None),
        P("ctx", None),
        P("head", "ctx"),
        P("ctx", "head"),
    )
    return jax.shard_map(
        per_device, mesh=mesh, in_specs=in_specs, out_specs=out_specs, check_vma=False
    )
```

```python
import math

import jax
import jax.numpy as jnp
from jax import lax
from jax.experimental import pallas as pl
from jax.experimental.pallas import tpu as pltpu
from jax.sharding import PartitionSpec as P

D = 8192
P_SIZE = 64
N = 128
KEPT = 64
Q = 128
TOK = 512
SPANS = TOK // Q
GROUP = 16
CAP = 12
COLS = CAP * P_SIZE
WIDE = GROUP * P_SIZE
PAIRS = CAP // 2
N_CTX = 16
N_HEAD = 8
HALF = COLS // 2
VMEM_LIMIT = 62 * 1024 * 1024

F32 = jnp.float32
BF = jnp.bfloat16
HIGH = lax.Precision.HIGHEST
MESH = pl.DeviceIdType.MESH
NN = (((1,), (0,)), ((), ()))
NT = (((1,), (1,)), ((), ()))
TN = (((0,), (0,)), ((), ()))


def dot(a, b, dims=NN, precision=None):
    return lax.dot_general(a, b, dims, precision=precision, preferred_element_type=F32)


def rcopy(src, dst, send_sem, recv_sem, device):
    return pltpu.make_async_remote_copy(
        src_ref=src,
        dst_ref=dst,
        send_sem=send_sem,
        recv_sem=recv_sem,
        device_id=device,
        device_id_type=MESH,
    )


def aligned(start, size, unit):
    return pl.ds(pl.multiple_of(start, unit), size)


def loop(lo, hi, body):
    def step(i, carry):
        body(i)
        return carry

    lax.fori_loop(lo, hi, step, 0)


class Gather:
    def __init__(self, block, half, send, recv, me, left, right, device):
        self.block, self.half, self.send, self.recv = block, half, send, recv
        self.me, self.left, self.right = me, left, right
        self.to_left, self.to_right = device(left), device(right)
        self.far = lax.rem(me + 2, 4)

    def copy(self, i):
        ref = (
            lambda: self.block(self.me),
            lambda: self.block(self.me),
            lambda: self.half(self.left, 0),
            lambda: self.half(self.right, 1),
        )[i]()
        return rcopy(ref, ref, self.send(i), self.recv(i), self.to_left if i % 2 else self.to_right)

    def landed(self, slot, ref):
        rcopy(ref, ref, self.send(slot), self.recv(slot), self.to_right).wait_recv()

    def start(self):
        self.copy(0).start()
        self.copy(1).start()

    def forward(self):
        self.landed(0, self.block(self.left))
        self.copy(2).start()
        self.landed(1, self.block(self.right))
        self.copy(3).start()

    def finish(self):
        self.landed(2, self.half(self.far, 0))
        self.landed(3, self.half(self.far, 1))

    def drain(self):
        for i in range(4):
            self.copy(i).wait_send()


class Scatter:
    def __init__(self, term, rows, far, right, left, via_l, via_r, from_l, from_r, own, send, recv, me, device):
        self.term, self.h = term, rows // 2
        self.far_buf, self.right_buf, self.left_buf = far, right, left
        self.via_l, self.via_r, self.from_l, self.from_r, self.own = via_l, via_r, from_l, from_r, own
        self.send, self.recv = send, recv
        self.me = me
        self.right, self.left, self.far = lax.rem(me + 1, 4), lax.rem(me + 3, 4), lax.rem(me + 2, 4)
        self.to_right, self.to_left = device(self.right), device(self.left)

    def copy(self, i):
        lo, hi = pl.ds(0, self.h), pl.ds(self.h, self.h)
        src, dst, to = (
            (self.far_buf.at[lo], self.via_l, self.to_right),
            (self.far_buf.at[hi], self.via_r, self.to_left),
            (self.right_buf.at[hi], self.from_l.at[hi], self.to_right),
            (self.left_buf.at[lo], self.from_r.at[lo], self.to_left),
            (self.right_buf.at[lo], self.from_l.at[lo], self.to_right),
            (self.left_buf.at[hi], self.from_r.at[hi], self.to_left),
        )[i]
        return rcopy(src, dst, self.send.at[i], self.recv.at[i], to)

    def first(self):
        h = self.h
        self.far_buf[...] = self.term(self.far).astype(BF)
        self.copy(0).start()
        self.copy(1).start()
        term = self.term(self.right)
        self.right_buf[h:] = term[h:].astype(BF)
        self.copy(2).start()
        self.own[:h] = term[:h]
        term = self.term(self.left)
        self.left_buf[:h] = term[:h].astype(BF)
        self.copy(3).start()
        self.own[h:] = term[h:]

    def second(self):
        h = self.h
        self.copy(0).wait_recv()
        self.right_buf[:h] = (self.own[:h] + self.via_l[...].astype(F32)).astype(BF)
        self.copy(4).start()
        self.copy(1).wait_recv()
        self.left_buf[h:] = (self.own[h:] + self.via_r[...].astype(F32)).astype(BF)
        self.copy(5).start()

    def last(self):
        self.own[...] = self.term(self.me)

    def finish(self):
        for i in (2, 3, 4, 5):
            self.copy(i).wait_recv()

    def result(self, rows, cols=slice(None)):
        return self.own[rows, cols] + self.from_l[rows, cols].astype(F32) + self.from_r[rows, cols].astype(F32)

    def drain(self):
        for i in range(6):
            self.copy(i).wait_send()


class Exchange:
    def __init__(self, source, landed, back, entering, sems, ci, hi):
        self.source, self.landed_ref, self.back, self.entering = source, landed, back, entering
        self.sems, self.ci, self.hi = sems, ci, hi

    def cut(self, r):
        return aligned(16 * (r // 2), 16, 16), aligned(HALF * lax.rem(r, 2), HALF, 128)

    def slot(self, r):
        return aligned(16 * r, 16, 16)

    def out_copy(self, k, at):
        to = lax.rem(self.ci + k, N_CTX)
        return rcopy(
            self.source.at[self.cut(to)], self.landed_ref.at[self.slot(at), :],
            self.sems.at[0, k], self.sems.at[1, k], (to, self.hi),
        )

    def back_copy(self, k, at):
        to = lax.rem(self.ci + k, N_CTX)
        return rcopy(
            self.back.at[self.slot(to), :], self.entering.at[self.cut(at)],
            self.sems.at[2, k], self.sems.at[3, k], (to, self.hi),
        )

    def start(self):
        loop(1, N_CTX, lambda k: self.out_copy(k, self.ci).start())
        self.landed_ref[self.slot(self.ci), :] = self.source[self.cut(self.ci)]

    def landed(self):
        loop(1, N_CTX, lambda k: self.out_copy(k, lax.rem(self.ci + N_CTX - k, N_CTX)).wait_recv())

    def scan(self, decays, order):
        state = jnp.zeros((16, HALF), F32)
        for i in order:
            rows = pl.ds(16 * i, 16)
            self.back[rows, :] = state.astype(BF)
            state = decays[pl.ds(8 * i, 1), :] * state + self.landed_ref[rows, :].astype(F32)

    def reply(self):
        loop(1, N_CTX, lambda k: self.back_copy(k, self.ci).start())
        self.entering[self.cut(self.ci)] = self.back[self.slot(self.ci), :]

    def replied(self):
        loop(1, N_CTX, lambda k: self.back_copy(k, lax.rem(self.ci + N_CTX - k, N_CTX)).wait_recv())

    def drain(self):
        def one(k):
            self.out_copy(k, self.ci).wait_send()
            self.back_copy(k, self.ci).wait_send()

        loop(1, N_CTX, one)


class HeadSum:
    def __init__(self, part, landed, total, whole, sems, own_sem, ci, hi):
        self.part, self.landed_ref, self.total, self.whole = part, landed, total, whole
        self.sems, self.own_sem, self.ci, self.hi = sems, own_sem, ci, hi

    def own_copy(self):
        return pltpu.make_async_copy(self.total, self.whole.at[self.share(self.hi), :], self.own_sem)

    def share(self, r):
        return aligned(TOK // N_HEAD * r, TOK // N_HEAD, TOK // N_HEAD)

    def out_copy(self, k, at):
        to = lax.rem(self.hi + k, N_HEAD)
        return rcopy(
            self.part.at[self.share(to), :], self.landed_ref.at[at],
            self.sems.at[0, k], self.sems.at[1, k], (self.ci, to),
        )

    def back_copy(self, k, at):
        to = lax.rem(self.hi + k, N_HEAD)
        return rcopy(
            self.total, self.whole.at[self.share(at), :], self.sems.at[2, k], self.sems.at[3, k], (self.ci, to)
        )

    def start(self):
        loop(1, N_HEAD, lambda k: self.out_copy(k, self.hi).start())
        self.landed_ref[self.hi] = self.part[self.share(self.hi), :]

    def reduce(self):
        loop(1, N_HEAD, lambda k: self.out_copy(k, lax.rem(self.hi + N_HEAD - k, N_HEAD)).wait_recv())
        total = self.landed_ref[0].astype(F32)
        for i in range(1, N_HEAD):
            total = total + self.landed_ref[i].astype(F32)
        self.total[...] = total.astype(BF)
        loop(1, N_HEAD, lambda k: self.back_copy(k, self.hi).start())
        self.own_copy().start()

    def finish(self):
        loop(1, N_HEAD, lambda k: self.back_copy(k, lax.rem(self.hi + N_HEAD - k, N_HEAD)).wait_recv())
        self.own_copy().wait()

    def drain(self):
        def one(k):
            self.out_copy(k, self.hi).wait_send()
            self.back_copy(k, self.hi).wait_send()

        loop(1, N_HEAD, one)


def one_hot(rows, cols, hit):
    r = lax.broadcasted_iota(jnp.int32, (rows, cols), 0)
    k = lax.broadcasted_iota(jnp.int32, (rows, cols), 1)
    return jnp.where(hit(r, k), 1.0, 0.0).astype(F32)


def parts(a):
    high = a.astype(BF)
    rest = a - high.astype(F32)
    middle = rest.astype(BF)
    return jnp.concatenate([high, middle, (rest - middle.astype(F32)).astype(BF)], axis=0)


def kernel(
    kept, g, w_in, x_in, b_in, c_in, logd_in,
    out_ig, out_b, out_c, out_decay, out_w,
    w, x, b, c, logd, S, S_T, E16, E16B, G, W, YT, XS, XT, CUME, CUMR, PART, STIN, ADJ, YF, YI, L, MS, GK, GH, IG, IGB, B0,
    AFTER, TOT, RD, DEC, ST, FL, FB, FE, AL, AB, AE, BP, BL, BT, CP, CL, CT, O_IG, O_D, O_W,
    a_far, a_right, a_left, a_vl, a_vr, a_fl, a_fr, a_own,
    b_far, b_right, b_left, b_vl, b_vr, b_fl, b_fr, b_own,
    w_far, w_right, w_left, w_vl, w_vr, w_fl, w_fr, w_own,
    loc_sem, own_sem, a2a_sem, xs_sem, xr_sem, sib_sem, wag_sem, yag_sem, hrs_sem, wrs_sem, dec_sem, fex_sem, bex_sem,
    b_sem, c_sem, out_sem,
):
    ci, hi = lax.axis_index("ctx"), lax.axis_index("head")
    z, y = ci // 4, lax.rem(ci, 4)
    xx, cc = hi // 2, lax.rem(hi, 2)
    half = y // 2
    cross = lax.rem(half + cc, 2)
    at_x = lambda p: (ci, 2 * p + cc)
    at_y = lambda p: (4 * z + p, hi)
    at_z = lambda p: (4 * p + y, hi)
    sibling = (ci, 2 * xx + 1 - cc)
    nxt = lambda p: lax.rem(p + 1, 4)
    prv = lambda p: lax.rem(p + 3, 4)

    barrier = pltpu.get_barrier_semaphore()

    def greet(device):
        pl.semaphore_signal(barrier, inc=1, device_id=device, device_id_type=MESH)

    loop(1, N_CTX, lambda k: greet((lax.rem(ci + k, N_CTX), hi)))
    loop(1, N_HEAD, lambda k: greet((ci, lax.rem(hi + k, N_HEAD))))

    @pl.when(cross == 1)
    def _():
        for p in range(2):
            greet((4 * z + 2 * cc + p, 2 * xx + 1 - cc))

    loads = [
        pltpu.make_async_copy(src, dst, loc_sem.at[i])
        for i, (src, dst) in enumerate(((w_in, w), (x_in, x), (b_in, b), (c_in, c), (logd_in, logd)))
    ]
    for load in loads:
        load.start()

    lanes = lax.broadcasted_iota(jnp.int32, (8, COLS), 1)

    def place(k, carry):
        headof, rank = carry
        local = kept[k] - GROUP * hi
        mine = (local >= 0) & (local < GROUP)
        headof = jnp.where(lanes // P_SIZE == jnp.where(mine, rank, -1), local, headof)
        return headof, rank + jnp.where(mine, 1, 0)

    headof, _ = lax.fori_loop(0, KEPT, place, (jnp.full((8, COLS), -1, jnp.int32), jnp.int32(0)))
    headof = headof[0:1, :]
    colidx = jnp.where(headof >= 0, P_SIZE * headof + lax.rem(lanes[0:1, :], P_SIZE), -1)

    def build(i):
        rows = lax.broadcasted_iota(jnp.int32, (128, COLS), 0) + 128 * i
        S[aligned(128 * i, 128, 128), :] = jnp.where(rows == colidx, 1.0, 0.0).astype(BF)

    loop(0, WIDE // 128, build)
    E16[...] = jnp.where(lax.broadcasted_iota(jnp.int32, (GROUP, COLS), 0) == headof, 1.0, 0.0).astype(F32)
    for i in range(3):
        E16B[pl.ds(GROUP * i, GROUP), :] = E16[...].astype(BF)

    for load in loads:
        load.wait()

    upto = one_hot(Q, Q, lambda r, k: r <= k)
    pick = one_hot(COLS, 128, lambda r, k: r == P_SIZE * k)
    slots = dot(E16[...], pick)[:, :GROUP].astype(BF)
    slots3 = jnp.concatenate([slots] * 3, axis=0)
    upto_low = upto.astype(BF)

    def decays(s):
        rows = aligned(Q * s, Q, Q)
        sums = dot(parts(logd[:, rows]), upto_low)
        cum = parts(sums[:GROUP] + sums[GROUP : 2 * GROUP] + sums[2 * GROUP :])
        CUMR[:, rows] = dot(slots3, cum, TN)
        CUME[rows, :] = dot(cum, E16B[...], TN)

    loop(0, SPANS, decays)
    totals = sum(CUMR[:, pl.ds(Q * s + Q - 1, 1)] for s in range(SPANS))
    TOT[...] = dot(jnp.broadcast_to(totals, (GROUP, 8)), one_hot(GROUP, 128, lambda r, k: r == k), TN, precision=HIGH)

    STIN[0] = jnp.zeros((N, COLS), F32)

    def local_states(s):
        rows = aligned(Q * s, Q, Q)
        cume = CUME[rows, :]
        total = cume[Q - 1 : Q, :]
        xs = dot(x[rows, :], S[...])
        XS[rows, :] = xs.astype(BF)
        xt = (jnp.exp(total - cume) * xs).astype(BF)
        XT[rows, :] = xt
        part = dot(b[rows, :], xt, TN)
        PART[s] = part
        STIN[0] = jnp.exp(total) * STIN[0] + part

    loop(0, SPANS, local_states)
    ST[0] = STIN[0].astype(BF)

    pl.semaphore_wait(barrier, N_CTX - 1 + N_HEAD - 1 + 2 * cross)

    def decay_copy(k, at):
        to = lax.rem(ci + k, N_CTX)
        return rcopy(TOT, RD.at[aligned(8 * at, 8, 8), :], dec_sem.at[0, k], dec_sem.at[1, k], (to, hi))

    loop(1, N_CTX, lambda k: decay_copy(k, ci).start())
    RD[aligned(8 * ci, 8, 8), :] = TOT[...]

    forward = Exchange(ST.at[0], FL, FB, FE, fex_sem, ci, hi)
    forward.start()


    def g_tile(token, feature, q):
        return G.at[token, :, q, :, aligned(TOK * feature, TOK, TOK)]

    def quarter(q, p):
        return g.at[:, q, :, pl.ds(TOK * p, TOK)]

    def a2a_copy(q, p, slot):
        return rcopy(
            quarter(q, p), g_tile(y, xx, q), a2a_sem.at[0, q, p], a2a_sem.at[1, q, slot], (4 * z + 2 * cc + p, 2 * xx + half)
        )

    def a2a_start(q):
        for p in range(2):

            @pl.when(2 * cc + p != y)
            def _():
                a2a_copy(q, p, lax.rem(y, 2)).start()

    def x_gather(q, t):
        token = 2 * cc + t
        return Gather(
            lambda p: g_tile(token, p, q),
            lambda p, h: G.at[token, h, q, :, aligned(TOK * p, TOK, TOK)],
            lambda i: xs_sem.at[q, t, i],
            lambda i: xr_sem.at[q, t, i],
            xx, prv(xx), nxt(xx), at_x,
        )

    x_gathers = [[x_gather(q, t) for t in range(2)] for q in range(2)]
    ring_x = (xx, prv(xx), nxt(xx), lax.rem(xx + 2, 4))

    def sibling_copy(q, t, j, core):
        tile = g_tile(2 * core + t, ring_x[j], q)
        return rcopy(tile, tile, sib_sem.at[0, q, t, j], sib_sem.at[1, q, t, j], sibling)

    def x_launch(q, t):
        x_gathers[q][t].start()
        sibling_copy(q, t, 0, cc).start()

    def own_copy(q, p):
        return pltpu.make_async_copy(quarter(q, p), g_tile(y, xx, q), own_sem.at[q])

    def x_own():
        for p in range(2):

            @pl.when(2 * cc + p == y)
            def _():
                for q in range(2):
                    own_copy(q, p).start()
                for q in range(2):
                    own_copy(q, p).wait()
                    x_launch(q, p)

    def x_rest(q):
        for t in range(2):

            @pl.when(2 * cc + t != y)
            def _():
                rcopy(
                    quarter(q, t), g_tile(2 * cc + t, xx, q), a2a_sem.at[0, q, t], a2a_sem.at[1, q, t], sibling
                ).wait_recv()
                x_launch(q, t)

    def x_forward(q):
        for t in range(2):
            x_gathers[q][t].forward()
            sibling_copy(q, t, 1, cc).start()
            sibling_copy(q, t, 2, cc).start()

    def x_finish(q):
        for t in range(2):
            x_gathers[q][t].finish()
            sibling_copy(q, t, 3, cc).start()
        for t in range(2):
            for j in range(4):
                sibling_copy(q, t, j, 1 - cc).wait_recv()

    a2a_start(0)
    x_own()

    def pick_w(i):
        W[aligned(TOK * z + 128 * i, 128, 128), :] = dot(w[aligned(128 * i, 128, 128), :], S[...]).astype(BF)

    loop(0, TOK // 128, pick_w)

    def w_gather(q):
        return Gather(
            lambda p: W.at[aligned(TOK * p + TOK // 2 * q, TOK // 2, TOK // 2), :],
            lambda p, h: W.at[aligned(TOK * p + TOK // 2 * q + TOK // 4 * h, TOK // 4, TOK // 4), :],
            lambda i: wag_sem.at[q, 0, i],
            lambda i: wag_sem.at[q, 1, i],
            z, prv(z), nxt(z), at_z,
        )

    w_gathers = [w_gather(q) for q in range(2)]
    sub = lax.broadcasted_iota(jnp.int32, (Q, Q), 0)
    lane = lax.broadcasted_iota(jnp.int32, (Q, Q), 1)
    left_half = lane < P_SIZE
    causal = lane <= sub

    def inside(s):
        rows = aligned(Q * s, Q, Q)
        cb = dot(c[rows, :], b[rows, :], NT)
        for k in range(PAIRS):
            cols = pl.ds(Q * k, Q)
            for h in range(2):
                head = 2 * k + h
                differ = CUME[rows, pl.ds(P_SIZE * head, 1)] - CUMR[pl.ds(head, 1), rows]
                low = jnp.where(causal, jnp.exp(jnp.where(causal, differ, 0.0)), 0.0)
                L[PAIRS * s + k, pl.ds(Q * h, Q), :] = low
                MS[PAIRS * s + k, pl.ds(Q * h, Q), :] = (low * cb).astype(BF)
            both = dot(MS[PAIRS * s + k], XS[rows, cols])
            YF[rows, cols] = jnp.where(left_half, both[:Q], both[Q:])

    rowidx = jnp.broadcast_to(colidx, (8, COLS)).astype(F32).T[:, 0:1].astype(jnp.int32)
    for i in range(COLS // 128):
        ids = lax.broadcasted_iota(jnp.int32, (128, WIDE), 1)
        S_T[pl.ds(128 * i, 128), :] = jnp.where(ids == rowidx[128 * i : 128 * i + 128], 1.0, 0.0).astype(BF)

    loop(0, SPANS, inside)

    loop(1, N_CTX, lambda k: decay_copy(k, lax.rem(ci + N_CTX - k, N_CTX)).wait_recv())
    first_slot = CAP // 2 * lax.rem(ci, 2)
    DEC[...] = jnp.exp(dot(RD[...], one_hot(128, HALF, lambda r, k: r == k // P_SIZE + first_slot), precision=HIGH))
    forward.landed()
    forward.scan(DEC, range(N_CTX))
    forward.reply()
    w_gathers[0].start()
    w_gathers[1].start()
    a2a_start(1)
    x_rest(0)
    forward.replied()
    STIN[0] = FE[...].astype(F32)

    def outputs(s):
        rows = aligned(Q * s, Q, Q)
        cume = CUME[rows, :]
        state_in = STIN[s]
        inter = jnp.exp(cume) * dot(c[rows, :], state_in.astype(BF))
        YI[rows, :] = inter
        whole = YF[rows, :] + inter
        YF[rows, :] = whole
        YT[:, aligned(TOK * y + Q * s, Q, Q)] = whole.T.astype(BF)
        STIN[s + 1] = jnp.exp(cume[Q - 1 : Q, :]) * state_in + PART[s]

    loop(0, SPANS, outputs)
    y_gather = Gather(
        lambda p: YT.at[:, aligned(TOK * p, TOK, TOK)],
        lambda p, h: YT.at[pl.ds(HALF * h, HALF), aligned(TOK * p, TOK, TOK)],
        lambda i: yag_sem.at[0, i],
        lambda i: yag_sem.at[1, i],
        y, prv(y), nxt(y), at_y,
    )
    y_gather.start()

    def head_term(q):
        return lambda block: dot(G[block, :, q].reshape(TOK // 2, 4 * TOK), W[...])

    def weight_term(block):
        return dot(YT[...], G[:, :, :, :, aligned(TOK * block, TOK, TOK)].reshape(4 * TOK, TOK))

    heads = (
        Scatter(
            head_term(0), TOK // 2, a_far, a_right, a_left, a_vl, a_vr, a_fl, a_fr, a_own,
            hrs_sem.at[0, 0], hrs_sem.at[0, 1], y, at_y,
        ),
        Scatter(
            head_term(1), TOK // 2, b_far, b_right, b_left, b_vl, b_vr, b_fl, b_fr, b_own,
            hrs_sem.at[1, 0], hrs_sem.at[1, 1], y, at_y,
        ),
    )
    weights = Scatter(
        weight_term, COLS, w_far, w_right, w_left, w_vl, w_vr, w_fl, w_fr, w_own,
        wrs_sem.at[0], wrs_sem.at[1], z, at_z,
    )

    def local_adjoint(s):
        rows = pl.ds(Q * s, Q)
        GK[rows, :] = heads[s % 2].result(pl.ds(Q * (s // 2), Q)).astype(BF)
        gh = (jnp.exp(CUME[rows, :]) * GK[rows, :].astype(F32)).astype(BF)
        GH[rows, :] = gh
        PART[s] = dot(c[rows, :], gh, TN)

    def inside_grad(s):
        rows = aligned(Q * s, Q, Q)
        total = jnp.zeros((Q, Q), F32)
        for k in range(PAIRS):
            cols = pl.ds(Q * k, Q)
            gk = GK[rows, cols].astype(F32)
            stack = jnp.concatenate(
                [jnp.where(left_half, gk, 0.0), jnp.where(left_half, 0.0, gk)], axis=0
            ).astype(BF)
            weighted = L[PAIRS * s + k] * dot(stack, XS[rows, cols], NT)
            total = total + weighted[:Q] + weighted[Q:]
            IG[rows, cols] = dot(MS[PAIRS * s + k], stack, TN)
        sg = total.astype(BF)
        B0[rows, :] = dot(sg, c[rows, :], TN)
        CP[rows, :] = (dot(sg, b[rows, :]) + dot(GH[rows, :], STIN[s].astype(BF), NT)).astype(BF)

    x_forward(0)
    x_rest(1)
    w_gathers[0].forward()
    w_gathers[1].forward()
    y_gather.forward()
    x_forward(1)
    w_gathers[0].finish()
    w_gathers[1].finish()
    x_finish(0)
    heads[0].first()
    x_finish(1)
    heads[0].second()
    y_gather.finish()
    weights.first()
    heads[1].first()
    heads[0].last()
    heads[0].finish()
    local_adjoint(0)
    local_adjoint(2)
    heads[1].second()
    heads[1].last()
    inside_grad(0)
    inside_grad(2)
    heads[1].finish()
    local_adjoint(1)
    local_adjoint(3)

    ADJ[SPANS] = jnp.zeros((N, COLS), F32)
    after = jnp.zeros((1, COLS), F32)
    for s in reversed(range(SPANS)):
        total = CUME[pl.ds(Q * s + Q - 1, 1), :]
        AFTER[pl.ds(s, 1), :] = jnp.exp(after)
        after = after + total
        ADJ[s] = jnp.exp(total) * ADJ[s + 1] + PART[s]
    ST[1] = ADJ[0].astype(BF)
    backward = Exchange(ST.at[1], AL, AB, AE, bex_sem, ci, hi)
    backward.start()
    inside_grad(1)
    inside_grad(3)

    def local_b(s):
        rows = aligned(Q * s, Q, Q)
        B0[rows, :] = B0[rows, :] + dot(XT[rows, :], ADJ[s + 1].astype(BF), NT)

    loop(0, SPANS - 1, local_b)
    c_sum = HeadSum(CP, CL, CT, out_c, c_sem, out_sem.at[1], ci, hi)
    c_sum.start()

    loop(1, N_CTX, lambda k: decay_copy(k, ci).wait_send())
    forward.drain()
    for q in range(2):
        w_gathers[q].drain()
    y_gather.drain()
    for q in range(2):
        for p in range(2):

            @pl.when(2 * cc + p != y)
            def _():
                a2a_copy(q, p, 0).wait_send()

        for t in range(2):
            x_gathers[q][t].drain()
            for j in range(4):
                sibling_copy(q, t, j, cc).wait_send()

    backward.landed()
    backward.scan(DEC, reversed(range(N_CTX)))
    backward.reply()
    weights.second()
    weights.last()
    c_sum.reduce()
    backward.replied()

    def whole_b(s):
        rows = aligned(Q * s, Q, Q)
        carried = (AFTER[pl.ds(s, 1), :] * AE[...].astype(F32)).astype(BF)
        BP[rows, :] = (B0[rows, :] + dot(XT[rows, :], carried, NT)).astype(BF)

    loop(0, SPANS, whole_b)
    b_sum = HeadSum(BP, BL, BT, out_b, b_sem, out_sem.at[2], ci, hi)
    b_sum.start()

    def closing(s):
        rows = aligned(Q * s, Q, Q)
        cume = CUME[rows, :]
        total = cume[Q - 1 : Q, :]
        adjoint = ADJ[s + 1] + AFTER[pl.ds(s, 1), :] * AE[...].astype(F32)
        in_grad = IG[rows, :] + jnp.exp(total - cume) * dot(b[rows, :], adjoint.astype(BF))
        IGB[rows, :] = in_grad.astype(BF)
        gk = GK[rows, :].astype(F32)
        step = XS[rows, :].astype(F32) * in_grad - gk * YF[rows, :]
        start = jnp.sum(gk * YI[rows, :], axis=0, keepdims=True) + jnp.exp(total) * jnp.sum(
            adjoint * STIN[s], axis=0, keepdims=True
        )
        row = lax.broadcasted_iota(jnp.int32, (Q, COLS), 0)
        step = jnp.where(row == 0, start, pltpu.roll(step, 1, 0))
        high = step.astype(BF)
        rest = (step - high.astype(F32)).astype(BF)
        steps = dot(E16B[:GROUP], high, NT) + dot(E16B[:GROUP], rest, NT)
        O_D[:, rows] = dot(steps, upto, precision=HIGH) * (1.0 / math.sqrt(P_SIZE * D))

    def spread_in(i):
        rows = aligned(128 * i, 128, 128)
        O_IG[rows, :] = dot(IGB[rows, :], S_T[...]).astype(BF)

    def spread_w(i):
        cols = aligned(128 * i, 128, 128)
        block = (weights.result(slice(None), cols) * (1.0 / math.sqrt(D))).astype(BF)
        O_W[cols, :] = dot(block, S_T[...], TN).astype(BF)

    stores = [
        pltpu.make_async_copy(O_IG, out_ig, out_sem.at[0]),
        pltpu.make_async_copy(O_D, out_decay, out_sem.at[3]),
        pltpu.make_async_copy(O_W, out_w, out_sem.at[4]),
    ]
    loop(0, SPANS, closing)
    stores[1].start()
    b_sum.reduce()
    loop(0, TOK // 128, spread_in)
    stores[0].start()
    weights.finish()
    loop(0, TOK // 128, spread_w)
    stores[2].start()
    c_sum.finish()
    heads[0].drain()
    heads[1].drain()
    weights.drain()
    backward.drain()
    c_sum.drain()
    b_sum.finish()

    b_sum.drain()
    for store in stores:
        store.wait()


def hand_over(*refs):
    ins, outs, held, scaled, sems = refs[:5], refs[5:10], refs[10:15], refs[15:17], refs[17]
    sources = [held[0], *scaled, held[3], held[4]]
    reads = [pltpu.make_async_copy(ins[i], held[i], sems.at[0, i]) for i in range(5)]
    writes = [pltpu.make_async_copy(sources[i], outs[i], sems.at[1, i]) for i in range(5)]
    for read in reads:
        read.start()
    for i in (0, 4, 3, 1, 2):
        reads[i].wait()
        if i == 1:
            scaled[0][...] = held[1][...].astype(F32) / math.sqrt(KEPT * P_SIZE)
        if i == 2:
            scaled[1][...] = held[2][...].astype(F32) * math.sqrt(N / (KEPT * P_SIZE * D))
        writes[i].start()
    for write in writes:
        write.wait()


def per_device(g_out, w_out, x_act, b_proj, c_proj, log_decay, kept_heads):
    hbm = pl.BlockSpec(memory_space=pl.ANY)
    buf = pltpu.VMEM
    dma = pltpu.SemaphoreType.DMA

    def ring(rows, cols):
        h = rows // 2
        return [
            buf((rows, cols), BF), buf((rows, cols), BF), buf((rows, cols), BF), buf((h, cols), BF), buf((h, cols), BF),
            buf((rows, cols), BF), buf((rows, cols), BF), buf((rows, cols), F32),
        ]

    def head_sum():
        return [
            buf((TOK, N), BF), buf((N_HEAD, TOK // N_HEAD, N), BF), buf((TOK // N_HEAD, N), BF)
        ]

    outs = (
        jax.ShapeDtypeStruct((TOK, WIDE), BF),
        jax.ShapeDtypeStruct((TOK, N), F32),
        jax.ShapeDtypeStruct((TOK, N), F32),
        jax.ShapeDtypeStruct((GROUP, TOK), F32),
        jax.ShapeDtypeStruct((TOK, WIDE), BF),
    )
    sums = jax.ShapeDtypeStruct((TOK, N), BF)
    held = (outs[0], sums, sums, *outs[3:])
    results = pl.pallas_call(
        kernel,
        out_shape=held,
        in_specs=[pl.BlockSpec(memory_space=pltpu.SMEM)] + [hbm] * 6,
        out_specs=[hbm] * 5,
        scratch_shapes=[
            buf((TOK, WIDE), BF), buf((TOK, WIDE), BF), buf((TOK, N), BF), buf((TOK, N), BF), buf((GROUP, TOK), F32),
            buf((WIDE, COLS), BF), buf((COLS, WIDE), BF), buf((GROUP, COLS), F32), buf((3 * GROUP, COLS), BF),
            buf((4, 2, 2, TOK // 4, 4 * TOK), BF), buf((4 * TOK, COLS), BF), buf((COLS, 4 * TOK), BF),
            buf((TOK, COLS), BF), buf((TOK, COLS), BF), buf((TOK, COLS), F32), buf((GROUP, TOK), F32),
            buf((SPANS, N, COLS), F32), buf((SPANS + 1, N, COLS), F32), buf((SPANS + 1, N, COLS), F32),
            buf((TOK, COLS), F32), buf((TOK, COLS), F32),
            buf((SPANS * PAIRS, 2 * Q, Q), F32), buf((SPANS * PAIRS, 2 * Q, Q), BF),
            buf((TOK, COLS), BF), buf((TOK, COLS), BF), buf((TOK, COLS), F32), buf((TOK, COLS), BF),
            buf((TOK, N), F32),
            buf((8, COLS), F32), buf((8, 128), F32), buf((8 * N_CTX, 128), F32), buf((8 * N_CTX, HALF), F32), buf((2, N, COLS), BF),
            buf((16 * N_CTX, HALF), BF), buf((16 * N_CTX, HALF), BF), buf((N, COLS), BF),
            buf((16 * N_CTX, HALF), BF), buf((16 * N_CTX, HALF), BF), buf((N, COLS), BF),
            *head_sum(), *head_sum(),
            buf((TOK, WIDE), BF), buf((GROUP, TOK), F32), buf((TOK, WIDE), BF),
            *ring(TOK // 2, COLS), *ring(TOK // 2, COLS), *ring(COLS, TOK),
            dma((5,)), dma((2,)), dma((2, 2, 2)), dma((2, 2, 4)), dma((2, 2, 4)), dma((2, 2, 2, 4)), dma((2, 2, 4)),
            dma((2, 4)), dma((2, 2, 6)), dma((2, 6)), dma((2, N_CTX)), dma((4, N_CTX)), dma((4, N_CTX)),
            dma((4, N_HEAD)), dma((4, N_HEAD)), dma((5,)),
        ],
        compiler_params=pltpu.CompilerParams(
            collective_id=0, has_side_effects=True, vmem_limit_bytes=VMEM_LIMIT
        ),
        cost_estimate=pl.CostEstimate(flops=14_000_000_000, bytes_accessed=8_000_000, transcendentals=4_000_000),
    )(
        kept_heads, g_out.reshape(2, 2, TOK // 4, WIDE), w_out, x_act, b_proj, c_proj, log_decay,
    )
    return pl.pallas_call(
        hand_over,
        out_shape=outs,
        in_specs=[hbm] * 5,
        out_specs=[hbm] * 5,
        scratch_shapes=[*(buf(out.shape, out.dtype) for out in (*held, *outs[1:3])), dma((2, 5))],
        compiler_params=pltpu.CompilerParams(has_side_effects=True, vmem_limit_bytes=VMEM_LIMIT),
    )(*results)


def solution(mesh):
    in_specs = (
        P("ctx", "head"),
        P("ctx", "head"),
        P("ctx", "head"),
        P("ctx", None),
        P("ctx", None),
        P("head", "ctx"),
        P(),
    )
    out_specs = (
        P("ctx", "head"),
        P("ctx", None),
        P("ctx", None),
        P("head", "ctx"),
        P("ctx", "head"),
    )
    return jax.shard_map(
        per_device, mesh=mesh, in_specs=in_specs, out_specs=out_specs, check_vma=False
    )
```

```python
import math

import jax
import jax.numpy as jnp
from jax import lax
from jax.experimental import pallas as pl
from jax.experimental.pallas import tpu as pltpu
from jax.sharding import PartitionSpec as P

D = 8192
P_SIZE = 64
N = 128
KEPT = 64
Q = 128
TOK = 512
SPANS = TOK // Q
GROUP = 16
CAP = 12
COLS = CAP * P_SIZE
WIDE = GROUP * P_SIZE
PAIRS = CAP // 2
N_CTX = 16
N_HEAD = 8
HALF = COLS // 2
VMEM_LIMIT = 62 * 1024 * 1024

F32 = jnp.float32
BF = jnp.bfloat16
HIGH = lax.Precision.HIGHEST
MESH = pl.DeviceIdType.MESH
NN = (((1,), (0,)), ((), ()))
NT = (((1,), (1,)), ((), ()))
TN = (((0,), (0,)), ((), ()))


def dot(a, b, dims=NN, precision=None):
    return lax.dot_general(a, b, dims, precision=precision, preferred_element_type=F32)


def rcopy(src, dst, send_sem, recv_sem, device):
    return pltpu.make_async_remote_copy(
        src_ref=src,
        dst_ref=dst,
        send_sem=send_sem,
        recv_sem=recv_sem,
        device_id=device,
        device_id_type=MESH,
    )


def aligned(start, size, unit):
    return pl.ds(pl.multiple_of(start, unit), size)


def loop(lo, hi, body):
    def step(i, carry):
        body(i)
        return carry

    lax.fori_loop(lo, hi, step, 0)


class Gather:
    def __init__(self, block, half, send, recv, me, left, right, device):
        self.block, self.half, self.send, self.recv = block, half, send, recv
        self.me, self.left, self.right = me, left, right
        self.to_left, self.to_right = device(left), device(right)
        self.far = lax.rem(me + 2, 4)

    def copy(self, i):
        ref = (
            lambda: self.block(self.me),
            lambda: self.block(self.me),
            lambda: self.half(self.left, 0),
            lambda: self.half(self.right, 1),
        )[i]()
        return rcopy(ref, ref, self.send(i), self.recv(i), self.to_left if i % 2 else self.to_right)

    def landed(self, slot, ref):
        rcopy(ref, ref, self.send(slot), self.recv(slot), self.to_right).wait_recv()

    def start(self):
        self.copy(0).start()
        self.copy(1).start()

    def forward(self):
        self.landed(0, self.block(self.left))
        self.copy(2).start()
        self.landed(1, self.block(self.right))
        self.copy(3).start()

    def finish(self):
        self.landed(2, self.half(self.far, 0))
        self.landed(3, self.half(self.far, 1))

    def drain(self):
        for i in range(4):
            self.copy(i).wait_send()


class Scatter:
    def __init__(self, term, rows, far, right, left, via_l, via_r, from_l, from_r, own, send, recv, me, device):
        self.term, self.h = term, rows // 2
        self.far_buf, self.right_buf, self.left_buf = far, right, left
        self.via_l, self.via_r, self.from_l, self.from_r, self.own = via_l, via_r, from_l, from_r, own
        self.send, self.recv = send, recv
        self.me = me
        self.right, self.left, self.far = lax.rem(me + 1, 4), lax.rem(me + 3, 4), lax.rem(me + 2, 4)
        self.to_right, self.to_left = device(self.right), device(self.left)

    def copy(self, i):
        lo, hi = pl.ds(0, self.h), pl.ds(self.h, self.h)
        src, dst, to = (
            (self.far_buf.at[lo], self.via_l, self.to_right),
            (self.far_buf.at[hi], self.via_r, self.to_left),
            (self.right_buf.at[hi], self.from_l.at[hi], self.to_right),
            (self.left_buf.at[lo], self.from_r.at[lo], self.to_left),
            (self.right_buf.at[lo], self.from_l.at[lo], self.to_right),
            (self.left_buf.at[hi], self.from_r.at[hi], self.to_left),
        )[i]
        return rcopy(src, dst, self.send.at[i], self.recv.at[i], to)

    def first(self):
        h = self.h
        self.far_buf[...] = self.term(self.far).astype(BF)
        self.copy(0).start()
        self.copy(1).start()
        term = self.term(self.right)
        self.right_buf[h:] = term[h:].astype(BF)
        self.copy(2).start()
        self.own[:h] = term[:h]
        term = self.term(self.left)
        self.left_buf[:h] = term[:h].astype(BF)
        self.copy(3).start()
        self.own[h:] = term[h:]

    def second(self):
        h = self.h
        self.copy(0).wait_recv()
        self.right_buf[:h] = (self.own[:h] + self.via_l[...].astype(F32)).astype(BF)
        self.copy(4).start()
        self.copy(1).wait_recv()
        self.left_buf[h:] = (self.own[h:] + self.via_r[...].astype(F32)).astype(BF)
        self.copy(5).start()

    def last(self):
        self.own[...] = self.term(self.me)

    def finish(self):
        for i in (2, 3, 4, 5):
            self.copy(i).wait_recv()

    def result(self, rows, cols=slice(None)):
        return self.own[rows, cols] + self.from_l[rows, cols].astype(F32) + self.from_r[rows, cols].astype(F32)

    def drain(self):
        for i in range(6):
            self.copy(i).wait_send()


class Exchange:
    def __init__(self, source, landed, back, entering, sems, ci, hi):
        self.source, self.landed_ref, self.back, self.entering = source, landed, back, entering
        self.sems, self.ci, self.hi = sems, ci, hi

    def cut(self, r):
        return aligned(16 * (r // 2), 16, 16), aligned(HALF * lax.rem(r, 2), HALF, 128)

    def slot(self, r):
        return aligned(16 * r, 16, 16)

    def out_copy(self, k, at):
        to = lax.rem(self.ci + k, N_CTX)
        return rcopy(
            self.source.at[self.cut(to)], self.landed_ref.at[self.slot(at), :],
            self.sems.at[0, k], self.sems.at[1, k], (to, self.hi),
        )

    def back_copy(self, k, at):
        to = lax.rem(self.ci + k, N_CTX)
        return rcopy(
            self.back.at[self.slot(to), :], self.entering.at[self.cut(at)],
            self.sems.at[2, k], self.sems.at[3, k], (to, self.hi),
        )

    def start(self):
        loop(1, N_CTX, lambda k: self.out_copy(k, self.ci).start())
        self.landed_ref[self.slot(self.ci), :] = self.source[self.cut(self.ci)]

    def landed(self):
        loop(1, N_CTX, lambda k: self.out_copy(k, lax.rem(self.ci + N_CTX - k, N_CTX)).wait_recv())

    def scan(self, decays, order):
        state = jnp.zeros((16, HALF), F32)
        for i in order:
            rows = pl.ds(16 * i, 16)
            self.back[rows, :] = state.astype(BF)
            state = decays[pl.ds(8 * i, 1), :] * state + self.landed_ref[rows, :].astype(F32)

    def reply(self):
        loop(1, N_CTX, lambda k: self.back_copy(k, self.ci).start())
        self.entering[self.cut(self.ci)] = self.back[self.slot(self.ci), :]

    def replied(self):
        loop(1, N_CTX, lambda k: self.back_copy(k, lax.rem(self.ci + N_CTX - k, N_CTX)).wait_recv())

    def drain(self):
        def one(k):
            self.out_copy(k, self.ci).wait_send()
            self.back_copy(k, self.ci).wait_send()

        loop(1, N_CTX, one)


class HeadSum:
    def __init__(self, part, landed, total, whole, sems, own_sem, ci, hi):
        self.part, self.landed_ref, self.total, self.whole = part, landed, total, whole
        self.sems, self.own_sem, self.ci, self.hi = sems, own_sem, ci, hi

    def own_copy(self):
        return pltpu.make_async_copy(self.total, self.whole.at[self.share(self.hi), :], self.own_sem)

    def share(self, r):
        return aligned(TOK // N_HEAD * r, TOK // N_HEAD, TOK // N_HEAD)

    def out_copy(self, k, at):
        to = lax.rem(self.hi + k, N_HEAD)
        return rcopy(
            self.part.at[self.share(to), :], self.landed_ref.at[at],
            self.sems.at[0, k], self.sems.at[1, k], (self.ci, to),
        )

    def back_copy(self, k, at):
        to = lax.rem(self.hi + k, N_HEAD)
        return rcopy(
            self.total, self.whole.at[self.share(at), :], self.sems.at[2, k], self.sems.at[3, k], (self.ci, to)
        )

    def start(self):
        loop(1, N_HEAD, lambda k: self.out_copy(k, self.hi).start())
        self.landed_ref[self.hi] = self.part[self.share(self.hi), :]

    def reduce(self):
        loop(1, N_HEAD, lambda k: self.out_copy(k, lax.rem(self.hi + N_HEAD - k, N_HEAD)).wait_recv())
        total = self.landed_ref[0].astype(F32)
        for i in range(1, N_HEAD):
            total = total + self.landed_ref[i].astype(F32)
        self.total[...] = total.astype(BF)
        loop(1, N_HEAD, lambda k: self.back_copy(k, self.hi).start())
        self.own_copy().start()

    def finish(self):
        loop(1, N_HEAD, lambda k: self.back_copy(k, lax.rem(self.hi + N_HEAD - k, N_HEAD)).wait_recv())
        self.own_copy().wait()

    def drain(self):
        def one(k):
            self.out_copy(k, self.hi).wait_send()
            self.back_copy(k, self.hi).wait_send()

        loop(1, N_HEAD, one)


def one_hot(rows, cols, hit):
    r = lax.broadcasted_iota(jnp.int32, (rows, cols), 0)
    k = lax.broadcasted_iota(jnp.int32, (rows, cols), 1)
    return jnp.where(hit(r, k), 1.0, 0.0).astype(F32)


def parts(a):
    high = a.astype(BF)
    rest = a - high.astype(F32)
    middle = rest.astype(BF)
    return jnp.concatenate([high, middle, (rest - middle.astype(F32)).astype(BF)], axis=0)


def kernel(
    kept, g, w_in, x_in, b_in, c_in, logd_in,
    out_ig, out_b, out_c, out_decay, out_w,
    w, x, b, c, logd, S, S_T, E16, E16B, G, W, YT, XS, XT, CUME, CUMR, PART, STIN, ADJ, YF, YI, L, MS, GK, GH, IG, IGB, B0,
    AFTER, TOT, RD, DEC, ST, FL, FB, FE, AL, AB, AE, BP, BL, BT, CP, CL, CT, O_IG, O_D, O_W,
    a_far, a_right, a_left, a_vl, a_vr, a_fl, a_fr, a_own,
    b_far, b_right, b_left, b_vl, b_vr, b_fl, b_fr, b_own,
    w_far, w_right, w_left, w_vl, w_vr, w_fl, w_fr, w_own,
    loc_sem, own_sem, a2a_sem, xs_sem, xr_sem, sib_sem, wag_sem, yag_sem, hrs_sem, wrs_sem, dec_sem, fex_sem, bex_sem,
    b_sem, c_sem, out_sem,
):
    ci, hi = lax.axis_index("ctx"), lax.axis_index("head")
    z, y = ci // 4, lax.rem(ci, 4)
    xx, cc = hi // 2, lax.rem(hi, 2)
    half = y // 2
    cross = lax.rem(half + cc, 2)
    at_x = lambda p: (ci, 2 * p + cc)
    at_y = lambda p: (4 * z + p, hi)
    at_z = lambda p: (4 * p + y, hi)
    sibling = (ci, 2 * xx + 1 - cc)
    nxt = lambda p: lax.rem(p + 1, 4)
    prv = lambda p: lax.rem(p + 3, 4)

    barrier = pltpu.get_barrier_semaphore()

    def greet(device):
        pl.semaphore_signal(barrier, inc=1, device_id=device, device_id_type=MESH)

    loop(1, N_CTX, lambda k: greet((lax.rem(ci + k, N_CTX), hi)))
    loop(1, N_HEAD, lambda k: greet((ci, lax.rem(hi + k, N_HEAD))))

    @pl.when(cross == 1)
    def _():
        for p in range(2):
            greet((4 * z + 2 * cc + p, 2 * xx + 1 - cc))

    loads = [
        pltpu.make_async_copy(src, dst, loc_sem.at[i])
        for i, (src, dst) in enumerate(((w_in, w), (x_in, x), (b_in, b), (c_in, c), (logd_in, logd)))
    ]
    for load in loads:
        load.start()

    lanes = lax.broadcasted_iota(jnp.int32, (8, COLS), 1)

    def place(k, carry):
        headof, rank = carry
        local = kept[k] - GROUP * hi
        mine = (local >= 0) & (local < GROUP)
        headof = jnp.where(lanes // P_SIZE == jnp.where(mine, rank, -1), local, headof)
        return headof, rank + jnp.where(mine, 1, 0)

    headof, _ = lax.fori_loop(0, KEPT, place, (jnp.full((8, COLS), -1, jnp.int32), jnp.int32(0)))
    headof = headof[0:1, :]
    colidx = jnp.where(headof >= 0, P_SIZE * headof + lax.rem(lanes[0:1, :], P_SIZE), -1)

    def build(i):
        rows = lax.broadcasted_iota(jnp.int32, (128, COLS), 0) + 128 * i
        S[aligned(128 * i, 128, 128), :] = jnp.where(rows == colidx, 1.0, 0.0).astype(BF)

    loop(0, WIDE // 128, build)
    E16[...] = jnp.where(lax.broadcasted_iota(jnp.int32, (GROUP, COLS), 0) == headof, 1.0, 0.0).astype(F32)
    for i in range(3):
        E16B[pl.ds(GROUP * i, GROUP), :] = E16[...].astype(BF)

    for load in loads:
        load.wait()

    upto = one_hot(Q, Q, lambda r, k: r <= k)
    pick = one_hot(COLS, 128, lambda r, k: r == P_SIZE * k)
    slots = dot(E16[...], pick)[:, :GROUP].astype(BF)
    slots3 = jnp.concatenate([slots] * 3, axis=0)
    upto_low = upto.astype(BF)

    def decays(s):
        rows = aligned(Q * s, Q, Q)
        sums = dot(parts(logd[:, rows]), upto_low)
        cum = parts(sums[:GROUP] + sums[GROUP : 2 * GROUP] + sums[2 * GROUP :])
        CUMR[:, rows] = dot(slots3, cum, TN)
        CUME[rows, :] = dot(cum, E16B[...], TN)

    loop(0, SPANS, decays)
    totals = sum(CUMR[:, pl.ds(Q * s + Q - 1, 1)] for s in range(SPANS))
    TOT[...] = dot(jnp.broadcast_to(totals, (GROUP, 8)), one_hot(GROUP, 128, lambda r, k: r == k), TN, precision=HIGH)

    STIN[0] = jnp.zeros((N, COLS), F32)

    def local_states(s):
        rows = aligned(Q * s, Q, Q)
        cume = CUME[rows, :]
        total = cume[Q - 1 : Q, :]
        xs = dot(x[rows, :], S[...])
        XS[rows, :] = xs.astype(BF)
        xt = (jnp.exp(total - cume) * xs).astype(BF)
        XT[rows, :] = xt
        part = dot(b[rows, :], xt, TN)
        PART[s] = part
        STIN[0] = jnp.exp(total) * STIN[0] + part

    loop(0, SPANS, local_states)
    ST[0] = STIN[0].astype(BF)

    pl.semaphore_wait(barrier, N_CTX - 1 + N_HEAD - 1 + 2 * cross)

    def decay_copy(k, at):
        to = lax.rem(ci + k, N_CTX)
        return rcopy(TOT, RD.at[aligned(8 * at, 8, 8), :], dec_sem.at[0, k], dec_sem.at[1, k], (to, hi))

    loop(1, N_CTX, lambda k: decay_copy(k, ci).start())
    RD[aligned(8 * ci, 8, 8), :] = TOT[...]

    forward = Exchange(ST.at[0], FL, FB, FE, fex_sem, ci, hi)
    forward.start()


    def g_tile(token, feature, q):
        return G.at[token, :, q, :, aligned(TOK * feature, TOK, TOK)]

    def quarter(q, p):
        return g.at[:, q, :, pl.ds(TOK * p, TOK)]

    def a2a_copy(q, p, slot):
        return rcopy(
            quarter(q, p), g_tile(y, xx, q), a2a_sem.at[0, q, p], a2a_sem.at[1, q, slot], (4 * z + 2 * cc + p, 2 * xx + half)
        )

    def a2a_start(q):
        for p in range(2):

            @pl.when(2 * cc + p != y)
            def _():
                a2a_copy(q, p, lax.rem(y, 2)).start()

    def x_gather(q, t):
        token = 2 * cc + t
        return Gather(
            lambda p: g_tile(token, p, q),
            lambda p, h: G.at[token, h, q, :, aligned(TOK * p, TOK, TOK)],
            lambda i: xs_sem.at[q, t, i],
            lambda i: xr_sem.at[q, t, i],
            xx, prv(xx), nxt(xx), at_x,
        )

    x_gathers = [[x_gather(q, t) for t in range(2)] for q in range(2)]
    ring_x = (xx, prv(xx), nxt(xx), lax.rem(xx + 2, 4))

    def sibling_copy(q, t, j, core):
        tile = g_tile(2 * core + t, ring_x[j], q)
        return rcopy(tile, tile, sib_sem.at[0, q, t, j], sib_sem.at[1, q, t, j], sibling)

    def x_launch(q, t):
        x_gathers[q][t].start()
        sibling_copy(q, t, 0, cc).start()

    def own_copy(q, p):
        return pltpu.make_async_copy(quarter(q, p), g_tile(y, xx, q), own_sem.at[q])

    def x_own():
        for p in range(2):

            @pl.when(2 * cc + p == y)
            def _():
                for q in range(2):
                    own_copy(q, p).start()
                for q in range(2):
                    own_copy(q, p).wait()
                    x_launch(q, p)

    def x_rest(q):
        for t in range(2):

            @pl.when(2 * cc + t != y)
            def _():
                rcopy(
                    quarter(q, t), g_tile(2 * cc + t, xx, q), a2a_sem.at[0, q, t], a2a_sem.at[1, q, t], sibling
                ).wait_recv()
                x_launch(q, t)

    def x_forward(q):
        for t in range(2):
            x_gathers[q][t].forward()
            sibling_copy(q, t, 1, cc).start()
            sibling_copy(q, t, 2, cc).start()

    def x_finish(q):
        for t in range(2):
            x_gathers[q][t].finish()
            sibling_copy(q, t, 3, cc).start()
        for t in range(2):
            for j in range(4):
                sibling_copy(q, t, j, 1 - cc).wait_recv()

    a2a_start(0)
    x_own()

    def pick_w(i):
        W[aligned(TOK * z + 128 * i, 128, 128), :] = dot(w[aligned(128 * i, 128, 128), :], S[...]).astype(BF)

    loop(0, TOK // 128, pick_w)

    def w_gather(q):
        return Gather(
            lambda p: W.at[aligned(TOK * p + TOK // 2 * q, TOK // 2, TOK // 2), :],
            lambda p, h: W.at[aligned(TOK * p + TOK // 2 * q + TOK // 4 * h, TOK // 4, TOK // 4), :],
            lambda i: wag_sem.at[q, 0, i],
            lambda i: wag_sem.at[q, 1, i],
            z, prv(z), nxt(z), at_z,
        )

    w_gathers = [w_gather(q) for q in range(2)]
    sub = lax.broadcasted_iota(jnp.int32, (Q, Q), 0)
    lane = lax.broadcasted_iota(jnp.int32, (Q, Q), 1)
    left_half = lane < P_SIZE
    causal = lane <= sub

    def inside(s):
        rows = aligned(Q * s, Q, Q)
        cb = dot(c[rows, :], b[rows, :], NT)
        for k in range(PAIRS):
            cols = pl.ds(Q * k, Q)
            for h in range(2):
                head = 2 * k + h
                differ = CUME[rows, pl.ds(P_SIZE * head, 1)] - CUMR[pl.ds(head, 1), rows]
                low = jnp.where(causal, jnp.exp(jnp.where(causal, differ, 0.0)), 0.0)
                L[PAIRS * s + k, pl.ds(Q * h, Q), :] = low
                MS[PAIRS * s + k, pl.ds(Q * h, Q), :] = (low * cb).astype(BF)
            both = dot(MS[PAIRS * s + k], XS[rows, cols])
            YF[rows, cols] = jnp.where(left_half, both[:Q], both[Q:])

    rowidx = jnp.broadcast_to(colidx, (8, COLS)).astype(F32).T[:, 0:1].astype(jnp.int32)
    for i in range(COLS // 128):
        ids = lax.broadcasted_iota(jnp.int32, (128, WIDE), 1)
        S_T[pl.ds(128 * i, 128), :] = jnp.where(ids == rowidx[128 * i : 128 * i + 128], 1.0, 0.0).astype(BF)

    loop(0, SPANS, inside)

    loop(1, N_CTX, lambda k: decay_copy(k, lax.rem(ci + N_CTX - k, N_CTX)).wait_recv())
    first_slot = CAP // 2 * lax.rem(ci, 2)
    DEC[...] = jnp.exp(dot(RD[...], one_hot(128, HALF, lambda r, k: r == k // P_SIZE + first_slot), precision=HIGH))
    forward.landed()
    forward.scan(DEC, range(N_CTX))
    forward.reply()
    w_gathers[0].start()
    w_gathers[1].start()
    a2a_start(1)
    x_rest(0)
    forward.replied()
    STIN[0] = FE[...].astype(F32)

    def outputs(s):
        rows = aligned(Q * s, Q, Q)
        cume = CUME[rows, :]
        state_in = STIN[s]
        inter = jnp.exp(cume) * dot(c[rows, :], state_in.astype(BF))
        YI[rows, :] = inter
        whole = YF[rows, :] + inter
        YF[rows, :] = whole
        YT[:, aligned(TOK * y + Q * s, Q, Q)] = whole.T.astype(BF)
        STIN[s + 1] = jnp.exp(cume[Q - 1 : Q, :]) * state_in + PART[s]

    def y_gather(q):
        return Gather(
            lambda p: YT.at[:, aligned(TOK * p + TOK // 2 * q, TOK // 2, TOK // 2)],
            lambda p, h: YT.at[pl.ds(HALF * h, HALF), aligned(TOK * p + TOK // 2 * q, TOK // 2, TOK // 2)],
            lambda i: yag_sem.at[q, 0, i],
            lambda i: yag_sem.at[q, 1, i],
            y, prv(y), nxt(y), at_y,
        )

    y_gathers = [y_gather(q) for q in range(2)]
    for q in range(2):
        loop(SPANS // 2 * q, SPANS // 2 * (q + 1), outputs)
        y_gathers[q].start()

    def head_term(q):
        return lambda block: dot(G[block, :, q].reshape(TOK // 2, 4 * TOK), W[...])

    def weight_term(block):
        return dot(YT[...], G[:, :, :, :, aligned(TOK * block, TOK, TOK)].reshape(4 * TOK, TOK))

    heads = (
        Scatter(
            head_term(0), TOK // 2, a_far, a_right, a_left, a_vl, a_vr, a_fl, a_fr, a_own,
            hrs_sem.at[0, 0], hrs_sem.at[0, 1], y, at_y,
        ),
        Scatter(
            head_term(1), TOK // 2, b_far, b_right, b_left, b_vl, b_vr, b_fl, b_fr, b_own,
            hrs_sem.at[1, 0], hrs_sem.at[1, 1], y, at_y,
        ),
    )
    weights = Scatter(
        weight_term, COLS, w_far, w_right, w_left, w_vl, w_vr, w_fl, w_fr, w_own,
        wrs_sem.at[0], wrs_sem.at[1], z, at_z,
    )

    def local_adjoint(s):
        rows = pl.ds(Q * s, Q)
        GK[rows, :] = heads[s % 2].result(pl.ds(Q * (s // 2), Q)).astype(BF)
        gh = (jnp.exp(CUME[rows, :]) * GK[rows, :].astype(F32)).astype(BF)
        GH[rows, :] = gh
        PART[s] = dot(c[rows, :], gh, TN)

    def inside_grad(s):
        rows = aligned(Q * s, Q, Q)
        total = jnp.zeros((Q, Q), F32)
        for k in range(PAIRS):
            cols = pl.ds(Q * k, Q)
            gk = GK[rows, cols].astype(F32)
            stack = jnp.concatenate(
                [jnp.where(left_half, gk, 0.0), jnp.where(left_half, 0.0, gk)], axis=0
            ).astype(BF)
            weighted = L[PAIRS * s + k] * dot(stack, XS[rows, cols], NT)
            total = total + weighted[:Q] + weighted[Q:]
            IG[rows, cols] = dot(MS[PAIRS * s + k], stack, TN)
        sg = total.astype(BF)
        B0[rows, :] = dot(sg, c[rows, :], TN)
        CP[rows, :] = (dot(sg, b[rows, :]) + dot(GH[rows, :], STIN[s].astype(BF), NT)).astype(BF)

    x_forward(0)
    x_rest(1)
    w_gathers[0].forward()
    y_gathers[0].forward()
    w_gathers[1].forward()
    x_forward(1)
    y_gathers[1].forward()
    w_gathers[0].finish()
    w_gathers[1].finish()
    x_finish(0)
    heads[0].first()
    x_finish(1)
    heads[0].second()
    y_gathers[0].finish()
    y_gathers[1].finish()
    weights.first()
    heads[1].first()
    heads[0].last()
    heads[0].finish()
    local_adjoint(0)
    local_adjoint(2)
    heads[1].second()
    heads[1].last()
    inside_grad(0)
    inside_grad(2)
    heads[1].finish()
    local_adjoint(1)
    local_adjoint(3)

    ADJ[SPANS] = jnp.zeros((N, COLS), F32)
    after = jnp.zeros((1, COLS), F32)
    for s in reversed(range(SPANS)):
        total = CUME[pl.ds(Q * s + Q - 1, 1), :]
        AFTER[pl.ds(s, 1), :] = jnp.exp(after)
        after = after + total
        ADJ[s] = jnp.exp(total) * ADJ[s + 1] + PART[s]
    ST[1] = ADJ[0].astype(BF)
    backward = Exchange(ST.at[1], AL, AB, AE, bex_sem, ci, hi)
    backward.start()
    inside_grad(1)
    inside_grad(3)

    def local_b(s):
        rows = aligned(Q * s, Q, Q)
        B0[rows, :] = B0[rows, :] + dot(XT[rows, :], ADJ[s + 1].astype(BF), NT)

    loop(0, SPANS - 1, local_b)
    c_sum = HeadSum(CP, CL, CT, out_c, c_sem, out_sem.at[1], ci, hi)
    c_sum.start()

    loop(1, N_CTX, lambda k: decay_copy(k, ci).wait_send())
    forward.drain()
    for q in range(2):
        w_gathers[q].drain()
    y_gathers[0].drain()
    y_gathers[1].drain()
    for q in range(2):
        for p in range(2):

            @pl.when(2 * cc + p != y)
            def _():
                a2a_copy(q, p, 0).wait_send()

        for t in range(2):
            x_gathers[q][t].drain()
            for j in range(4):
                sibling_copy(q, t, j, cc).wait_send()

    backward.landed()
    backward.scan(DEC, reversed(range(N_CTX)))
    backward.reply()
    weights.second()
    weights.last()
    c_sum.reduce()
    backward.replied()

    def whole_b(s):
        rows = aligned(Q * s, Q, Q)
        carried = (AFTER[pl.ds(s, 1), :] * AE[...].astype(F32)).astype(BF)
        BP[rows, :] = (B0[rows, :] + dot(XT[rows, :], carried, NT)).astype(BF)

    loop(0, SPANS, whole_b)
    b_sum = HeadSum(BP, BL, BT, out_b, b_sem, out_sem.at[2], ci, hi)
    b_sum.start()

    def closing(s):
        rows = aligned(Q * s, Q, Q)
        cume = CUME[rows, :]
        total = cume[Q - 1 : Q, :]
        adjoint = ADJ[s + 1] + AFTER[pl.ds(s, 1), :] * AE[...].astype(F32)
        in_grad = IG[rows, :] + jnp.exp(total - cume) * dot(b[rows, :], adjoint.astype(BF))
        IGB[rows, :] = in_grad.astype(BF)
        gk = GK[rows, :].astype(F32)
        step = XS[rows, :].astype(F32) * in_grad - gk * YF[rows, :]
        start = jnp.sum(gk * YI[rows, :], axis=0, keepdims=True) + jnp.exp(total) * jnp.sum(
            adjoint * STIN[s], axis=0, keepdims=True
        )
        row = lax.broadcasted_iota(jnp.int32, (Q, COLS), 0)
        step = jnp.where(row == 0, start, pltpu.roll(step, 1, 0))
        high = step.astype(BF)
        rest = (step - high.astype(F32)).astype(BF)
        steps = dot(E16B[:GROUP], high, NT) + dot(E16B[:GROUP], rest, NT)
        O_D[:, rows] = dot(steps, upto, precision=HIGH) * (1.0 / math.sqrt(P_SIZE * D))

    def spread_in(i):
        rows = aligned(128 * i, 128, 128)
        O_IG[rows, :] = dot(IGB[rows, :], S_T[...]).astype(BF)

    def spread_w(i):
        cols = aligned(128 * i, 128, 128)
        block = (weights.result(slice(None), cols) * (1.0 / math.sqrt(D))).astype(BF)
        O_W[cols, :] = dot(block, S_T[...], TN).astype(BF)

    stores = [
        pltpu.make_async_copy(O_IG, out_ig, out_sem.at[0]),
        pltpu.make_async_copy(O_D, out_decay, out_sem.at[3]),
        pltpu.make_async_copy(O_W, out_w, out_sem.at[4]),
    ]
    loop(0, SPANS, closing)
    stores[1].start()
    b_sum.reduce()
    loop(0, TOK // 128, spread_in)
    stores[0].start()
    weights.finish()
    loop(0, TOK // 128, spread_w)
    stores[2].start()
    c_sum.finish()
    heads[0].drain()
    heads[1].drain()
    weights.drain()
    backward.drain()
    c_sum.drain()
    b_sum.finish()

    b_sum.drain()
    for store in stores:
        store.wait()


def hand_over(*refs):
    ins, outs, held, scaled, sems = refs[:5], refs[5:10], refs[10:15], refs[15:17], refs[17]
    sources = [held[0], *scaled, held[3], held[4]]
    cuts = [(i, pl.ds(TOK // 4 * k, TOK // 4)) for k in range(4) for i in (0, 4)]
    cuts += [(3, pl.ds(0, GROUP)), (2, pl.ds(0, TOK)), (1, pl.ds(0, TOK))]
    reads, writes = [], []
    for n, (i, rows) in enumerate(cuts):
        reads.append(pltpu.make_async_copy(ins[i].at[rows], held[i].at[rows], sems.at[0, n]))
        writes.append(pltpu.make_async_copy(sources[i].at[rows], outs[i].at[rows], sems.at[1, n]))
    for read in reads:
        read.start()
    for (i, _), read, write in zip(cuts, reads, writes):
        read.wait()
        if i == 1:
            scaled[0][...] = held[1][...].astype(F32) / math.sqrt(KEPT * P_SIZE)
        if i == 2:
            scaled[1][...] = held[2][...].astype(F32) * math.sqrt(N / (KEPT * P_SIZE * D))
        write.start()
    for write in writes:
        write.wait()


def per_device(g_out, w_out, x_act, b_proj, c_proj, log_decay, kept_heads):
    hbm = pl.BlockSpec(memory_space=pl.ANY)
    buf = pltpu.VMEM
    dma = pltpu.SemaphoreType.DMA

    def ring(rows, cols):
        h = rows // 2
        return [
            buf((rows, cols), BF), buf((rows, cols), BF), buf((rows, cols), BF), buf((h, cols), BF), buf((h, cols), BF),
            buf((rows, cols), BF), buf((rows, cols), BF), buf((rows, cols), F32),
        ]

    def head_sum():
        return [
            buf((TOK, N), BF), buf((N_HEAD, TOK // N_HEAD, N), BF), buf((TOK // N_HEAD, N), BF)
        ]

    outs = (
        jax.ShapeDtypeStruct((TOK, WIDE), BF),
        jax.ShapeDtypeStruct((TOK, N), F32),
        jax.ShapeDtypeStruct((TOK, N), F32),
        jax.ShapeDtypeStruct((GROUP, TOK), F32),
        jax.ShapeDtypeStruct((TOK, WIDE), BF),
    )
    sums = jax.ShapeDtypeStruct((TOK, N), BF)
    held = (outs[0], sums, sums, *outs[3:])
    results = pl.pallas_call(
        kernel,
        out_shape=held,
        in_specs=[pl.BlockSpec(memory_space=pltpu.SMEM)] + [hbm] * 6,
        out_specs=[hbm] * 5,
        scratch_shapes=[
            buf((TOK, WIDE), BF), buf((TOK, WIDE), BF), buf((TOK, N), BF), buf((TOK, N), BF), buf((GROUP, TOK), F32),
            buf((WIDE, COLS), BF), buf((COLS, WIDE), BF), buf((GROUP, COLS), F32), buf((3 * GROUP, COLS), BF),
            buf((4, 2, 2, TOK // 4, 4 * TOK), BF), buf((4 * TOK, COLS), BF), buf((COLS, 4 * TOK), BF),
            buf((TOK, COLS), BF), buf((TOK, COLS), BF), buf((TOK, COLS), F32), buf((GROUP, TOK), F32),
            buf((SPANS, N, COLS), F32), buf((SPANS + 1, N, COLS), F32), buf((SPANS + 1, N, COLS), F32),
            buf((TOK, COLS), F32), buf((TOK, COLS), F32),
            buf((SPANS * PAIRS, 2 * Q, Q), F32), buf((SPANS * PAIRS, 2 * Q, Q), BF),
            buf((TOK, COLS), BF), buf((TOK, COLS), BF), buf((TOK, COLS), F32), buf((TOK, COLS), BF),
            buf((TOK, N), F32),
            buf((8, COLS), F32), buf((8, 128), F32), buf((8 * N_CTX, 128), F32), buf((8 * N_CTX, HALF), F32), buf((2, N, COLS), BF),
            buf((16 * N_CTX, HALF), BF), buf((16 * N_CTX, HALF), BF), buf((N, COLS), BF),
            buf((16 * N_CTX, HALF), BF), buf((16 * N_CTX, HALF), BF), buf((N, COLS), BF),
            *head_sum(), *head_sum(),
            buf((TOK, WIDE), BF), buf((GROUP, TOK), F32), buf((TOK, WIDE), BF),
            *ring(TOK // 2, COLS), *ring(TOK // 2, COLS), *ring(COLS, TOK),
            dma((5,)), dma((2,)), dma((2, 2, 2)), dma((2, 2, 4)), dma((2, 2, 4)), dma((2, 2, 2, 4)), dma((2, 2, 4)),
            dma((2, 2, 4)), dma((2, 2, 6)), dma((2, 6)), dma((2, N_CTX)), dma((4, N_CTX)), dma((4, N_CTX)),
            dma((4, N_HEAD)), dma((4, N_HEAD)), dma((5,)),
        ],
        compiler_params=pltpu.CompilerParams(
            collective_id=0, has_side_effects=True, vmem_limit_bytes=VMEM_LIMIT
        ),
        cost_estimate=pl.CostEstimate(flops=14_000_000_000, bytes_accessed=8_000_000, transcendentals=4_000_000),
    )(
        kept_heads, g_out.reshape(2, 2, TOK // 4, WIDE), w_out, x_act, b_proj, c_proj, log_decay,
    )
    return pl.pallas_call(
        hand_over,
        out_shape=outs,
        in_specs=[hbm] * 5,
        out_specs=[hbm] * 5,
        scratch_shapes=[*(buf(out.shape, out.dtype) for out in (*held, *outs[1:3])), dma((2, 11))],
        compiler_params=pltpu.CompilerParams(has_side_effects=True, vmem_limit_bytes=VMEM_LIMIT),
    )(*results)


def solution(mesh):
    in_specs = (
        P("ctx", "head"),
        P("ctx", "head"),
        P("ctx", "head"),
        P("ctx", None),
        P("ctx", None),
        P("head", "ctx"),
        P(),
    )
    out_specs = (
        P("ctx", "head"),
        P("ctx", None),
        P("ctx", None),
        P("head", "ctx"),
        P("ctx", "head"),
    )
    return jax.shard_map(
        per_device, mesh=mesh, in_specs=in_specs, out_specs=out_specs, check_vma=False
    )
```

```python
import math

import jax
import jax.numpy as jnp
from jax import lax
from jax.experimental import pallas as pl
from jax.experimental.pallas import tpu as pltpu
from jax.sharding import PartitionSpec as P

D = 8192
P_SIZE = 64
N = 128
KEPT = 64
Q = 128
TOK = 512
SPANS = TOK // Q
GROUP = 16
CAP = 12
COLS = CAP * P_SIZE
WIDE = GROUP * P_SIZE
PAIRS = CAP // 2
N_CTX = 16
N_HEAD = 8
HALF = COLS // 2
VMEM_LIMIT = 62 * 1024 * 1024

F32 = jnp.float32
BF = jnp.bfloat16
HIGH = lax.Precision.HIGHEST
MESH = pl.DeviceIdType.MESH
NN = (((1,), (0,)), ((), ()))
NT = (((1,), (1,)), ((), ()))
TN = (((0,), (0,)), ((), ()))


def dot(a, b, dims=NN, precision=None):
    return lax.dot_general(a, b, dims, precision=precision, preferred_element_type=F32)


def rcopy(src, dst, send_sem, recv_sem, device):
    return pltpu.make_async_remote_copy(
        src_ref=src,
        dst_ref=dst,
        send_sem=send_sem,
        recv_sem=recv_sem,
        device_id=device,
        device_id_type=MESH,
    )


def aligned(start, size, unit):
    return pl.ds(pl.multiple_of(start, unit), size)


def loop(lo, hi, body):
    def step(i, carry):
        body(i)
        return carry

    lax.fori_loop(lo, hi, step, 0)


class Gather:
    def __init__(self, block, half, send, recv, me, left, right, device):
        self.block, self.half, self.send, self.recv = block, half, send, recv
        self.me, self.left, self.right = me, left, right
        self.to_left, self.to_right = device(left), device(right)
        self.far = lax.rem(me + 2, 4)

    def copy(self, i):
        ref = (
            lambda: self.block(self.me),
            lambda: self.block(self.me),
            lambda: self.half(self.left, 0),
            lambda: self.half(self.right, 1),
        )[i]()
        return rcopy(ref, ref, self.send(i), self.recv(i), self.to_left if i % 2 else self.to_right)

    def landed(self, slot, ref):
        rcopy(ref, ref, self.send(slot), self.recv(slot), self.to_right).wait_recv()

    def start(self):
        self.copy(0).start()
        self.copy(1).start()

    def forward(self):
        self.landed(0, self.block(self.left))
        self.copy(2).start()
        self.landed(1, self.block(self.right))
        self.copy(3).start()

    def finish(self):
        self.landed(2, self.half(self.far, 0))
        self.landed(3, self.half(self.far, 1))

    def drain(self):
        for i in range(4):
            self.copy(i).wait_send()


class Scatter:
    def __init__(self, term, rows, far, right, left, via_l, via_r, from_l, from_r, own, send, recv, me, device):
        self.term, self.h = term, rows // 2
        self.far_buf, self.right_buf, self.left_buf = far, right, left
        self.via_l, self.via_r, self.from_l, self.from_r, self.own = via_l, via_r, from_l, from_r, own
        self.send, self.recv = send, recv
        self.me = me
        self.right, self.left, self.far = lax.rem(me + 1, 4), lax.rem(me + 3, 4), lax.rem(me + 2, 4)
        self.to_right, self.to_left = device(self.right), device(self.left)

    def copy(self, i):
        lo, hi = pl.ds(0, self.h), pl.ds(self.h, self.h)
        src, dst, to = (
            (self.far_buf.at[lo], self.via_l, self.to_right),
            (self.far_buf.at[hi], self.via_r, self.to_left),
            (self.right_buf.at[hi], self.from_l.at[hi], self.to_right),
            (self.left_buf.at[lo], self.from_r.at[lo], self.to_left),
            (self.right_buf.at[lo], self.from_l.at[lo], self.to_right),
            (self.left_buf.at[hi], self.from_r.at[hi], self.to_left),
        )[i]
        return rcopy(src, dst, self.send.at[i], self.recv.at[i], to)

    def first(self):
        h = self.h
        self.far_buf[...] = self.term(self.far).astype(BF)
        self.copy(0).start()
        self.copy(1).start()
        term = self.term(self.right)
        self.right_buf[h:] = term[h:].astype(BF)
        self.copy(2).start()
        self.own[:h] = term[:h]
        term = self.term(self.left)
        self.left_buf[:h] = term[:h].astype(BF)
        self.copy(3).start()
        self.own[h:] = term[h:]

    def second(self):
        h = self.h
        self.copy(0).wait_recv()
        self.right_buf[:h] = (self.own[:h] + self.via_l[...].astype(F32)).astype(BF)
        self.copy(4).start()
        self.copy(1).wait_recv()
        self.left_buf[h:] = (self.own[h:] + self.via_r[...].astype(F32)).astype(BF)
        self.copy(5).start()

    def last(self):
        self.own[...] = self.term(self.me)

    def finish(self):
        for i in (2, 3, 4, 5):
            self.copy(i).wait_recv()

    def result(self, rows, cols=slice(None)):
        return self.own[rows, cols] + self.from_l[rows, cols].astype(F32) + self.from_r[rows, cols].astype(F32)

    def drain(self):
        for i in range(6):
            self.copy(i).wait_send()


class Exchange:
    def __init__(self, source, landed, back, entering, sems, ci, hi):
        self.source, self.landed_ref, self.back, self.entering = source, landed, back, entering
        self.sems, self.ci, self.hi = sems, ci, hi

    def cut(self, r):
        return aligned(16 * (r // 2), 16, 16), aligned(HALF * lax.rem(r, 2), HALF, 128)

    def slot(self, r):
        return aligned(16 * r, 16, 16)

    def out_copy(self, k, at):
        to = lax.rem(self.ci + k, N_CTX)
        return rcopy(
            self.source.at[self.cut(to)], self.landed_ref.at[self.slot(at), :],
            self.sems.at[0, k], self.sems.at[1, k], (to, self.hi),
        )

    def back_copy(self, k, at):
        to = lax.rem(self.ci + k, N_CTX)
        return rcopy(
            self.back.at[self.slot(to), :], self.entering.at[self.cut(at)],
            self.sems.at[2, k], self.sems.at[3, k], (to, self.hi),
        )

    def start(self):
        loop(1, N_CTX, lambda k: self.out_copy(k, self.ci).start())
        self.landed_ref[self.slot(self.ci), :] = self.source[self.cut(self.ci)]

    def landed(self):
        loop(1, N_CTX, lambda k: self.out_copy(k, lax.rem(self.ci + N_CTX - k, N_CTX)).wait_recv())

    def scan(self, decays, order):
        state = jnp.zeros((16, HALF), F32)
        for i in order:
            rows = pl.ds(16 * i, 16)
            self.back[rows, :] = state.astype(BF)
            state = decays[pl.ds(8 * i, 1), :] * state + self.landed_ref[rows, :].astype(F32)

    def reply(self):
        loop(1, N_CTX, lambda k: self.back_copy(k, self.ci).start())
        self.entering[self.cut(self.ci)] = self.back[self.slot(self.ci), :]

    def replied(self):
        loop(1, N_CTX, lambda k: self.back_copy(k, lax.rem(self.ci + N_CTX - k, N_CTX)).wait_recv())

    def drain(self):
        def one(k):
            self.out_copy(k, self.ci).wait_send()
            self.back_copy(k, self.ci).wait_send()

        loop(1, N_CTX, one)


class HeadSum:
    def __init__(self, part, landed, total, whole, sems, own_sem, ci, hi):
        self.part, self.landed_ref, self.total, self.whole = part, landed, total, whole
        self.sems, self.own_sem, self.ci, self.hi = sems, own_sem, ci, hi

    def own_copy(self):
        return pltpu.make_async_copy(self.total, self.whole.at[self.share(self.hi), :], self.own_sem)

    def share(self, r):
        return aligned(TOK // N_HEAD * r, TOK // N_HEAD, TOK // N_HEAD)

    def out_copy(self, k, at):
        to = lax.rem(self.hi + k, N_HEAD)
        return rcopy(
            self.part.at[self.share(to), :], self.landed_ref.at[at],
            self.sems.at[0, k], self.sems.at[1, k], (self.ci, to),
        )

    def back_copy(self, k, at):
        to = lax.rem(self.hi + k, N_HEAD)
        return rcopy(
            self.total, self.whole.at[self.share(at), :], self.sems.at[2, k], self.sems.at[3, k], (self.ci, to)
        )

    def start(self):
        loop(1, N_HEAD, lambda k: self.out_copy(k, self.hi).start())
        self.landed_ref[self.hi] = self.part[self.share(self.hi), :]

    def reduce(self):
        loop(1, N_HEAD, lambda k: self.out_copy(k, lax.rem(self.hi + N_HEAD - k, N_HEAD)).wait_recv())
        total = self.landed_ref[0].astype(F32)
        for i in range(1, N_HEAD):
            total = total + self.landed_ref[i].astype(F32)
        self.total[...] = total.astype(BF)
        loop(1, N_HEAD, lambda k: self.back_copy(k, self.hi).start())
        self.own_copy().start()

    def finish(self):
        loop(1, N_HEAD, lambda k: self.back_copy(k, lax.rem(self.hi + N_HEAD - k, N_HEAD)).wait_recv())
        self.own_copy().wait()

    def drain(self):
        def one(k):
            self.out_copy(k, self.hi).wait_send()
            self.back_copy(k, self.hi).wait_send()

        loop(1, N_HEAD, one)


def one_hot(rows, cols, hit):
    r = lax.broadcasted_iota(jnp.int32, (rows, cols), 0)
    k = lax.broadcasted_iota(jnp.int32, (rows, cols), 1)
    return jnp.where(hit(r, k), 1.0, 0.0).astype(F32)


def parts(a):
    high = a.astype(BF)
    rest = a - high.astype(F32)
    middle = rest.astype(BF)
    return jnp.concatenate([high, middle, (rest - middle.astype(F32)).astype(BF)], axis=0)


def kernel(
    kept, g, w_in, x_in, b_in, c_in, logd_in,
    out_ig, out_b, out_c, out_decay, out_w,
    w, x, b, c, logd, S, S_T, E16, E16B, G, W, YT, XS, XT, CUME, CUMR, PART, STIN, ADJ, YF, YI, L, MS, GK, GH, IG, IGB, B0,
    AFTER, TOT, RD, DEC, ST, FL, FB, FE, AL, AB, AE, BP, BL, BT, CP, CL, CT, O_IG, O_D, O_W,
    a_far, a_right, a_left, a_vl, a_vr, a_fl, a_fr, a_own,
    b_far, b_right, b_left, b_vl, b_vr, b_fl, b_fr, b_own,
    w_far, w_right, w_left, w_vl, w_vr, w_fl, w_fr, w_own,
    loc_sem, own_sem, a2a_sem, xs_sem, xr_sem, sib_sem, wag_sem, yag_sem, hrs_sem, wrs_sem, dec_sem, fex_sem, bex_sem,
    b_sem, c_sem, out_sem,
):
    ci, hi = lax.axis_index("ctx"), lax.axis_index("head")
    z, y = ci // 4, lax.rem(ci, 4)
    xx, cc = hi // 2, lax.rem(hi, 2)
    half = y // 2
    cross = lax.rem(half + cc, 2)
    at_x = lambda p: (ci, 2 * p + cc)
    at_y = lambda p: (4 * z + p, hi)
    at_z = lambda p: (4 * p + y, hi)
    sibling = (ci, 2 * xx + 1 - cc)
    nxt = lambda p: lax.rem(p + 1, 4)
    prv = lambda p: lax.rem(p + 3, 4)

    barrier = pltpu.get_barrier_semaphore()

    def greet(device):
        pl.semaphore_signal(barrier, inc=1, device_id=device, device_id_type=MESH)

    loop(1, N_CTX, lambda k: greet((lax.rem(ci + k, N_CTX), hi)))
    loop(1, N_HEAD, lambda k: greet((ci, lax.rem(hi + k, N_HEAD))))

    @pl.when(cross == 1)
    def _():
        for p in range(2):
            greet((4 * z + 2 * cc + p, 2 * xx + 1 - cc))

    loads = [
        pltpu.make_async_copy(src, dst, loc_sem.at[i])
        for i, (src, dst) in enumerate(((w_in, w), (x_in, x), (b_in, b), (c_in, c), (logd_in, logd)))
    ]
    for load in loads:
        load.start()

    lanes = lax.broadcasted_iota(jnp.int32, (8, COLS), 1)

    def place(k, carry):
        headof, rank = carry
        local = kept[k] - GROUP * hi
        mine = (local >= 0) & (local < GROUP)
        headof = jnp.where(lanes // P_SIZE == jnp.where(mine, rank, -1), local, headof)
        return headof, rank + jnp.where(mine, 1, 0)

    headof, _ = lax.fori_loop(0, KEPT, place, (jnp.full((8, COLS), -1, jnp.int32), jnp.int32(0)))
    headof = headof[0:1, :]
    colidx = jnp.where(headof >= 0, P_SIZE * headof + lax.rem(lanes[0:1, :], P_SIZE), -1)

    def build(i):
        rows = lax.broadcasted_iota(jnp.int32, (128, COLS), 0) + 128 * i
        S[aligned(128 * i, 128, 128), :] = jnp.where(rows == colidx, 1.0, 0.0).astype(BF)

    loop(0, WIDE // 128, build)
    E16[...] = jnp.where(lax.broadcasted_iota(jnp.int32, (GROUP, COLS), 0) == headof, 1.0, 0.0).astype(F32)
    for i in range(3):
        E16B[pl.ds(GROUP * i, GROUP), :] = E16[...].astype(BF)

    for load in loads:
        load.wait()

    upto = one_hot(Q, Q, lambda r, k: r <= k)
    pick = one_hot(COLS, 128, lambda r, k: r == P_SIZE * k)
    slots = dot(E16[...], pick)[:, :GROUP].astype(BF)
    slots3 = jnp.concatenate([slots] * 3, axis=0)
    upto_low = upto.astype(BF)

    def decays(s):
        rows = aligned(Q * s, Q, Q)
        sums = dot(parts(logd[:, rows]), upto_low)
        cum = parts(sums[:GROUP] + sums[GROUP : 2 * GROUP] + sums[2 * GROUP :])
        CUMR[:, rows] = dot(slots3, cum, TN)
        CUME[rows, :] = dot(cum, E16B[...], TN)

    loop(0, SPANS, decays)
    totals = sum(CUMR[:, pl.ds(Q * s + Q - 1, 1)] for s in range(SPANS))
    TOT[...] = dot(jnp.broadcast_to(totals, (GROUP, 8)), one_hot(GROUP, 128, lambda r, k: r == k), TN, precision=HIGH)

    STIN[0] = jnp.zeros((N, COLS), F32)

    def local_states(s):
        rows = aligned(Q * s, Q, Q)
        cume = CUME[rows, :]
        total = cume[Q - 1 : Q, :]
        xs = dot(x[rows, :], S[...])
        XS[rows, :] = xs.astype(BF)
        xt = (jnp.exp(total - cume) * xs).astype(BF)
        XT[rows, :] = xt
        part = dot(b[rows, :], xt, TN)
        PART[s] = part
        STIN[0] = jnp.exp(total) * STIN[0] + part

    loop(0, SPANS, local_states)
    ST[0] = STIN[0].astype(BF)

    pl.semaphore_wait(barrier, N_CTX - 1 + N_HEAD - 1 + 2 * cross)

    def decay_copy(k, at):
        to = lax.rem(ci + k, N_CTX)
        return rcopy(TOT, RD.at[aligned(8 * at, 8, 8), :], dec_sem.at[0, k], dec_sem.at[1, k], (to, hi))

    loop(1, N_CTX, lambda k: decay_copy(k, ci).start())
    RD[aligned(8 * ci, 8, 8), :] = TOT[...]

    forward = Exchange(ST.at[0], FL, FB, FE, fex_sem, ci, hi)
    forward.start()


    def g_tile(token, feature, q):
        return G.at[token, :, q, :, aligned(TOK * feature, TOK, TOK)]

    def quarter(q, p):
        return g.at[:, q, :, pl.ds(TOK * p, TOK)]

    def a2a_copy(q, p, slot):
        return rcopy(
            quarter(q, p), g_tile(y, xx, q), a2a_sem.at[0, q, p], a2a_sem.at[1, q, slot], (4 * z + 2 * cc + p, 2 * xx + half)
        )

    def a2a_start(q):
        for p in range(2):

            @pl.when(2 * cc + p != y)
            def _():
                a2a_copy(q, p, lax.rem(y, 2)).start()

    def x_gather(q, t):
        token = 2 * cc + t
        return Gather(
            lambda p: g_tile(token, p, q),
            lambda p, h: G.at[token, h, q, :, aligned(TOK * p, TOK, TOK)],
            lambda i: xs_sem.at[q, t, i],
            lambda i: xr_sem.at[q, t, i],
            xx, prv(xx), nxt(xx), at_x,
        )

    x_gathers = [[x_gather(q, t) for t in range(2)] for q in range(2)]
    ring_x = (xx, prv(xx), nxt(xx), lax.rem(xx + 2, 4))

    def sibling_copy(q, t, j, core):
        tile = g_tile(2 * core + t, ring_x[j], q)
        return rcopy(tile, tile, sib_sem.at[0, q, t, j], sib_sem.at[1, q, t, j], sibling)

    def x_launch(q, t):
        x_gathers[q][t].start()
        sibling_copy(q, t, 0, cc).start()

    def own_copy(q, p):
        return pltpu.make_async_copy(quarter(q, p), g_tile(y, xx, q), own_sem.at[q])

    def x_own():
        for p in range(2):

            @pl.when(2 * cc + p == y)
            def _():
                for q in range(2):
                    own_copy(q, p).start()
                for q in range(2):
                    own_copy(q, p).wait()
                    x_launch(q, p)

    def x_rest(q):
        for t in range(2):

            @pl.when(2 * cc + t != y)
            def _():
                rcopy(
                    quarter(q, t), g_tile(2 * cc + t, xx, q), a2a_sem.at[0, q, t], a2a_sem.at[1, q, t], sibling
                ).wait_recv()
                x_launch(q, t)

    def x_forward(q):
        for t in range(2):
            x_gathers[q][t].forward()
            sibling_copy(q, t, 1, cc).start()
            sibling_copy(q, t, 2, cc).start()

    def x_finish(q):
        for t in range(2):
            x_gathers[q][t].finish()
            sibling_copy(q, t, 3, cc).start()
        for t in range(2):
            for j in range(4):
                sibling_copy(q, t, j, 1 - cc).wait_recv()

    a2a_start(0)
    x_own()

    def pick_w(i):
        W[aligned(TOK * z + 128 * i, 128, 128), :] = dot(w[aligned(128 * i, 128, 128), :], S[...]).astype(BF)

    loop(0, TOK // 128, pick_w)

    def w_gather(q):
        return Gather(
            lambda p: W.at[aligned(TOK * p + TOK // 2 * q, TOK // 2, TOK // 2), :],
            lambda p, h: W.at[aligned(TOK * p + TOK // 2 * q + TOK // 4 * h, TOK // 4, TOK // 4), :],
            lambda i: wag_sem.at[q, 0, i],
            lambda i: wag_sem.at[q, 1, i],
            z, prv(z), nxt(z), at_z,
        )

    w_gathers = [w_gather(q) for q in range(2)]
    sub = lax.broadcasted_iota(jnp.int32, (Q, Q), 0)
    lane = lax.broadcasted_iota(jnp.int32, (Q, Q), 1)
    left_half = lane < P_SIZE
    causal = lane <= sub

    def inside(s):
        rows = aligned(Q * s, Q, Q)
        cb = dot(c[rows, :], b[rows, :], NT)
        for k in range(PAIRS):
            cols = pl.ds(Q * k, Q)
            for h in range(2):
                head = 2 * k + h
                differ = CUME[rows, pl.ds(P_SIZE * head, 1)] - CUMR[pl.ds(head, 1), rows]
                low = jnp.where(causal, jnp.exp(jnp.where(causal, differ, 0.0)), 0.0)
                L[PAIRS * s + k, pl.ds(Q * h, Q), :] = low
                MS[PAIRS * s + k, pl.ds(Q * h, Q), :] = (low * cb).astype(BF)
            both = dot(MS[PAIRS * s + k], XS[rows, cols])
            YF[rows, cols] = jnp.where(left_half, both[:Q], both[Q:])

    rowidx = jnp.broadcast_to(colidx, (8, COLS)).astype(F32).T[:, 0:1].astype(jnp.int32)
    for i in range(COLS // 128):
        ids = lax.broadcasted_iota(jnp.int32, (128, WIDE), 1)
        S_T[pl.ds(128 * i, 128), :] = jnp.where(ids == rowidx[128 * i : 128 * i + 128], 1.0, 0.0).astype(BF)

    loop(0, SPANS, inside)

    loop(1, N_CTX, lambda k: decay_copy(k, lax.rem(ci + N_CTX - k, N_CTX)).wait_recv())
    first_slot = CAP // 2 * lax.rem(ci, 2)
    DEC[...] = jnp.exp(dot(RD[...], one_hot(128, HALF, lambda r, k: r == k // P_SIZE + first_slot), precision=HIGH))
    forward.landed()
    forward.scan(DEC, range(N_CTX))
    forward.reply()
    w_gathers[0].start()
    w_gathers[1].start()
    a2a_start(1)
    x_rest(0)
    forward.replied()
    STIN[0] = FE[...].astype(F32)

    def outputs(s):
        rows = aligned(Q * s, Q, Q)
        cume = CUME[rows, :]
        state_in = STIN[s]
        inter = jnp.exp(cume) * dot(c[rows, :], state_in.astype(BF))
        YI[rows, :] = inter
        whole = YF[rows, :] + inter
        YF[rows, :] = whole
        YT[:, aligned(TOK * y + Q * s, Q, Q)] = whole.T.astype(BF)
        STIN[s + 1] = jnp.exp(cume[Q - 1 : Q, :]) * state_in + PART[s]

    def y_gather(q):
        return Gather(
            lambda p: YT.at[:, aligned(TOK * p + TOK // 2 * q, TOK // 2, TOK // 2)],
            lambda p, h: YT.at[pl.ds(HALF * h, HALF), aligned(TOK * p + TOK // 2 * q, TOK // 2, TOK // 2)],
            lambda i: yag_sem.at[q, 0, i],
            lambda i: yag_sem.at[q, 1, i],
            y, prv(y), nxt(y), at_y,
        )

    y_gathers = [y_gather(q) for q in range(2)]
    for q in range(2):
        loop(SPANS // 2 * q, SPANS // 2 * (q + 1), outputs)
        y_gathers[q].start()

    def head_term(q):
        return lambda block: dot(G[block, :, q].reshape(TOK // 2, 4 * TOK), W[...])

    def weight_term(block):
        return dot(YT[...], G[:, :, :, :, aligned(TOK * block, TOK, TOK)].reshape(4 * TOK, TOK))

    heads = (
        Scatter(
            head_term(0), TOK // 2, a_far, a_right, a_left, a_vl, a_vr, a_fl, a_fr, a_own,
            hrs_sem.at[0, 0], hrs_sem.at[0, 1], y, at_y,
        ),
        Scatter(
            head_term(1), TOK // 2, b_far, b_right, b_left, b_vl, b_vr, b_fl, b_fr, b_own,
            hrs_sem.at[1, 0], hrs_sem.at[1, 1], y, at_y,
        ),
    )
    weights = Scatter(
        weight_term, COLS, w_far, w_right, w_left, w_vl, w_vr, w_fl, w_fr, w_own,
        wrs_sem.at[0], wrs_sem.at[1], z, at_z,
    )

    def local_adjoint(s):
        rows = pl.ds(Q * s, Q)
        GK[rows, :] = heads[s % 2].result(pl.ds(Q * (s // 2), Q)).astype(BF)
        gh = (jnp.exp(CUME[rows, :]) * GK[rows, :].astype(F32)).astype(BF)
        GH[rows, :] = gh
        PART[s] = dot(c[rows, :], gh, TN)

    def inside_grad(s):
        rows = aligned(Q * s, Q, Q)
        total = jnp.zeros((Q, Q), F32)
        for k in range(PAIRS):
            cols = pl.ds(Q * k, Q)
            gk = GK[rows, cols].astype(F32)
            stack = jnp.concatenate(
                [jnp.where(left_half, gk, 0.0), jnp.where(left_half, 0.0, gk)], axis=0
            ).astype(BF)
            weighted = L[PAIRS * s + k] * dot(stack, XS[rows, cols], NT)
            total = total + weighted[:Q] + weighted[Q:]
            IG[rows, cols] = dot(MS[PAIRS * s + k], stack, TN)
        sg = total.astype(BF)
        B0[rows, :] = dot(sg, c[rows, :], TN)
        CP[rows, :] = (dot(sg, b[rows, :]) + dot(GH[rows, :], STIN[s].astype(BF), NT)).astype(BF)

    x_rest(1)
    x_forward(0)
    w_gathers[0].forward()
    y_gathers[0].forward()
    w_gathers[1].forward()
    x_forward(1)
    y_gathers[1].forward()
    w_gathers[0].finish()
    w_gathers[1].finish()
    x_finish(0)
    heads[0].first()
    x_finish(1)
    heads[0].second()
    y_gathers[0].finish()
    y_gathers[1].finish()
    weights.first()
    heads[1].first()
    heads[0].last()
    heads[0].finish()
    local_adjoint(0)
    local_adjoint(2)
    heads[1].second()
    heads[1].last()
    inside_grad(0)
    inside_grad(2)
    heads[1].finish()
    local_adjoint(1)
    local_adjoint(3)

    ADJ[SPANS] = jnp.zeros((N, COLS), F32)
    after = jnp.zeros((1, COLS), F32)
    for s in reversed(range(SPANS)):
        total = CUME[pl.ds(Q * s + Q - 1, 1), :]
        AFTER[pl.ds(s, 1), :] = jnp.exp(after)
        after = after + total
        ADJ[s] = jnp.exp(total) * ADJ[s + 1] + PART[s]
    ST[1] = ADJ[0].astype(BF)
    backward = Exchange(ST.at[1], AL, AB, AE, bex_sem, ci, hi)
    backward.start()
    inside_grad(1)
    inside_grad(3)

    def local_b(s):
        rows = aligned(Q * s, Q, Q)
        B0[rows, :] = B0[rows, :] + dot(XT[rows, :], ADJ[s + 1].astype(BF), NT)

    loop(0, SPANS - 1, local_b)
    c_sum = HeadSum(CP, CL, CT, out_c, c_sem, out_sem.at[1], ci, hi)
    c_sum.start()

    loop(1, N_CTX, lambda k: decay_copy(k, ci).wait_send())
    forward.drain()
    for q in range(2):
        w_gathers[q].drain()
    y_gathers[0].drain()
    y_gathers[1].drain()
    for q in range(2):
        for p in range(2):

            @pl.when(2 * cc + p != y)
            def _():
                a2a_copy(q, p, 0).wait_send()

        for t in range(2):
            x_gathers[q][t].drain()
            for j in range(4):
                sibling_copy(q, t, j, cc).wait_send()

    backward.landed()
    backward.scan(DEC, reversed(range(N_CTX)))
    backward.reply()
    weights.second()
    weights.last()
    c_sum.reduce()
    backward.replied()

    def whole_b(s):
        rows = aligned(Q * s, Q, Q)
        carried = (AFTER[pl.ds(s, 1), :] * AE[...].astype(F32)).astype(BF)
        BP[rows, :] = (B0[rows, :] + dot(XT[rows, :], carried, NT)).astype(BF)

    loop(0, SPANS, whole_b)
    b_sum = HeadSum(BP, BL, BT, out_b, b_sem, out_sem.at[2], ci, hi)
    b_sum.start()

    def closing(s):
        rows = aligned(Q * s, Q, Q)
        cume = CUME[rows, :]
        total = cume[Q - 1 : Q, :]
        adjoint = ADJ[s + 1] + AFTER[pl.ds(s, 1), :] * AE[...].astype(F32)
        in_grad = IG[rows, :] + jnp.exp(total - cume) * dot(b[rows, :], adjoint.astype(BF))
        IGB[rows, :] = in_grad.astype(BF)
        gk = GK[rows, :].astype(F32)
        step = XS[rows, :].astype(F32) * in_grad - gk * YF[rows, :]
        start = jnp.sum(gk * YI[rows, :], axis=0, keepdims=True) + jnp.exp(total) * jnp.sum(
            adjoint * STIN[s], axis=0, keepdims=True
        )
        row = lax.broadcasted_iota(jnp.int32, (Q, COLS), 0)
        step = jnp.where(row == 0, start, pltpu.roll(step, 1, 0))
        high = step.astype(BF)
        rest = (step - high.astype(F32)).astype(BF)
        steps = dot(E16B[:GROUP], high, NT) + dot(E16B[:GROUP], rest, NT)
        O_D[:, rows] = dot(steps, upto, precision=HIGH) * (1.0 / math.sqrt(P_SIZE * D))

    def spread_in(i):
        rows = aligned(128 * i, 128, 128)
        O_IG[rows, :] = dot(IGB[rows, :], S_T[...]).astype(BF)

    def spread_w(i):
        cols = aligned(128 * i, 128, 128)
        block = (weights.result(slice(None), cols) * (1.0 / math.sqrt(D))).astype(BF)
        O_W[cols, :] = dot(block, S_T[...], TN).astype(BF)

    stores = [
        pltpu.make_async_copy(O_IG, out_ig, out_sem.at[0]),
        pltpu.make_async_copy(O_D, out_decay, out_sem.at[3]),
        pltpu.make_async_copy(O_W, out_w, out_sem.at[4]),
    ]
    loop(0, SPANS, closing)
    stores[1].start()
    b_sum.reduce()
    loop(0, TOK // 128, spread_in)
    stores[0].start()
    weights.finish()
    loop(0, TOK // 128, spread_w)
    stores[2].start()
    c_sum.finish()
    heads[0].drain()
    heads[1].drain()
    weights.drain()
    backward.drain()
    c_sum.drain()
    b_sum.finish()

    b_sum.drain()
    for store in stores:
        store.wait()


def hand_over(*refs):
    ins, outs, held, scaled, sems = refs[:5], refs[5:10], refs[10:15], refs[15:17], refs[17]
    sources = [held[0], *scaled, held[3], held[4]]
    cuts = [(i, pl.ds(TOK // 4 * k, TOK // 4)) for k in range(4) for i in (0, 4)]
    cuts += [(3, pl.ds(0, GROUP)), (2, pl.ds(0, TOK)), (1, pl.ds(0, TOK))]
    reads, writes = [], []
    for n, (i, rows) in enumerate(cuts):
        reads.append(pltpu.make_async_copy(ins[i].at[rows], held[i].at[rows], sems.at[0, n]))
        writes.append(pltpu.make_async_copy(sources[i].at[rows], outs[i].at[rows], sems.at[1, n]))
    for read in reads:
        read.start()
    for (i, _), read, write in zip(cuts, reads, writes):
        read.wait()
        if i == 1:
            scaled[0][...] = held[1][...].astype(F32) / math.sqrt(KEPT * P_SIZE)
        if i == 2:
            scaled[1][...] = held[2][...].astype(F32) * math.sqrt(N / (KEPT * P_SIZE * D))
        write.start()
    for write in writes:
        write.wait()


def per_device(g_out, w_out, x_act, b_proj, c_proj, log_decay, kept_heads):
    hbm = pl.BlockSpec(memory_space=pl.ANY)
    buf = pltpu.VMEM
    dma = pltpu.SemaphoreType.DMA

    def ring(rows, cols):
        h = rows // 2
        return [
            buf((rows, cols), BF), buf((rows, cols), BF), buf((rows, cols), BF), buf((h, cols), BF), buf((h, cols), BF),
            buf((rows, cols), BF), buf((rows, cols), BF), buf((rows, cols), F32),
        ]

    def head_sum():
        return [
            buf((TOK, N), BF), buf((N_HEAD, TOK // N_HEAD, N), BF), buf((TOK // N_HEAD, N), BF)
        ]

    outs = (
        jax.ShapeDtypeStruct((TOK, WIDE), BF),
        jax.ShapeDtypeStruct((TOK, N), F32),
        jax.ShapeDtypeStruct((TOK, N), F32),
        jax.ShapeDtypeStruct((GROUP, TOK), F32),
        jax.ShapeDtypeStruct((TOK, WIDE), BF),
    )
    sums = jax.ShapeDtypeStruct((TOK, N), BF)
    held = (outs[0], sums, sums, *outs[3:])
    results = pl.pallas_call(
        kernel,
        out_shape=held,
        in_specs=[pl.BlockSpec(memory_space=pltpu.SMEM)] + [hbm] * 6,
        out_specs=[hbm] * 5,
        scratch_shapes=[
            buf((TOK, WIDE), BF), buf((TOK, WIDE), BF), buf((TOK, N), BF), buf((TOK, N), BF), buf((GROUP, TOK), F32),
            buf((WIDE, COLS), BF), buf((COLS, WIDE), BF), buf((GROUP, COLS), F32), buf((3 * GROUP, COLS), BF),
            buf((4, 2, 2, TOK // 4, 4 * TOK), BF), buf((4 * TOK, COLS), BF), buf((COLS, 4 * TOK), BF),
            buf((TOK, COLS), BF), buf((TOK, COLS), BF), buf((TOK, COLS), F32), buf((GROUP, TOK), F32),
            buf((SPANS, N, COLS), F32), buf((SPANS + 1, N, COLS), F32), buf((SPANS + 1, N, COLS), F32),
            buf((TOK, COLS), F32), buf((TOK, COLS), F32),
            buf((SPANS * PAIRS, 2 * Q, Q), F32), buf((SPANS * PAIRS, 2 * Q, Q), BF),
            buf((TOK, COLS), BF), buf((TOK, COLS), BF), buf((TOK, COLS), F32), buf((TOK, COLS), BF),
            buf((TOK, N), F32),
            buf((8, COLS), F32), buf((8, 128), F32), buf((8 * N_CTX, 128), F32), buf((8 * N_CTX, HALF), F32), buf((2, N, COLS), BF),
            buf((16 * N_CTX, HALF), BF), buf((16 * N_CTX, HALF), BF), buf((N, COLS), BF),
            buf((16 * N_CTX, HALF), BF), buf((16 * N_CTX, HALF), BF), buf((N, COLS), BF),
            *head_sum(), *head_sum(),
            buf((TOK, WIDE), BF), buf((GROUP, TOK), F32), buf((TOK, WIDE), BF),
            *ring(TOK // 2, COLS), *ring(TOK // 2, COLS), *ring(COLS, TOK),
            dma((5,)), dma((2,)), dma((2, 2, 2)), dma((2, 2, 4)), dma((2, 2, 4)), dma((2, 2, 2, 4)), dma((2, 2, 4)),
            dma((2, 2, 4)), dma((2, 2, 6)), dma((2, 6)), dma((2, N_CTX)), dma((4, N_CTX)), dma((4, N_CTX)),
            dma((4, N_HEAD)), dma((4, N_HEAD)), dma((5,)),
        ],
        compiler_params=pltpu.CompilerParams(
            collective_id=0, has_side_effects=True, vmem_limit_bytes=VMEM_LIMIT
        ),
        cost_estimate=pl.CostEstimate(flops=14_000_000_000, bytes_accessed=8_000_000, transcendentals=4_000_000),
    )(
        kept_heads, g_out.reshape(2, 2, TOK // 4, WIDE), w_out, x_act, b_proj, c_proj, log_decay,
    )
    return pl.pallas_call(
        hand_over,
        out_shape=outs,
        in_specs=[hbm] * 5,
        out_specs=[hbm] * 5,
        scratch_shapes=[*(buf(out.shape, out.dtype) for out in (*held, *outs[1:3])), dma((2, 11))],
        compiler_params=pltpu.CompilerParams(has_side_effects=True, vmem_limit_bytes=VMEM_LIMIT),
    )(*results)


def solution(mesh):
    in_specs = (
        P("ctx", "head"),
        P("ctx", "head"),
        P("ctx", "head"),
        P("ctx", None),
        P("ctx", None),
        P("head", "ctx"),
        P(),
    )
    out_specs = (
        P("ctx", "head"),
        P("ctx", None),
        P("ctx", None),
        P("head", "ctx"),
        P("ctx", "head"),
    )
    return jax.shard_map(
        per_device, mesh=mesh, in_specs=in_specs, out_specs=out_specs, check_vma=False
    )
```
